32 devices in a mesh: strip: 4 (over x, core), canvas: 8 (over z, y).
Axes of the slice: x: 2, y: 2, z: 4, core: 2. Of those that a mesh axis runs over, the one named last changes fastest.
Arguments:
- tokens: bfloat16 [32, 32, 32, 768], P('canvas', 'strip'), may hold values from -40 to 40
- conditioning: bfloat16 [32, 768], P('canvas'), may hold values from -6 to 6
- latent_ids: int32 [32, 4], P('canvas'), may hold values from 0 to 3, as said below
- w_ada: bfloat16 [768, 4608], replicated, may hold values from -0.21875 to 0.21875
- b_ada: bfloat16 [4608], replicated, may hold values from -1.75 to 1.75
- w_dw1: bfloat16 [9, 768], replicated, may hold values from -2 to 2
- b_dw1: bfloat16 [768], replicated, may hold values from -3 to 3
- w_qkv: bfloat16 [768, 2304], replicated, may hold values from -0.21875 to 0.21875
- b_qv: bfloat16 [1536], replicated, may hold values from -3 to 3
- w_out: bfloat16 [768, 768], replicated, may hold values from -0.875 to 0.875
- b_out: bfloat16 [768], replicated, may hold values from -3 to 3
- w_fc1: bfloat16 [768, 3072], replicated, may hold values from -0.21875 to 0.21875
- b_fc1: bfloat16 [3072], replicated, may hold values from -3 to 3
- w_dw2: bfloat16 [9, 3072], replicated, may hold values from -2 to 2
- b_dw2: bfloat16 [3072], replicated, may hold values from -3 to 3
- w_fc2: bfloat16 [3072, 768], replicated, may hold values from -0.109375 to 0.109375
- b_fc2: bfloat16 [768], replicated, may hold values from -3 to 3
- out_grad: bfloat16 [32, 32, 32, 768], P('canvas', 'strip'), may hold values from -6 to 6
Outputs:
- output: bfloat16 [32, 32, 32, 768], P('canvas', 'strip')
- token_input_gradient: float32 [32, 32, 32, 768], P('canvas', 'strip')
- grad_conditioning: float32 [32, 768], P('canvas')
- grad_w_ada: float32 [768, 4608], P(('strip', 'canvas'))
- grad_b_ada: float32 [4608], P(('strip', 'canvas'))
- grad_w_dw1: float32 [9, 768], P(None, ('strip', 'canvas'))
- grad_b_dw1: float32 [768], P(('strip', 'canvas'))
- grad_w_qkv: float32 [768, 2304], P(('strip', 'canvas'))
- grad_b_qv: float32 [1536], P(('strip', 'canvas'))
- grad_w_out: float32 [768, 768], P(None, ('strip', 'canvas'))
- grad_b_out: float32 [768], P(('strip', 'canvas'))
- grad_w_fc1: float32 [768, 3072], P(('strip', 'canvas'))
- grad_b_fc1: float32 [3072], P(('strip', 'canvas'))
- grad_w_dw2: float32 [9, 3072], P(None, ('strip', 'canvas'))
- grad_b_dw2: float32 [3072], P(('strip', 'canvas'))
- grad_w_fc2: float32 [3072, 768], P(None, ('strip', 'canvas'))
- grad_b_fc2: float32 [768], P(('strip', 'canvas'))
The draws below stay inside these ranges and needn't reach their ends.
Inputs may be any that keep to these rules, and one draw needn't show every extreme that they name: `latent_ids`: quadrants are in row-major order; quadrants with equal numbers hold one image, and in every canvas some image covers a top quadrant and the quadrant below it.
All inputs are finite; a program needn't handle non-finite values.
Results may differ from the reference program's by a relative error of at most 0.015.
The reference program's roundings to bfloat16 on the way count: a program that leaves them out, or rounds other values in their place, can miss the bound.
Values may be sent and summed in bfloat16 or wider, within the bound.
No kernel may reach another device: no remote copies, remote signals or barrier semaphores. Data moves between devices by JAX's collectives and lax.ppermute only.
A program may use at most 320 MiB of HBM per device.

```python
import math
import jax
import jax.numpy as jnp
from jax import lax

D = 768
HEADS = 12
HEAD_DIM = 64
FF = 3072
SIDE = 32
CANVASES = 32


def draw_tokens(key, part):
    key = jax.random.fold_in(key, 11)
    noise_key, column_key, row_key = jax.random.split(key, 3)
    full_shape = (CANVASES, SIDE, SIDE, D)
    column_scale = jnp.exp(jax.random.uniform(column_key, (D,), jnp.float32) * math.log(10.0))
    row_scale = jnp.exp(jax.random.uniform(row_key, (CANVASES, SIDE, SIDE, 1), jnp.float32) * math.log(10.0))
    base = jnp.clip(jax.random.normal(noise_key, full_shape, jnp.float32), -4.0, 4.0)
    return (base * row_scale * column_scale / 10.0).astype(jnp.bfloat16)


def draw_latent_ids(key, part):
    key = jax.random.fold_in(key, 23)
    pick_key, column_key = jax.random.split(key)
    numbers = jax.random.randint(pick_key, (CANVASES, 4), 0, 4, jnp.int32)
    first_canvas = jnp.arange(CANVASES, dtype=jnp.int32)[:, None] == 0
    quadrant = jnp.arange(4, dtype=jnp.int32)[None, :]
    numbers = jnp.where(first_canvas & (quadrant == 0), 0, numbers)
    numbers = jnp.where(first_canvas & (quadrant == 1), 3, numbers)
    column = jax.random.randint(column_key, (CANVASES, 1), 0, 2, jnp.int32)
    above = jnp.where(column == 0, numbers[:, 0:1], numbers[:, 1:2])
    return jnp.where(quadrant == column + 2, above, numbers).astype(jnp.int32)


def raised(values, rng, source, target, parts, factor):
    owner, partner = [(jnp.arange(values.shape[dim]) // (values.shape[dim] // parts)).reshape([-1 if axis == dim else 1 for axis in range(values.ndim)]) for dim in (source, target)]
    chosen = jax.random.permutation(rng, parts)[partner]
    strong = (owner == chosen) | (owner == (partner + parts // 2) % parts)
    return jnp.where(strong, factor * values, values)


def shard_levels(key, shape, pieces, low, high):
    factor_of, own = 1.0, jax.random.fold_in(key, 6)
    for dim, blocks in pieces:
        heights = jnp.exp(jax.random.uniform(jax.random.fold_in(own, dim), (blocks,), jnp.float32, low / len(pieces), high / len(pieces)))
        factor_of = factor_of * jnp.repeat(heights, shape[dim] // blocks).reshape([-1 if axis == dim else 1 for axis in range(len(shape))])
    return factor_of


def noise(stream_key, dims, deviation, reach, shards=(), kind=jnp.bfloat16):
    drawn = jax.random.normal(stream_key, dims, jnp.float32) * deviation
    if len(shards) > 0:
        drawn = shard_levels(stream_key, dims, shards, -0.22, 0.18) * drawn
    return jnp.clip(drawn, min=-reach, max=reach).astype(kind)


def heavy_noise(stream_key, dims, spread, bound, cuts, heavy, held_as=jnp.bfloat16):
    array = spread * jax.random.normal(stream_key, dims, jnp.float32)
    if cuts:
        array = array * shard_levels(stream_key, dims, cuts, -0.22, 0.18)
    return jnp.clip(raised(array, jax.random.fold_in(stream_key, 3), *heavy), -bound, bound).astype(held_as)


def setup_inputs(seed: int = 0) -> dict:
    key_of = jax.random.split(jax.random.key(seed), 19)
    tokens = draw_tokens(jax.random.fold_in(key_of[18], 71), 0)
    conditioning = noise(key_of[1], (CANVASES, D), 1.0, 6.0, ((0, 8),))
    latent_ids = draw_latent_ids(jax.random.fold_in(key_of[18], 71), 0)
    w_ada = noise(key_of[3], (D, 6 * D), D ** -0.5, 0.21875)
    b_ada = noise(key_of[4], (6 * D,), 0.3, 1.75)
    w_dw1 = noise(key_of[5], (9, D), 0.35, 2.0)
    b_dw1 = noise(key_of[6], (D,), 0.5, 3.0)
    w_qkv = noise(key_of[7], (D, 3 * D), D ** -0.5, 0.21875)
    b_qv = noise(key_of[8], (2 * D,), 0.5, 3.0)
    w_out = noise(key_of[9], (D, D), (D // 16) ** -0.5, 0.875)
    b_out = noise(key_of[10], (D,), 0.5, 3.0)
    w_fc1 = noise(key_of[11], (D, FF), D ** -0.5, 0.21875)
    b_fc1 = noise(key_of[12], (FF,), 0.5, 3.0)
    w_dw2 = noise(key_of[13], (9, FF), 0.35, 2.0)
    b_dw2 = noise(key_of[14], (FF,), 0.5, 3.0)
    w_fc2 = noise(key_of[15], (FF, D), FF ** -0.5, 0.109375)
    b_fc2 = noise(key_of[16], (D,), 0.5, 3.0)
    out_grad = heavy_noise(key_of[17], (CANVASES, SIDE, SIDE, D), 1.0, 6.0, ((0, 8), (1, 4)), (0, 3, 8, 2.0))
    return dict(tokens=tokens, conditioning=conditioning, latent_ids=latent_ids, w_ada=w_ada, b_ada=b_ada, w_dw1=w_dw1, b_dw1=b_dw1, w_qkv=w_qkv, b_qv=b_qv, w_out=w_out, b_out=b_out, w_fc1=w_fc1, b_fc1=b_fc1, w_dw2=w_dw2, b_dw2=b_dw2, w_fc2=w_fc2, b_fc2=b_fc2, out_grad=out_grad)


@jax.custom_vjp
def low(v):
    return lax.optimization_barrier(v.astype(jnp.bfloat16)).astype(jnp.float32)

@jax.custom_vjp
def low_back(v):
    return v

def low_keep(v):
    return (low(v), None)

def low_pass(kept, grad):
    return (grad,)

def back_keep(v):
    return (v, None)

def back_low(kept, grad):
    return (low(grad),)
low.defvjp(low_keep, low_pass)
low_back.defvjp(back_keep, back_low)
norm_eps = 1e-06
neg_fill = -1e+30
highest = lax.Precision.HIGHEST

def latent_grid(latent_ids, first_row, row_count, side_len):
    row_pos = first_row + jnp.arange(row_count, dtype=jnp.int32)
    col_pos = jnp.arange(side_len, dtype=jnp.int32)
    half_side = side_len // 2
    quadrant = 2 * (row_pos[:, None] // half_side) + col_pos[None, :] // half_side
    picked = jnp.zeros((latent_ids.shape[0], row_count, side_len), jnp.int32)
    for slot_id in range(4):
        picked = jnp.where((quadrant == slot_id)[None], latent_ids[:, slot_id][:, None, None], picked)
    inside = (row_pos >= 0) & (row_pos < side_len)
    return jnp.where(inside[None, :, None], picked, -1)

def tap_masks(latent_pad, row_count, col_count):
    centre = latent_pad[:, 1:1 + row_count, 1:1 + col_count]
    listed = []
    for tap_id in range(9):
        row_step = tap_id // 3 - 1
        col_step = tap_id % 3 - 1
        shifted = latent_pad[:, 1 + row_step:1 + row_step + row_count, 1 + col_step:1 + col_step + col_count]
        listed.append((centre == shifted).astype(jnp.float32))
    return jnp.stack(listed)

def depthwise(padded, tap_weights, tap_mask, row_count, col_count):
    summed = jnp.zeros((padded.shape[0], row_count, col_count, padded.shape[-1]), jnp.float32)
    for tap_id in range(9):
        row_step = tap_id // 3 - 1
        col_step = tap_id % 3 - 1
        window = padded[:, 1 + row_step:1 + row_step + row_count, 1 + col_step:1 + col_step + col_count]
        summed = summed + tap_weights[tap_id] * tap_mask[tap_id][..., None] * window
    return summed

def matmul_rows(left, right):
    flat_left = left.reshape(-1, left.shape[-1])
    product = jnp.dot(flat_left, right, precision=highest, preferred_element_type=jnp.float32)
    return product.reshape(left.shape[:-1] + (right.shape[1],))

def layer_norm(values):
    centred = values - lax.optimization_barrier(jnp.mean(values, -1, keepdims=True))
    return centred * lax.rsqrt(lax.optimization_barrier(jnp.mean(centred * centred, -1, keepdims=True)) + norm_eps)

def unshuffle_groups(full):
    batch_size = full.shape[0]
    side_len = full.shape[1]
    feature_count = full.shape[3]
    regrouped = full.reshape(batch_size, side_len // 2, 2, side_len // 2, 2, feature_count)
    regrouped = regrouped.transpose(0, 2, 4, 1, 3, 5)
    return regrouped.reshape(batch_size, 4, side_len // 2 * (side_len // 2), feature_count)

def shuffle_back(grouped, side_len):
    batch_size = grouped.shape[0]
    feature_count = grouped.shape[3]
    half_side = side_len // 2
    regrouped = grouped.reshape(batch_size, 2, 2, half_side, half_side, feature_count)
    regrouped = regrouped.transpose(0, 3, 1, 4, 2, 5)
    return regrouped.reshape(batch_size, side_len, side_len, feature_count)

def canvas_block(token_block, cond_block, id_block, weight_list):
    w_ada, b_ada, w_dw1, b_dw1, w_qkv, b_qv, w_out, b_out, w_fc1, b_fc1, w_dw2, b_dw2, w_fc2, b_fc2 = weight_list
    batch_size = token_block.shape[0]
    side_len = token_block.shape[1]
    cond_act = low(jax.nn.silu(cond_block))
    modulation = low_back(matmul_rows(cond_act, w_ada) + b_ada)
    mod_parts = [modulation[:, None, None, part_id * D:(part_id + 1) * D] for part_id in range(6)]
    first_offset, first_scale, gate_a, second_offset, second_scale, gate_b = mod_parts
    latent_pad = jnp.pad(latent_grid(id_block, 0, side_len, side_len), ((0, 0), (1, 1), (1, 1)), constant_values=-1)
    tap_mask = tap_masks(latent_pad, side_len, side_len)
    normalized_first = low(layer_norm(token_block) * (1.0 + first_scale) + first_offset)
    pad_a = jnp.pad(normalized_first, ((0, 0), (1, 1), (1, 1), (0, 0)))
    conv_a = low_back(low(depthwise(pad_a, w_dw1, tap_mask, side_len, side_len) + b_dw1))
    grouped = unshuffle_groups(conv_a)
    group_len = grouped.shape[2]
    projected = matmul_rows(grouped, w_qkv)
    queries = low_back(low(projected[..., :D] + b_qv[:D]))
    key_rows = low_back(low(projected[..., D:2 * D]))
    value_rows = low_back(low(projected[..., 2 * D:] + b_qv[D:]))

    def split_heads(rows_in):
        return rows_in.reshape(batch_size, 4, group_len, HEADS, HEAD_DIM)
    scores = jnp.einsum('bgqhd,bgkhd->bghqk', split_heads(queries), split_heads(key_rows), precision=highest)
    scores = low_back(scores * HEAD_DIM ** (-0.5))
    group_ids = latent_grid(id_block, 0, side_len // 2, side_len // 2).reshape(batch_size, group_len)
    same_latent = group_ids[:, :, None] == group_ids[:, None, :]
    scores = jnp.where(same_latent[:, None, None], scores, neg_fill)
    attn_probs = low(jax.nn.softmax(scores, axis=-1))
    mixed_rows = jnp.einsum('bghqk,bgkhd->bgqhd', attn_probs, split_heads(value_rows), precision=highest)
    mixed_rows = low_back(low(mixed_rows.reshape(batch_size, 4, group_len, D)))
    projection = low_back(matmul_rows(shuffle_back(mixed_rows, side_len), w_out) + b_out)
    middle_tokens = token_block + gate_a * projection
    normalized_second = low(layer_norm(middle_tokens) * (1.0 + second_scale) + second_offset)
    hidden = low_back(low(matmul_rows(normalized_second, w_fc1) + b_fc1))
    pad_h = jnp.pad(hidden, ((0, 0), (1, 1), (1, 1), (0, 0)))
    pre_act = low_back(depthwise(pad_h, w_dw2, tap_mask, side_len, side_len) + b_dw2)
    activated = low(jax.nn.gelu(pre_act, approximate=False))
    branch = low_back(matmul_rows(activated, w_fc2) + b_fc2)
    return middle_tokens + gate_b * branch

def reference(tokens, conditioning, latent_ids, w_ada, b_ada, w_dw1, b_dw1, w_qkv, b_qv, w_out, b_out, w_fc1, b_fc1, w_dw2, b_dw2, w_fc2, b_fc2, out_grad):
    weight_args = (w_ada, b_ada, w_dw1, b_dw1, w_qkv, b_qv, w_out, b_out, w_fc1, b_fc1, w_dw2, b_dw2, w_fc2, b_fc2)
    weights = tuple((weight_arg.astype(jnp.float32) for weight_arg in weight_args))
    block_count = tokens.shape[0] // 4

    def forward(token_all, cond_all, weight_list):

        def block_fn(token_block, cond_block, id_block):
            return canvas_block(token_block, cond_block, id_block, weight_list)
        block_step = jax.checkpoint(block_fn)

        def scan_step(carry_in, blocks_in):
            return (carry_in, block_step(blocks_in[0], blocks_in[1], blocks_in[2]))
        stacked = (token_all.reshape((block_count, 4) + token_all.shape[1:]), cond_all.reshape(block_count, 4, cond_all.shape[1]), latent_ids.reshape(block_count, 4, 4))
        carry_out, outputs = lax.scan(scan_step, jnp.zeros((), jnp.float32), stacked)
        return outputs.reshape(token_all.shape)
    primal, pullback = jax.vjp(forward, tokens.astype(jnp.float32), conditioning.astype(jnp.float32), weights)
    grad_tokens, grad_cond, weight_grads = pullback(out_grad.astype(jnp.float32))
    return (primal.astype(jnp.bfloat16), grad_tokens, grad_cond, weight_grads[0], weight_grads[1], weight_grads[2], weight_grads[3], weight_grads[4], weight_grads[5], weight_grads[6], weight_grads[7], weight_grads[8], weight_grads[9], weight_grads[10], weight_grads[11], weight_grads[12], weight_grads[13])
```

```python
import functools
import jax, jax.numpy as jnp
from jax import lax
from jax.sharding import Mesh, PartitionSpec as P
from jax.experimental import pallas as pl
from jax.experimental.pallas import tpu as pltpu

LANES = 128
F32 = jnp.float32
BF16 = jnp.bfloat16


def dot_nn(left, right):
    return jnp.dot(left, right, preferred_element_type=F32)


def dot_nt(left, right):
    return lax.dot_general(left, right, (((1,), (1,)), ((), ())), preferred_element_type=F32)


def cost(micros):
    return pl.CostEstimate(flops=int(micros * 1e9), bytes_accessed=int(micros * 1e6), transcendentals=0)


KINDS = ((2, 0, 1), (0, 1, 3))


def seam_masks(ids, side):
    half = side // 2
    place = jnp.arange(half)
    first, last, mid = place == 0, place == half - 1, half // 2
    same = lambda p, q: (ids[p] == ids[q]).astype(F32)
    one = jnp.ones((half,), F32)
    col = lambda at, seam, edge: jnp.where(edge, 0.0, jnp.where(place == at, seam, one))
    left_top = col(mid, same(0, 1), first)
    left_low = col(mid, same(2, 3), first)
    right_top = col(mid - 1, same(0, 1), last)
    right_low = col(mid - 1, same(2, 3), last)
    rows = jnp.where(place < mid, same(0, 2), same(1, 3))
    from_top = jnp.where(first, 0.0, jnp.where(place == mid, same(0, 3), rows))
    from_top_r = jnp.where(last, 0.0, jnp.where(place == mid - 1, same(1, 2), rows))
    from_low = jnp.where(first, 0.0, jnp.where(place == mid, same(1, 2), rows))
    from_low_r = jnp.where(last, 0.0, jnp.where(place == mid - 1, same(0, 3), rows))
    left = jnp.concatenate([jnp.tile(left_top, half // 2), jnp.tile(left_low, half // 2)])
    right = jnp.concatenate([jnp.tile(right_top, half // 2), jnp.tile(right_low, half // 2)])
    wide = lambda v: jnp.broadcast_to(v[:, None], (v.shape[0], LANES))
    return (
        jnp.stack([wide(left), wide(right)]),
        jnp.stack([wide(rows), wide(from_top), wide(from_top_r), wide(from_low), wide(from_low_r)]),
    )


def clear_rims(store, half, width):
    zero = jnp.zeros((half, width), F32)
    for a in range(2):
        for kind in range(4):
            store[a, kind, 0:half, :] = zero
            store[a, kind, (half + 2) * half : (half + 3) * half, :] = zero


def fill_seam(store, seams, half, lanes):
    mid = half // 2
    seam_at = pl.ds((mid + 1) * half, half)
    for a, source, left_id, right_id in ((1, mid, 1, 2), (0, mid + 2, 3, 4)):
        rows = pl.ds(source * half, half)
        even = store[a, 0, rows, lanes]
        odd = store[a, 1, rows, lanes]
        store[a, 0, seam_at, lanes] = even * seams[0]
        store[a, 1, seam_at, lanes] = odd * seams[0]
        store[a, 2, seam_at, lanes] = pltpu.roll(odd, 1, 0) * seams[left_id]
        store[a, 3, seam_at, lanes] = pltpu.roll(even, half - 1, 0) * seams[right_id]


def put_row(store, a, e, place, lanes, value, sides, rows, half):
    store[a, e, place, lanes] = value
    if e == 1:
        store[a, 2, place, lanes] = pltpu.roll(value, 1, 0) * sides[0, rows, :]
    else:
        store[a, 3, place, lanes] = pltpu.roll(value, half - 1, 0) * sides[1, rows, :]


def row_sources(store, at, half, lanes):
    spots = ((1, -1), (0, 0), (1, 0), (0, 1))
    return [
        [store[a, kind, pl.ds(pl.multiple_of((at + off) * half, half), half), lanes] for kind in range(4)]
        for a, off in spots
    ]


def tap_source(sources, a, e, tap):
    return sources[a + tap // 3][KINDS[e][tap % 3]]


def store_row(step, half):
    return step + 1 + (step >= half // 2).astype(jnp.int32)


def gelu_pair(u):
    size = jnp.abs(u)
    decay = jnp.exp(-0.5 * u * u)
    base = 1.0 + 0.23164190 * size
    guess = pl.reciprocal(base, approx=True)
    t = guess * (2.0 - base * guess)
    poly = t * (0.127414796 + t * (-0.142248368 + t * (0.710706870 + t * (-0.726576013 + t * 0.530702714))))
    tail = poly * decay
    share = jnp.where(u >= 0.0, 1.0 - tail, tail)
    return u * share, share + u * (decay * 0.3989422804014327)


def ff_kernel(half, nb, nbt, db, dbt, w1, b1, wd, bd, w2, sides, seams,
              gk, gs, small, branch, dnb, S, D, dact, act, dh):
    width = w1.shape[1]
    group = half * half
    blocks = [pl.ds(lb * LANES, LANES) for lb in range(width // LANES)]
    half_rows = nbt.shape[0] // 2

    @pl.when(pl.program_id(0) == 0)
    def _():
        clear_rims(S, half, width)
        clear_rims(D, half, width)
        branch[...] = jnp.zeros_like(branch)
        dnb[...] = jnp.zeros_like(dnb)

    mid_rows = group // 2
    for g in range(4):
        a, e = g // 2, g % 2
        rows = pl.ds(g * group, group)
        h = dot_nn(nb[rows, :], w1[...]) + b1[...]
        h = h.astype(BF16).astype(F32)
        for part in range(2):
            cut = slice(part * mid_rows, (part + 1) * mid_rows)
            place = pl.ds(half + part * (mid_rows + half), mid_rows)
            S[a, e, place, :] = h[cut]
        shifted = pltpu.roll(h, 1 if e == 1 else group - 1, 0)
        for lb, lanes in enumerate(blocks):
            moved = shifted[:, lb * LANES : (lb + 1) * LANES] * sides[0 if e == 1 else 1]
            for part in range(2):
                cut = slice(part * mid_rows, (part + 1) * mid_rows)
                place = pl.ds(half + part * (mid_rows + half), mid_rows)
                S[a, 2 if e == 1 else 3, place, lanes] = moved[cut]
        dact[rows, :] = dot_nt(db[rows, :], w2[...])
    for lanes in blocks:
        fill_seam(S, seams, half, lanes)

    for lanes in blocks:
        taps = [wd[t : t + 1, lanes] for t in range(9)]
        bias = bd[:, lanes]

        def forward(step, carry):
            at = store_row(step, half)
            rows = pl.ds(pl.multiple_of(step * half, half), half)
            place = pl.ds(pl.multiple_of(at * half, half), half)
            sources = row_sources(S, at, half, lanes)
            for a in range(2):
                for e in range(2):
                    pre = bias + taps[0] * tap_source(sources, a, e, 0)
                    for t in range(1, 9):
                        pre = pre + taps[t] * tap_source(sources, a, e, t)
                    value, slope = gelu_pair(pre)
                    token = pl.ds(pl.multiple_of((2 * a + e) * group + step * half, half), half)
                    act[token, lanes] = value.astype(BF16)
                    d_pre = (dact[token, lanes] * slope).astype(BF16).astype(F32)
                    put_row(D, a, e, place, lanes, d_pre, sides, rows, half)
            return carry

        lax.fori_loop(0, half, forward, 0)
    for lanes in blocks:
        fill_seam(D, seams, half, lanes)

    for lanes in blocks:
        taps = [wd[t : t + 1, lanes] for t in range(9)]

        def backward(step, sums):
            sums = list(sums)
            at = store_row(step, half)
            place = pl.ds(pl.multiple_of(at * half, half), half)
            sources = row_sources(D, at, half, lanes)
            fold = lambda v: v[0:8] + v[8:16] if half == 16 else v.reshape(-1, 8, LANES).sum(0)
            for a in range(2):
                for e in range(2):
                    hid = S[a, e, place, lanes]
                    total = None
                    for t in range(9):
                        x = tap_source(sources, a, e, t)
                        term = taps[8 - t] * x
                        total = term if total is None else total + term
                        sums[8 - t] = sums[8 - t] + fold(hid * x)
                    d_hid = total.astype(BF16)
                    token = pl.ds(pl.multiple_of((2 * a + e) * group + step * half, half), half)
                    dh[token, lanes] = d_hid
                    sums[9] = sums[9] + fold(sources[a + 1][e])
                    sums[10] = sums[10] + fold(d_hid.astype(F32))
            return tuple(sums)

        sums = lax.fori_loop(0, half, backward, tuple(jnp.zeros((8, LANES), F32) for _ in range(11)))
        for at, total in enumerate(sums):
            small[at : at + 1, lanes] = jnp.sum(total, 0, keepdims=True)

    branch[...] += dot_nn(act[...], w2[...])
    dnb[...] += dot_nt(dh[...], w1[...])
    for at, (left, right) in enumerate(((nbt, dh), (dbt, act))):
        gk[at] = dot_nn(left[0:half_rows, :], right[...]).astype(BF16)
        gs[at] = dot_nn(left[half_rows:, :], right[...]).astype(BF16)


def feed_forward(nb, nbt, db, dbt, w1, b1, wd, bd, w2, sides, seams, half, chunk):
    tokens, model = nb.shape
    hidden = w1.shape[1]
    padded = (half + 3) * half
    whole = lambda shape: pl.BlockSpec(shape, lambda i: (0,) * len(shape))
    column = lambda rows: pl.BlockSpec((rows, chunk), lambda i: (0, i))
    sds = jax.ShapeDtypeStruct
    return pl.pallas_call(
        functools.partial(ff_kernel, half),
        grid=(hidden // chunk,),
        in_specs=[
            whole((tokens, model)), whole((model, tokens)), whole((tokens, model)), whole((model, tokens)),
            column(model), column(1), column(9), column(1),
            pl.BlockSpec((chunk, model), lambda i: (i, 0)),
            whole(sides.shape), whole(seams.shape),
        ],
        out_specs=[pl.BlockSpec((2, model // 2, chunk), lambda i: (0, 0, i))] * 2 + [column(16), whole((tokens, model)), whole((tokens, model))],
        out_shape=[sds((2, model // 2, hidden), BF16)] * 2
        + [sds((16, hidden), F32), sds((tokens, model), F32), sds((tokens, model), F32)],
        scratch_shapes=[
            pltpu.VMEM((2, 4, padded, chunk), F32),
            pltpu.VMEM((2, 4, padded, chunk), F32),
            pltpu.VMEM((tokens, chunk), F32),
            pltpu.VMEM((tokens, chunk), BF16),
            pltpu.VMEM((tokens, chunk), BF16),
        ],
        compiler_params=pltpu.CompilerParams(vmem_limit_bytes=60 << 20),
        cost_estimate=cost(90),
        name="feed_forward",
    )(nb, nbt, db, dbt, w1, b1, wd, bd, w2, sides, seams)


HEADS = 12
HEAD_DIM = 64
norm_eps = 1e-06


def dot_tn(left, right):
    return lax.dot_general(left, right, (((0,), (0,)), ((), ())), preferred_element_type=F32)


def whole(shape):
    return pl.BlockSpec(shape, lambda *_: (0,) * len(shape))


def standardize(values):
    centred = values - jnp.mean(values, -1, keepdims=True)
    inv_std = lax.rsqrt(jnp.mean(centred * centred, -1, keepdims=True) + norm_eps)
    return centred * inv_std, inv_std


def norm_reverse(grad_hat, normed_hat, inv_std):
    mean_grad = jnp.mean(grad_hat, -1, keepdims=True)
    mean_cross = jnp.mean(grad_hat * normed_hat, -1, keepdims=True)
    return inv_std * (grad_hat - mean_grad - normed_hat * mean_cross)


def take_strip(strip, pieces, order, store, group, each, part):
    for k, piece in enumerate(pieces):
        source = jnp.bitwise_xor(strip, k)
        moved = dot_nn(order, piece)
        for g in range(4):
            at = pl.multiple_of(g * group + source * each, each)
            store[pl.ds(at, each), :] = moved[g * each : (g + 1) * each].astype(store.dtype)


def ordered_rows(keep, value, target, lanes):
    quarter = value.shape[0] // 4
    for part in range(4):
        x, core = part // 2, part % 2
        at = jnp.bitwise_xor(core, keep) * (2 * quarter) + x * quarter
        target[pl.ds(pl.multiple_of(at, quarter), quarter), lanes] = value[part * quarter : (part + 1) * quarter]


def first_kernel(half, place_ref, own, r1, r2, r3, order, mod, wd, bd, sides, seams,
                 xg, na, cat, S, conv):
    group = half * half
    each = own.shape[1] // 4
    strip = place_ref[0]
    take_strip(strip, (own[0], r1[...], r2[...], r3[...]), order[...], xg, group, each, 0)
    width = xg.shape[1]
    clear_rims(S, half, width)
    mid_rows = group // 2
    for g in range(4):
        a, e = g // 2, g % 2
        rows = pl.ds(g * group, group)
        hat, _ = standardize(xg[rows, :].astype(F32))
        low = (hat * (1.0 + mod[1:2, :]) + mod[0:1, :]).astype(BF16)
        na[rows, :] = low
        h = low.astype(F32)
        for part in range(2):
            S[a, e, pl.ds(half + part * (mid_rows + half), mid_rows), :] = h[part * mid_rows : (part + 1) * mid_rows]
        shifted = pltpu.roll(h, 1 if e == 1 else group - 1, 0)
        for lb in range(width // LANES):
            lanes = pl.ds(lb * LANES, LANES)
            moved = shifted[:, lb * LANES : (lb + 1) * LANES] * sides[0 if e == 1 else 1]
            for part in range(2):
                S[a, 2 if e == 1 else 3, pl.ds(half + part * (mid_rows + half), mid_rows), lanes] = (
                    moved[part * mid_rows : (part + 1) * mid_rows]
                )

    def block(lb, carry):
        lanes = pl.ds(pl.multiple_of(lb * LANES, LANES), LANES)
        fill_seam(S, seams, half, lanes)
        taps = [wd[t : t + 1, lanes] for t in range(9)]
        bias = bd[:, lanes]

        def forward(step, inner):
            at = store_row(step, half)
            sources = row_sources(S, at, half, lanes)
            for a in range(2):
                for e in range(2):
                    pre = bias + taps[0] * tap_source(sources, a, e, 0)
                    for t in range(1, 9):
                        pre = pre + taps[t] * tap_source(sources, a, e, t)
                    token = pl.ds(pl.multiple_of((2 * a + e) * group + step * half, half), half)
                    conv[token, lanes] = pre.astype(BF16)
            return inner

        return lax.fori_loop(0, half, forward, carry)

    lax.fori_loop(0, width // LANES, block, 0)
    for g in range(4):
        rows = pl.ds(g * group, group)
        cat[:, rows] = conv[rows, :].T


def first_norm(place, own, r1, r2, r3, order, mod, wd, bd, sides, seams, half):
    tokens, model = 4 * half * half, own.shape[2]
    sds = jax.ShapeDtypeStruct
    return pl.pallas_call(
        functools.partial(first_kernel, half),
        grid_spec=pltpu.PrefetchScalarGridSpec(
            num_scalar_prefetch=1,
            grid=(1,),
            in_specs=[
                pl.BlockSpec((1,) + own.shape[1:], lambda i, p: (p[0], 0, 0)),
                whole(r1.shape), whole(r2.shape), whole(r3.shape), whole(order.shape), whole(mod.shape),
                whole(wd.shape), whole(bd.shape), whole(sides.shape), whole(seams.shape),
            ],
            out_specs=[whole((tokens, model)), whole((tokens, model)), whole((model, tokens))],
            scratch_shapes=[
                pltpu.VMEM((2, 4, (half + 3) * half, model), F32),
                pltpu.VMEM((tokens, model), BF16),
            ],
        ),
        out_shape=[sds((tokens, model), BF16), sds((tokens, model), BF16), sds((model, tokens), BF16)],
        compiler_params=pltpu.CompilerParams(vmem_limit_bytes=56 << 20),
        cost_estimate=cost(10),
        name="first_norm",
    )(place, own, r1, r2, r3, order, mod, wd, bd, sides, seams)


def attend_kernel(half, place_ref, cat, wt, bias, mask, wout, bout, mod, xg,
                  qkvt, lse, ot, proj, mid, nb, nbt):
    group = half * half
    model = cat.shape[0]
    for part in range(3):
        rows = pl.ds(part * model, model)
        qkvt[rows, :] = (dot_nn(wt[rows, :], cat[...]) + bias[rows, 0:1]).astype(BF16)
    blocked = mask[...]
    for h in range(HEADS):
        q = qkvt[h * HEAD_DIM : (h + 1) * HEAD_DIM, :]
        k = qkvt[model + h * HEAD_DIM : model + (h + 1) * HEAD_DIM, :]
        v = qkvt[2 * model + h * HEAD_DIM : 2 * model + (h + 1) * HEAD_DIM, :]
        s = dot_tn(k, q) * HEAD_DIM ** (-0.5) + blocked
        top = jnp.max(s, 0, keepdims=True)
        p = jnp.exp(s - top)
        total = jnp.sum(p, 0, keepdims=True)
        p = (p * (1.0 / total)).astype(BF16)
        lse[0, h : h + 1, :] = top + jnp.log(total)
        ot[h * HEAD_DIM : (h + 1) * HEAD_DIM, :] = dot_nn(v, p).astype(BF16)
    projection = dot_tn(ot[...], wout[...]) + bout[...]
    proj[...] = projection
    middle = xg[...].astype(F32) + mod[2:3, :] * projection
    mid[...] = middle
    hat, _ = standardize(middle)
    low = (hat * (1.0 + mod[4:5, :]) + mod[3:4, :]).astype(BF16)
    nb[...] = low
    ordered_rows(place_ref[1], low.T, nbt, slice(None))


def attend(place, cat, wt, bias, mask, wout, bout, mod, xg, half):
    model, tokens = cat.shape
    group = half * half
    sds = jax.ShapeDtypeStruct
    tall = lambda rows: pl.BlockSpec((rows, group), lambda i: (0, i))
    flat = pl.BlockSpec((group, model), lambda i: (i, 0))
    return pl.pallas_call(
        functools.partial(attend_kernel, half),
        grid=(4,),
        in_specs=[
            pl.BlockSpec(memory_space=pltpu.SMEM),
            tall(model), whole(wt.shape), whole(bias.shape), whole(mask.shape), whole(wout.shape),
            whole(bout.shape), whole(mod.shape), flat,
        ],
        out_specs=[tall(3 * model), pl.BlockSpec((1, 16, group), lambda i: (i, 0, 0)), tall(model),
                   flat, flat, flat, tall(model)],
        out_shape=[sds((3 * model, tokens), BF16), sds((4, 16, group), F32), sds((model, tokens), BF16),
                   sds((tokens, model), F32), sds((tokens, model), F32), sds((tokens, model), BF16),
                   sds((model, tokens), BF16)],
        compiler_params=pltpu.CompilerParams(vmem_limit_bytes=56 << 20),
        cost_estimate=cost(26),
        name="attend",
    )(place, cat, wt, bias, mask, wout, bout, mod, xg)


def gate_kernel(half, place_ref, own, r1, r2, r3, order, mod, gg, db, dbt, small):
    group = half * half
    each = own.shape[1] // 4
    take_strip(place_ref[0], (own[0], r1[...], r2[...], r3[...]), order[...], gg, group, each, 0)
    total = jnp.zeros((1, gg.shape[1]), F32)
    for g in range(4):
        rows = pl.ds(g * group, group)
        low = (mod[5:6, :] * gg[rows, :].astype(F32)).astype(BF16)
        db[rows, :] = low
        total = total + jnp.sum(low.astype(F32), 0, keepdims=True)
        ordered_rows(place_ref[1], low.T, dbt, rows)
    small[...] = total


def gate(place, own, r1, r2, r3, order, mod, half):
    tokens, model = 4 * half * half, own.shape[2]
    sds = jax.ShapeDtypeStruct
    return pl.pallas_call(
        functools.partial(gate_kernel, half),
        grid_spec=pltpu.PrefetchScalarGridSpec(
            num_scalar_prefetch=1,
            grid=(1,),
            in_specs=[
                pl.BlockSpec((1,) + own.shape[1:], lambda i, p: (p[0], 0, 0)),
                whole(r1.shape), whole(r2.shape), whole(r3.shape), whole(order.shape), whole(mod.shape),
            ],
            out_specs=[whole((tokens, model)), whole((tokens, model)), whole((model, tokens)), whole((1, model))],
        ),
        out_shape=[sds((tokens, model), BF16), sds((tokens, model), BF16), sds((model, tokens), BF16), sds((1, model), F32)],
        compiler_params=pltpu.CompilerParams(vmem_limit_bytes=56 << 20),
        cost_estimate=cost(5),
        name="gate",
    )(place, own, r1, r2, r3, order, mod)


def give_strip(strip, store, order_back, outs, group, each):
    for k, out in enumerate(outs):
        target = jnp.bitwise_xor(strip, k)
        rows = [store[pl.ds(pl.multiple_of(g * group + target * each, each), each), :] for g in range(4)]
        out[...] = dot_nn(order_back, jnp.concatenate(rows, 0)).astype(out.dtype)


def middle_kernel(half, place_ref, branch, dnb, mid, proj, gg, wout, bfc2, mod, back,
                  o0, o1, o2, o3, dmid, dot_, dpt, small, res):
    step = pl.program_id(0)
    group = half * half

    @pl.when(step == 0)
    def _():
        small[...] = jnp.zeros_like(small)

    full = branch[...] + bfc2[...]
    middle = mid[...]
    g = gg[...].astype(F32)
    res[pl.ds(pl.multiple_of(step * group, group), group), :] = (middle + mod[5:6, :] * full).astype(BF16)
    hat, inv = standardize(middle)
    d = dnb[...]
    d_mid = g + norm_reverse(d * (1.0 + mod[4:5, :]), hat, inv)
    dmid[...] = d_mid
    low = (mod[2:3, :] * d_mid).astype(BF16)
    rows = (
        d_mid * proj[...], d, d * hat, g * full, low.astype(F32),
    )
    for at, value in enumerate(rows):
        small[at : at + 1, :] += jnp.sum(value, 0, keepdims=True)
    dot_[...] = dot_nt(wout[...], low).astype(BF16)
    ordered_rows(place_ref[1], low.T, dpt, slice(None))

    @pl.when(step == pl.num_programs(0) - 1)
    def _():
        give_strip(place_ref[0], res, back[...], (o0, o1, o2, o3), group, back.shape[0] // 4)


def middle(place, branch, dnb, mid, proj, gg, wout, bfc2, mod, back, half):
    tokens, model = mid.shape
    group = half * half
    sds = jax.ShapeDtypeStruct
    tall = pl.BlockSpec((model, group), lambda i: (0, i))
    flat = pl.BlockSpec((group, model), lambda i: (i, 0))
    strip = back.shape[0]
    return pl.pallas_call(
        functools.partial(middle_kernel, half),
        grid=(4,),
        in_specs=[pl.BlockSpec(memory_space=pltpu.SMEM), flat, flat, flat, flat, flat,
                  whole(wout.shape), whole(bfc2.shape), whole(mod.shape), whole(back.shape)],
        out_specs=[whole((strip, model))] * 4 + [flat, tall, tall, whole((8, model))],
        out_shape=[sds((strip, model), BF16)] * 4 + [sds((tokens, model), F32), sds((model, tokens), BF16),
                   sds((model, tokens), BF16), sds((8, model), F32)],
        scratch_shapes=[pltpu.VMEM((tokens, model), BF16)],
        compiler_params=pltpu.CompilerParams(vmem_limit_bytes=56 << 20),
        cost_estimate=cost(12),
        name="middle",
    )(place, branch, dnb, mid, proj, gg, wout, bfc2, mod, back)


def attend_back_kernel(half, span, place_ref, q, k, v, do, ot, lse, mask, cat, dpt, wt,
                       gk, gs, dct, small, catp, acc):
    group = half * half
    step = pl.program_id(0)
    model = cat.shape[0]

    @pl.when(step == 0)
    def _():
        ordered_rows(place_ref[1], cat[...], catp, slice(None))
        acc[...] = jnp.zeros_like(acc)

    blocked = mask[...]
    scale = HEAD_DIM ** (-0.5)
    parts = [[], [], []]
    for h in range(span // HEAD_DIM):
        rows = slice(h * HEAD_DIM, (h + 1) * HEAD_DIM)
        lists = [[], [], []]
        for g in range(4):
            cols = slice(g * group, (g + 1) * group)
            qh, kh, vh, dh = q[rows, cols], k[rows, cols], v[rows, cols], do[rows, cols]
            s = dot_tn(kh, qh) * scale + blocked
            p = jnp.exp(s - lse[g, pl.ds(step * (span // HEAD_DIM) + h, 1), :])
            dp = dot_tn(vh, dh)
            delta = jnp.sum(p * dp, 0, keepdims=True)
            ds = (p * (dp - delta)).astype(BF16)
            lists[0].append((dot_nn(kh, ds) * scale).astype(BF16))
            lists[1].append((dot_nt(qh, ds) * scale).astype(BF16))
            lists[2].append(dot_nt(dh, p.astype(BF16)).astype(BF16))
        for part in range(3):
            parts[part].append(jnp.concatenate(lists[part], 1))
    total = acc[...]
    for part in range(3):
        grads = jnp.concatenate(parts[part], 0)
        if part != 1:
            small[:, (part // 2) * span : (part // 2 + 1) * span] = jnp.sum(grads.astype(F32).T, 0, keepdims=True)
        product = dot_nt(catp[...], grads).astype(BF16)
        gk[part] = product[: model // 2]
        gs[part] = product[model // 2 :]
        total = total + dot_tn(wt[part], grads)
    acc[...] = total
    product = dot_nt(dpt[...], ot[...]).astype(BF16)
    gk[3] = product[: model // 2]
    gs[3] = product[model // 2 :]

    @pl.when(step == pl.num_programs(0) - 1)
    def _():
        dct[...] = acc[...].astype(BF16)


def attend_back(place, qkvt, dot_, ot, lse, mask, cat, dpt, wt, half, span=256):
    model, tokens = cat.shape
    group = half * half
    steps = model // span
    sds = jax.ShapeDtypeStruct
    part = lambda n: pl.BlockSpec((span, tokens), lambda i: (n * steps + i, 0))
    return pl.pallas_call(
        functools.partial(attend_back_kernel, half, span),
        grid=(steps,),
        in_specs=[
            pl.BlockSpec(memory_space=pltpu.SMEM),
            part(0), part(1), part(2), part(0), part(0), whole(lse.shape), whole(mask.shape), whole(cat.shape),
            whole(dpt.shape),
            pl.BlockSpec((3, span, model), lambda i: (0, i, 0)),
        ],
        out_specs=[pl.BlockSpec((4, model // 2, span), lambda i: (0, 0, i))] * 2
        + [whole((model, tokens)), pl.BlockSpec((1, 2 * span), lambda i: (0, i))],
        out_shape=[sds((4, model // 2, model), BF16)] * 2 + [sds((model, tokens), BF16), sds((1, 2 * model), F32)],
        scratch_shapes=[pltpu.VMEM((model, tokens), BF16), pltpu.VMEM((model, tokens), F32)],
        compiler_params=pltpu.CompilerParams(vmem_limit_bytes=58 << 20),
        cost_estimate=cost(30),
        name="attend_back",
    )(place, qkvt, qkvt, qkvt, dot_, ot, lse, mask, cat, dpt, wt.reshape(3, model, model))


def last_kernel(half, place_ref, dct, na, xg, dmid, mod, wd, sides, seams, back,
                o0, o1, o2, o3, small, D, dna, tig):
    group = half * half
    width = xg.shape[1]
    clear_rims(D, half, width)
    mid_rows = group // 2
    for g in range(4):
        a, e = g // 2, g % 2
        rows = pl.ds(g * group, group)
        h = dct[:, rows].T.astype(F32)
        for part in range(2):
            D[a, e, pl.ds(half + part * (mid_rows + half), mid_rows), :] = h[part * mid_rows : (part + 1) * mid_rows]
        shifted = pltpu.roll(h, 1 if e == 1 else group - 1, 0)
        for lb in range(width // LANES):
            lanes = pl.ds(lb * LANES, LANES)
            moved = shifted[:, lb * LANES : (lb + 1) * LANES] * sides[0 if e == 1 else 1]
            for part in range(2):
                D[a, 2 if e == 1 else 3, pl.ds(half + part * (mid_rows + half), mid_rows), lanes] = (
                    moved[part * mid_rows : (part + 1) * mid_rows]
                )

    def block(lb, carry):
        lanes = pl.ds(pl.multiple_of(lb * LANES, LANES), LANES)
        fill_seam(D, seams, half, lanes)
        taps = [wd[t : t + 1, lanes] for t in range(9)]

        def backward(step, sums):
            sums = list(sums)
            at = store_row(step, half)
            sources = row_sources(D, at, half, lanes)
            fold = lambda v: v.reshape(-1, 8, LANES).sum(0)
            for a in range(2):
                for e in range(2):
                    token = pl.ds(pl.multiple_of((2 * a + e) * group + step * half, half), half)
                    hid = na[token, lanes].astype(F32)
                    total = None
                    for t in range(9):
                        x = tap_source(sources, a, e, t)
                        term = taps[8 - t] * x
                        total = term if total is None else total + term
                        sums[8 - t] = sums[8 - t] + fold(hid * x)
                    dna[token, lanes] = total
                    sums[9] = sums[9] + fold(sources[a + 1][e])
                    sums[10] = sums[10] + fold(total)
            return tuple(sums)

        sums = lax.fori_loop(0, half, backward, tuple(jnp.zeros((8, LANES), F32) for _ in range(11)))
        for at, total in enumerate(sums):
            small[at : at + 1, lanes] = jnp.sum(total, 0, keepdims=True)
        return carry

    lax.fori_loop(0, width // LANES, block, 0)
    scale_sum = jnp.zeros((1, width), F32)
    for g in range(4):
        rows = pl.ds(g * group, group)
        hat, inv = standardize(xg[rows, :].astype(F32))
        d = dna[rows, :]
        scale_sum = scale_sum + jnp.sum(d * hat, 0, keepdims=True)
        tig[rows, :] = (dmid[rows, :] + norm_reverse(d * (1.0 + mod[1:2, :]), hat, inv)).astype(BF16)
    small[11:12, :] = scale_sum
    give_strip(place_ref[0], tig, back[...], (o0, o1, o2, o3), group, back.shape[0] // 4)


def last(place, dct, na, xg, dmid, mod, wd, sides, seams, back, half):
    tokens, model = xg.shape
    sds = jax.ShapeDtypeStruct
    args = (dct, na, xg, dmid, mod, wd, sides, seams, back)
    strip = back.shape[0]
    return pl.pallas_call(
        functools.partial(last_kernel, half),
        in_specs=[pl.BlockSpec(memory_space=pltpu.SMEM)] + [whole(v.shape) for v in args],
        out_specs=[whole((strip, model))] * 4 + [whole((16, model))],
        out_shape=[sds((strip, model), BF16)] * 4 + [sds((16, model), F32)],
        scratch_shapes=[pltpu.VMEM((2, 4, (half + 3) * half, model), F32), pltpu.VMEM((tokens, model), F32),
                        pltpu.VMEM((tokens, model), BF16)],
        compiler_params=pltpu.CompilerParams(vmem_limit_bytes=60 << 20),
        cost_estimate=cost(13),
        name="last",
    )(place, *args)


def strip_order(rows, cols):
    m = jnp.arange(rows * cols)
    each, half = rows * cols // 4, cols // 2
    a, e = m // (2 * each), (m // each) % 2
    i, j = (m % each) // half, m % half
    source = (2 * i + a) * cols + 2 * j + e
    return (source[:, None] == m[None, :]).astype(BF16)


def gather_kernel(place_ref, own, c1, c2, c3, out):
    for k, piece in enumerate((own, c1, c2, c3)):
        @pl.when(pl.program_id(0) == k)
        def _():
            out[0] = piece[...].astype(out.dtype)


def gather_strips(place, own, c1, c2, c3, dtype):
    rows, model = own.shape
    return pl.pallas_call(
        gather_kernel,
        grid_spec=pltpu.PrefetchScalarGridSpec(
            num_scalar_prefetch=1,
            grid=(4,),
            in_specs=[whole(own.shape)] * 4,
            out_specs=pl.BlockSpec((1, rows, model), lambda i, p: (jnp.bitwise_xor(p[0], i), 0, 0)),
        ),
        out_shape=jax.ShapeDtypeStruct((4, rows, model), dtype),
        cost_estimate=cost(3),
        name="gather_strips",
    )(place, own, c1, c2, c3)


def swap(values, axis):
    return lax.ppermute(values, axis, [(0, 1), (1, 0)])


def pick(values, at, dim):
    return lax.dynamic_index_in_dim(values, at, dim, keepdims=False)


def add_low(left, right):
    return (left.astype(F32) + right.astype(F32)).astype(BF16)


def scatter_sum(keep, send, z_count):
    parts, rows, width = keep.shape
    total = add_low(keep, swap(send, "core"))
    shard = rows // (4 * z_count)
    total = total.reshape(parts, 2, 2 * z_count, shard, width)
    x = lax.axis_index("x")
    total = add_low(pick(total, x, 1), swap(pick(total, 1 - x, 1), "x"))
    total = total.reshape(parts, z_count, 2, shard, width)
    y = lax.axis_index("y")
    total = add_low(pick(total, y, 2), swap(pick(total, 1 - y, 2), "y"))
    got = lax.all_to_all(total, "z", split_axis=1, concat_axis=1, tiled=True)
    return jnp.sum(got.astype(F32), 1)


def latent_mask(ids, half):
    place = jnp.arange(half)
    quad = (2 * (place[:, None] // (half // 2)) + place[None] // (half // 2)).reshape(-1)
    named = jnp.sum(jnp.where(quad[:, None] == jnp.arange(4)[None], ids[None], 0), 1)
    return jnp.where(named[:, None] == named[None], 0.0, -1e30).astype(F32)


def shards(
    tokens, conditioning, latent_ids, w_ada, b_ada, w_dw1, b_dw1, w_qkv, b_qv, w_out, b_out,
    w_fc1, b_fc1, w_dw2, b_dw2, w_fc2, b_fc2, out_grad,
):
    canvases, rows, cols, model = tokens.shape
    half = cols // 2
    hidden = w_fc1.shape[1]
    core, x = lax.axis_index("core"), lax.axis_index("x")
    z_count = lax.axis_size("z")
    canvas_groups = 2 * z_count
    devices = 4 * canvas_groups
    strip = 2 * x + core
    place = jnp.stack([strip, core]).astype(jnp.int32)
    strips = ("x", "core")

    def exchange(pieces):
        return [lax.ppermute(piece, strips, [(i, i ^ (k + 1)) for i in range(4)]) for k, piece in enumerate(pieces)]

    def to_canvas(values):
        flat = values.reshape(canvases, rows * cols, model)
        got = exchange([pick(flat, jnp.bitwise_xor(strip, k), 0) for k in (1, 2, 3)])
        return [flat] + got

    token_pieces = to_canvas(tokens)
    grad_pieces = to_canvas(out_grad)

    cond_vals = conditioning.astype(F32)
    cond_act = jax.nn.silu(cond_vals).astype(BF16)
    modulation = jnp.dot(cond_act, w_ada, preferred_element_type=F32) + b_ada.astype(F32)
    mod = jnp.pad(pick(modulation, strip, 0).reshape(6, model), ((0, 2), (0, 0)))
    shard = model // devices
    cond_cols = pick(cond_act.reshape(canvases, 4, canvas_groups, shard), strip, 1)
    cond_cols = lax.all_to_all(cond_cols.astype(F32), ("z", "y"), split_axis=1, concat_axis=0, tiled=True)
    cond_cols = cond_cols.reshape(devices, shard).astype(BF16)

    ids = pick(latent_ids, strip, 0)
    sides, seams = seam_masks(ids, cols)
    mask = latent_mask(ids, half)
    order = strip_order(rows, cols)
    back = order.T
    row = lambda b: b.astype(F32)[None]
    bias = jnp.concatenate([b_qv[:model], jnp.zeros((model,), b_qv.dtype), b_qv[model:]]).astype(F32)
    bias = jnp.broadcast_to(bias[:, None], (3 * model, LANES))
    wt = w_qkv.T
    taps_one, taps_two = w_dw1.astype(F32), w_dw2.astype(F32)

    xg, na, cat = first_norm(place, *token_pieces, order, mod, taps_one, row(b_dw1), sides, seams, half)
    qkvt, lse, ot, proj, mid, nb, nbt = attend(
        place, cat, wt, bias, mask, w_out, row(b_out), mod, xg, half
    )
    gg, db, dbt, small_fc2 = gate(place, *grad_pieces, order, mod, half)
    ff_keep, ff_send, small_ff, branch, dnb = feed_forward(
        nb, nbt, db, dbt, w_fc1, row(b_fc1), taps_two, row(b_dw2), w_fc2, sides, seams, half, 256
    )
    *res, dmid, dot_, dpt, small_mid = middle(
        place, branch, dnb, mid, proj, gg, w_out, row(b_fc2), mod, back, half
    )
    res = [res[0]] + exchange(res[1:])
    ff_sum = scatter_sum(ff_keep, ff_send, z_count)
    span = 256
    at_keep, at_send, dct, small_qv = attend_back(
        place, qkvt, dot_, ot, lse, mask, cat, dpt, wt, half, span
    )
    at_sum = scatter_sum(at_keep, at_send, z_count)
    *tig, small_last = last(place, dct, na, xg, dmid, mod, taps_one, sides, seams, back, half)
    tig = [tig[0]] + exchange(tig[1:])

    d_mod = jnp.concatenate(
        [small_last[10], small_last[11], small_mid[0], small_mid[1], small_mid[2], small_mid[3]]
    ).astype(BF16).astype(F32)
    qv = small_qv.reshape(-1, 2, span)
    vectors = (
        small_last[:9], small_last[9], qv[:, 0].reshape(-1), qv[:, 1].reshape(-1), small_mid[4],
        small_ff[10], small_ff[:9], small_ff[9], small_fc2[0],
    )
    def by_shard(v):
        if v.ndim == 1:
            return v.reshape(devices, -1)
        return v.reshape(9, devices, -1).transpose(1, 0, 2).reshape(devices, -1)
    qv_all = jnp.concatenate([vectors[2], vectors[3]])
    listed = [by_shard(v) for v in vectors[:2] + (qv_all,) + vectors[4:]]
    widths = [v.shape[1] for v in listed]
    small = jnp.concatenate(listed, 1)
    count = small.shape[1]
    message = jnp.concatenate(
        [small.reshape(4, canvas_groups * count), jnp.broadcast_to(d_mod[None], (4, d_mod.shape[0]))], 1
    )
    got = lax.all_to_all(message, strips, split_axis=0, concat_axis=0, tiled=True)
    small = jnp.sum(got[:, : canvas_groups * count], 0).reshape(canvas_groups, count)
    d_mod = got[:, canvas_groups * count :]
    message = jnp.concatenate(
        [small, jnp.broadcast_to(d_mod.reshape(1, -1), (canvas_groups, d_mod.size))], 1
    )
    got = lax.all_to_all(message, ("z", "y"), split_axis=0, concat_axis=0, tiled=True)
    small = jnp.sum(got[:, :count], 0)
    d_mod_all = got[:, count:].reshape(devices, -1)
    pieces, at = [], 0
    for width in widths:
        pieces.append(small[at : at + width])
        at += width
    g_w_dw1, g_b_dw1, g_b_qv, g_b_out, g_b_fc1, g_w_dw2, g_b_dw2, g_b_fc2 = pieces

    g_w_ada = lax.dot_general(
        cond_cols, d_mod_all.astype(BF16), (((0,), (0,)), ((), ())), preferred_element_type=F32
    )
    index = strip * canvas_groups + lax.axis_index("z") * 2 + lax.axis_index("y")
    own = d_mod_all.shape[1] // devices
    g_b_ada = lax.dynamic_slice_in_dim(jnp.sum(d_mod_all, 0), index * own, own, 0)
    d_cond = lax.dot_general(
        d_mod.astype(BF16), w_ada, (((1,), (1,)), ((), ())), preferred_element_type=F32
    )
    sigmoid_c = jax.nn.sigmoid(cond_vals)
    grad_cond = d_cond * sigmoid_c * (1.0 + cond_vals * (1.0 - sigmoid_c))
    result = gather_strips(place, *res, BF16).reshape(tokens.shape)
    token_grad = gather_strips(place, *tig, F32).reshape(tokens.shape)
    return (
        result, token_grad, grad_cond, g_w_ada, g_b_ada,
        g_w_dw1.reshape(9, -1), g_b_dw1,
        jnp.concatenate([at_sum[0], at_sum[1], at_sum[2]], 1), g_b_qv,
        at_sum[3].T, g_b_out,
        ff_sum[0], g_b_fc1, g_w_dw2.reshape(9, -1), g_b_dw2, ff_sum[1].T, g_b_fc2,
    )


def solution(mesh):
    strip, canvas = mesh.devices.shape
    finer = Mesh(mesh.devices.reshape(strip // 2, 2, canvas // 2, 2), ("x", "core", "z", "y"))
    strips, groups, every = ("x", "core"), ("z", "y"), ("x", "core", "z", "y")
    block = P(groups, strips, None, None)
    return jax.shard_map(
        shards,
        mesh=finer,
        in_specs=(block, P(groups, None), P(groups, None)) + (P(),) * 14 + (block,),
        out_specs=(
            block, block, P(groups, None), P(every, None), P(every),
            P(None, every), P(every), P(every, None), P(every),
            P(None, every), P(every), P(every, None), P(every),
            P(None, every), P(every), P(None, every), P(every),
        ),
        check_vma=False,
    )
```

```python
import functools
import jax, jax.numpy as jnp
from jax import lax
from jax.sharding import Mesh, PartitionSpec as P
from jax.experimental import pallas as pl
from jax.experimental.pallas import tpu as pltpu

LANES = 128
F32 = jnp.float32
BF16 = jnp.bfloat16


class Order:
    last = ()

    @classmethod
    def passed(cls, outputs):
        cls.last = (outputs[0] if isinstance(outputs, (list, tuple)) else outputs,)
        return outputs


def ordered_call(kernel, in_specs, deps=(), micros=1, vmem=60, prefetch=None, **kw):
    deps = tuple(deps) + Order.last
    front = 0 if prefetch is None else 1
    skip, first = len(deps), front + len(in_specs)

    def body(*refs):
        return kernel(*refs[front:first], *refs[first + skip :])

    in_specs = list(in_specs) + [pl.BlockSpec(memory_space=pl.ANY)] * skip
    if prefetch is None:
        kw["in_specs"] = in_specs
    else:
        inner = {name: kw.pop(name) for name in ("grid", "out_specs")}
        kw["grid_spec"] = pltpu.PrefetchScalarGridSpec(num_scalar_prefetch=1, in_specs=in_specs, **inner)
    call = pl.pallas_call(
        body,
        compiler_params=pltpu.CompilerParams(vmem_limit_bytes=vmem << 20),
        cost_estimate=cost(micros),
        **kw,
    )
    given = () if prefetch is None else (prefetch,)
    return lambda *args: Order.passed(call(*given, *args, *deps))


def my_core():
    return lax.axis_index("core")


def my_strip():
    return 2 * lax.axis_index("x") + lax.axis_index("core")


def dot_nn(left, right):
    return jnp.dot(left, right, preferred_element_type=F32)


def dot_nt(left, right):
    return lax.dot_general(left, right, (((1,), (1,)), ((), ())), preferred_element_type=F32)


def cost(micros):
    return pl.CostEstimate(flops=int(micros * 5e6), bytes_accessed=int(micros * 5e3), transcendentals=0)


KINDS = ((2, 0, 1), (0, 1, 3))


def prep_kernel(half, ids, sides, seams, mask, order, back):
    mid, group = half // 2, half * half
    same = lambda p, q: (ids[0, p] == ids[0, q]).astype(F32)
    shape = (group, LANES)
    spot = lax.broadcasted_iota(jnp.int32, shape, 0)
    place, line = spot % half, spot // half
    top = line < mid
    col = jnp.where(top, same(0, 1), same(2, 3))
    sides[0] = jnp.where(place == 0, 0.0, jnp.where(place == mid, col, 1.0))
    sides[1] = jnp.where(place == half - 1, 0.0, jnp.where(place == mid - 1, col, 1.0))
    place = lax.broadcasted_iota(jnp.int32, (half, LANES), 0)
    rows = jnp.where(place < mid, same(0, 2), same(1, 3))
    down, up = same(0, 3), same(1, 2)
    seams[0] = rows
    seams[1] = jnp.where(place == 0, 0.0, jnp.where(place == mid, down, rows))
    seams[2] = jnp.where(place == half - 1, 0.0, jnp.where(place == mid - 1, up, rows))
    seams[3] = jnp.where(place == 0, 0.0, jnp.where(place == mid, up, rows))
    seams[4] = jnp.where(place == half - 1, 0.0, jnp.where(place == mid - 1, down, rows))

    def named(axis):
        spot = lax.broadcasted_iota(jnp.int32, (group, group), axis)
        upper, left = spot // half < mid, spot % half < mid
        return jnp.where(
            upper, jnp.where(left, ids[0, 0], ids[0, 1]), jnp.where(left, ids[0, 2], ids[0, 3])
        )

    mask[...] = jnp.where(named(0) == named(1), 0.0, -1e30)

    def source(axis):
        n = order.shape[0]
        m = lax.broadcasted_iota(jnp.int32, (n, n), axis)
        each = n // 4
        a, e = m // (2 * each), (m // each) % 2
        i, j = (m % each) // half, m % half
        return (2 * i + a) * 2 * half + 2 * j + e, lax.broadcasted_iota(jnp.int32, (n, n), 1 - axis)

    wanted, here = source(0)
    order[...] = jnp.where(wanted == here, 1.0, 0.0).astype(BF16)
    wanted, here = source(1)
    back[...] = jnp.where(wanted == here, 1.0, 0.0).astype(BF16)


def prep(ids, half, strip_rows):
    group = half * half
    sds = jax.ShapeDtypeStruct
    shapes = [sds((2, group, LANES), F32), sds((5, half, LANES), F32), sds((group, group), F32),
              sds((strip_rows, strip_rows), BF16), sds((strip_rows, strip_rows), BF16)]
    return ordered_call(
        functools.partial(prep_kernel, half),
        [pl.BlockSpec(memory_space=pltpu.SMEM)],
        out_specs=[pl.BlockSpec(v.shape) for v in shapes],
        out_shape=shapes,
        micros=3,
        name="prep",
    )(ids)


def clear_rims(store, half, width):
    zero = jnp.zeros((half, width), F32)
    for a in range(2):
        for kind in range(4):
            store[a, kind, 0:half, :] = zero
            store[a, kind, (half + 2) * half : (half + 3) * half, :] = zero


def fill_seam(store, seams, half, lanes):
    mid = half // 2
    seam_at = pl.ds((mid + 1) * half, half)
    for a, source, left_id, right_id in ((1, mid, 1, 2), (0, mid + 2, 3, 4)):
        rows = pl.ds(source * half, half)
        even = store[a, 0, rows, lanes]
        odd = store[a, 1, rows, lanes]
        store[a, 0, seam_at, lanes] = even * seams[0]
        store[a, 1, seam_at, lanes] = odd * seams[0]
        store[a, 2, seam_at, lanes] = pltpu.roll(odd, 1, 0) * seams[left_id]
        store[a, 3, seam_at, lanes] = pltpu.roll(even, half - 1, 0) * seams[right_id]


def put_row(store, a, e, place, lanes, value, sides, rows, half):
    store[a, e, place, lanes] = value
    if e == 1:
        store[a, 2, place, lanes] = pltpu.roll(value, 1, 0) * sides[0, rows, :]
    else:
        store[a, 3, place, lanes] = pltpu.roll(value, half - 1, 0) * sides[1, rows, :]


def row_sources(store, at, half, lanes):
    spots = ((1, -1), (0, 0), (1, 0), (0, 1))
    return [
        [store[a, kind, pl.ds(pl.multiple_of((at + off) * half, half), half), lanes] for kind in range(4)]
        for a, off in spots
    ]


def tap_source(sources, a, e, tap):
    return sources[a + tap // 3][KINDS[e][tap % 3]]


def store_row(step, half):
    return step + 1 + (step >= half // 2).astype(jnp.int32)


def gelu_pair(u):
    size = jnp.abs(u)
    decay = jnp.exp2((u * u) * -0.7213475204444817)
    base = 1.0 + 0.23164190 * size
    guess = pl.reciprocal(base, approx=True)
    t = guess * (2.0 - base * guess)
    poly = t * (0.127414796 + t * (-0.142248368 + t * (0.710706870 + t * (-0.726576013 + t * 0.530702714))))
    tail = poly * decay
    share = jnp.where(u >= 0.0, 1.0 - tail, tail)
    return u * share, share + u * (decay * 0.3989422804014327)


def ff_kernel(half, nb, nbt, db, dbt, w1_next, w1_last, w2, w2_next, b1, b1_next, wd, bd, sides, seams,
              grads, small, branch, dnb, S, D, dact, act, dh, held):
    step_at, steps = pl.program_id(0), pl.num_programs(0) - 1
    width = w2.shape[0]
    group, mid = half * half, half // 2
    blocks = [pl.ds(lb * LANES, LANES) for lb in range(width // LANES)]
    now = step_at % 2
    later = 1 - now

    def put_hidden(store, a, w1, bias, which=(0, 1)):
        for e in which:
            rows = pl.ds(pl.multiple_of((2 * a + e) * group, group), group)
            h = dot_nn(nb[rows, :], w1[...]) + bias[...]
            h = h.astype(BF16).astype(F32)
            shifted = pltpu.roll(h, 1 if e == 1 else group - 1, 0)
            for part in range(2):
                cut = slice(part * group // 2, (part + 1) * group // 2)
                place = pl.ds(half + part * (group // 2 + half), group // 2)
                store[a, e, place, :] = h[cut]
                for lb, lanes in enumerate(blocks):
                    moved = shifted[cut, lb * LANES : (lb + 1) * LANES] * sides[1 - e, cut, :]
                    store[a, 3 - e, place, lanes] = moved

    def put_dact(a, weights, which=(0, 1)):
        for e in which:
            rows = pl.ds(pl.multiple_of((2 * a + e) * group, group), group)
            dact[rows, :] = dot_nt(db[rows, :], weights[...])

    tile = 256

    def add_rows(total, left, weights, n, transposed):
        cols = pl.ds(n * tile, tile)
        if transposed:
            total[:, cols] += dot_nt(left[...], weights[cols, :])
        else:
            total[:, cols] += dot_nn(left[...], weights[:, cols])

    def add_gradient(acc, left, right, k):
        cols = pl.ds(k * tile, tile)
        acc[...] += dot_nn(left[:, cols], right[cols, :])

    def close_gradient():
        grads[:, 0:width] = dot_nn(nbt[...], dh[...]).astype(BF16)
        grads[:, width:] = held[...]

    def hold_gradient():
        held[...] = dot_nn(dbt[...], act[...]).astype(BF16)

    def post_back():
        units = [functools.partial(add_rows, dnb, dh, w1_last, n, True) for n in range(nbt.shape[0] // tile)]
        return units + [close_gradient]

    def woven(lines, units):
        done = 0
        for at, line in enumerate(lines):
            line()
            while done < len(units) and (done + 1) * len(lines) <= (at + 1) * len(units):
                units[done]()
                done += 1

    @pl.when(step_at == 0)
    def _():
        for parity in range(2):
            clear_rims(S.at[parity], half, width)
        clear_rims(D, half, width)
        branch[...] = jnp.zeros_like(branch)
        dnb[...] = jnp.zeros_like(dnb)
        dh[...] = jnp.zeros_like(dh)
        held[...] = jnp.zeros_like(held)
        for a in range(2):
            put_hidden(S.at[0], a, w1_last, b1)
            put_dact(a, w2)
        for lanes in blocks:
            fill_seam(S.at[0], seams, half, lanes)

    @pl.when(step_at < steps)
    def _():
        here, there = S.at[now], S.at[later]
        wide_taps = wd[...].astype(F32)
        lane_taps = lambda lb: [wide_taps[t : t + 1, lb * LANES : (lb + 1) * LANES] for t in range(9)]

        def forward():
            def line_of(lb, a_now, line):
                lanes = blocks[lb]
                taps, bias = lane_taps(lb), bd[:, lanes]
                step = a_now * mid + line
                at = step + 1 + a_now
                rows = pl.ds(pl.multiple_of(step * half, half), half)
                place = pl.ds(pl.multiple_of(at * half, half), half)
                sources = row_sources(here, at, half, lanes)
                for a in range(2):
                    for e in range(2):
                        pre = bias + taps[0] * tap_source(sources, a, e, 0)
                        for t in range(1, 9):
                            pre = pre + taps[t] * tap_source(sources, a, e, t)
                        value, slope = gelu_pair(pre)
                        token = pl.ds(pl.multiple_of((2 * a + e) * group + step * half, half), half)
                        act[token, lanes] = value.astype(BF16)
                        d_pre = (dact[token, lanes] * slope).astype(BF16).astype(F32)
                        put_row(D, a, e, place, lanes, d_pre, sides, rows, half)

            units = [functools.partial(put_hidden, there, a, w1_next, b1_next) for a in range(2)] + post_back()
            woven([functools.partial(line_of, lb, a, line) for lb in range(len(blocks)) for a in range(2)
                   for line in range(mid)], units)

        forward()
        for lanes in blocks:
            fill_seam(D, seams, half, lanes)
            fill_seam(there, seams, half, lanes)

        def backward(sums):
            sums = [list(v) for v in sums]
            fold = lambda v: v.reshape(-1, 8, LANES).sum(0)

            def line_of(lb, a_now, line):
                lanes = blocks[lb]
                taps, total_of = lane_taps(lb), sums[lb]
                step = a_now * mid + line
                at = step + 1 + a_now
                place = pl.ds(pl.multiple_of(at * half, half), half)
                sources = row_sources(D, at, half, lanes)
                for a in range(2):
                    for e in range(2):
                        hid = here[a, e, place, lanes]
                        total = None
                        for t in range(9):
                            x = tap_source(sources, a, e, t)
                            term = taps[8 - t] * x
                            total = term if total is None else total + term
                            total_of[8 - t] = total_of[8 - t] + fold(hid * x)
                        d_hid = total.astype(BF16)
                        token = pl.ds(pl.multiple_of((2 * a + e) * group + step * half, half), half)
                        dh[token, lanes] = d_hid
                        total_of[9] = total_of[9] + fold(sources[a + 1][e])
                        total_of[10] = total_of[10] + fold(d_hid.astype(F32))

            units = [functools.partial(add_rows, branch, act, w2, n, False) for n in range(nbt.shape[0] // tile)]
            units += [hold_gradient]
            units += [functools.partial(put_dact, a, w2_next) for a in range(2)]
            woven([functools.partial(line_of, lb, a, line) for lb in range(len(blocks)) for a in range(2)
                   for line in range(mid)], units)
            return tuple(tuple(v) for v in sums)

        zero = jnp.zeros((8, LANES), F32)
        sums = backward(tuple((zero,) * 11 for _ in blocks))
        for lanes, total_of in zip(blocks, sums):
            for at, total in enumerate(total_of):
                small[at : at + 1, lanes] = jnp.sum(total, 0, keepdims=True)

    @pl.when(step_at == steps)
    def _():
        for unit in post_back():
            unit()


def feed_forward(nb, nbt, db, dbt, w1, wd, w2, biases, sides, seams, half, chunk, deps=()):
    tokens, model = nb.shape
    hidden = w1.shape[1]
    padded = (half + 3) * half
    steps = hidden // chunk
    last = lambda i: jnp.maximum(i - 1, 0)
    this = lambda i: jnp.minimum(i, steps - 1)
    ahead = lambda i: jnp.minimum(i + 1, steps - 1)
    column = lambda rows, when, at=0: pl.BlockSpec((rows, chunk), lambda i: (0, at + when(i)))
    flat = lambda when: pl.BlockSpec((chunk, model), lambda i: (when(i), 0))
    sds = jax.ShapeDtypeStruct
    return ordered_call(
        functools.partial(ff_kernel, half),
        [
            whole((tokens, model)), whole((model, tokens)), whole((tokens, model)), whole((model, tokens)),
            column(model, ahead), column(model, last), flat(this), flat(ahead),
            column(1, this), column(1, ahead), column(9, this), column(1, this, steps),
            whole(sides.shape), whole(seams.shape),
        ],
        deps,
        grid=(steps + 1,),
        out_specs=[pl.BlockSpec((model, 2 * chunk), lambda i: (0, last(i)))]
        + [column(16, this), whole((tokens, model)), whole((tokens, model))],
        out_shape=[sds((model, 2 * hidden), BF16)]
        + [sds((16, hidden), F32), sds((tokens, model), F32), sds((tokens, model), F32)],
        scratch_shapes=[
            pltpu.VMEM((2, 2, 4, padded, chunk), F32),
            pltpu.VMEM((2, 4, padded, chunk), F32),
            pltpu.VMEM((tokens, chunk), F32),
            pltpu.VMEM((tokens, chunk), BF16),
            pltpu.VMEM((tokens, chunk), BF16),
            pltpu.VMEM((model, chunk), BF16),
        ],
        micros=70,
        name="feed_forward",
    )(nb, nbt, db, dbt, w1, w1, w2, w2, biases, biases, wd, biases, sides, seams)


HEADS = 12
HEAD_DIM = 64
norm_eps = 1e-06


def dot_tn(left, right):
    return lax.dot_general(left, right, (((0,), (0,)), ((), ())), preferred_element_type=F32)


def whole(shape):
    return pl.BlockSpec(shape, lambda *_: (0,) * len(shape))


def mod_rows(mod):
    width = mod.shape[1] // 6
    return [mod[pl.ds(my_strip(), 1), part * width : (part + 1) * width] for part in range(6)]


def standardize(values):
    centred = values - jnp.mean(values, -1, keepdims=True)
    inv_std = lax.rsqrt(jnp.mean(centred * centred, -1, keepdims=True) + norm_eps)
    return centred * inv_std, inv_std


def norm_reverse(grad_hat, normed_hat, inv_std):
    mean_grad = jnp.mean(grad_hat, -1, keepdims=True)
    mean_cross = jnp.mean(grad_hat * normed_hat, -1, keepdims=True)
    return inv_std * (grad_hat - mean_grad - normed_hat * mean_cross)


def take_strip(strip, pieces, order, store, group, each, part):
    for k, piece in enumerate(pieces):
        source = jnp.bitwise_xor(strip, k)
        moved = dot_nn(order, piece)
        for g in range(4):
            at = pl.multiple_of(g * group + source * each, each)
            store[pl.ds(at, each), :] = moved[g * each : (g + 1) * each].astype(store.dtype)


def first_kernel(half, own, r1, r2, r3, order, mod, wd, bd, sides, seams,
                 xg, na, cat, S, conv):
    group = half * half
    each = own.shape[1] // 4
    strip = my_strip()
    parts_of = mod_rows(mod)
    take_strip(strip, (own[strip], r1[...], r2[...], r3[...]), order[...], xg, group, each, 0)
    width = xg.shape[1]
    clear_rims(S, half, width)
    mid_rows = group // 2
    for g in range(4):
        a, e = g // 2, g % 2
        rows = pl.ds(g * group, group)
        hat, _ = standardize(xg[rows, :].astype(F32))
        low = (hat * (1.0 + parts_of[1]) + parts_of[0]).astype(BF16)
        na[rows, :] = low
        h = low.astype(F32)
        for part in range(2):
            S[a, e, pl.ds(half + part * (mid_rows + half), mid_rows), :] = h[part * mid_rows : (part + 1) * mid_rows]
        shifted = pltpu.roll(h, 1 if e == 1 else group - 1, 0)
        for lb in range(width // LANES):
            lanes = pl.ds(lb * LANES, LANES)
            moved = shifted[:, lb * LANES : (lb + 1) * LANES] * sides[0 if e == 1 else 1]
            for part in range(2):
                S[a, 2 if e == 1 else 3, pl.ds(half + part * (mid_rows + half), mid_rows), lanes] = (
                    moved[part * mid_rows : (part + 1) * mid_rows]
                )

    def block(lb, carry):
        lanes = pl.ds(pl.multiple_of(lb * LANES, LANES), LANES)
        fill_seam(S, seams, half, lanes)
        wide_taps = wd[:, lanes].astype(F32)
        taps = [wide_taps[t : t + 1] for t in range(9)]
        bias = bd[:, lanes]

        def forward(step, inner):
            at = store_row(step, half)
            sources = row_sources(S, at, half, lanes)
            for a in range(2):
                for e in range(2):
                    pre = bias + taps[0] * tap_source(sources, a, e, 0)
                    for t in range(1, 9):
                        pre = pre + taps[t] * tap_source(sources, a, e, t)
                    token = pl.ds(pl.multiple_of((2 * a + e) * group + step * half, half), half)
                    conv[token, lanes] = pre.astype(BF16)
            return inner

        return lax.fori_loop(0, half, forward, carry)

    lax.fori_loop(0, width // LANES, block, 0)
    for g in range(4):
        rows = pl.ds(g * group, group)
        cat[:, rows] = conv[rows, :].T


def first_norm(own, r1, r2, r3, order, mod, wd, biases, sides, seams, half, at, deps=()):
    tokens, model = 4 * half * half, own.shape[2]
    sds = jax.ShapeDtypeStruct
    return ordered_call(
        functools.partial(first_kernel, half),
        [
            whole(own.shape), whole(r1.shape), whole(r2.shape), whole(r3.shape), whole(order.shape),
            whole(mod.shape), whole(wd.shape), pl.BlockSpec((1, model), lambda i: (0, at)),
            whole(sides.shape), whole(seams.shape),
        ],
        deps,
        grid=(1,),
        out_specs=[whole((tokens, model)), whole((tokens, model)), whole((model, tokens))],
        scratch_shapes=[
            pltpu.VMEM((2, 4, (half + 3) * half, model), F32),
            pltpu.VMEM((tokens, model), BF16),
        ],
        out_shape=[sds((tokens, model), BF16), sds((tokens, model), BF16), sds((model, tokens), BF16)],
        micros=10,
        name="first_norm",
    )(own, r1, r2, r3, order, mod, wd, biases, sides, seams)


def attend_kernel(half, cat, wt, bias, mask, wout, bout, mod, xg, perm,
                  qkvt, lse, ot, proj, mid, nb, nbt):
    group = half * half
    model = cat.shape[0]
    parts_of = mod_rows(mod)
    pick_row = (lax.broadcasted_iota(jnp.int32, (8, group), 0) == 0).astype(BF16)
    for part in range(3):
        rows = pl.ds(part * model, model)
        product = dot_nn(wt[rows, :], cat[...])
        if part != 1:
            own = bias[:, (part // 2) * model : (part // 2 + 1) * model].astype(BF16)
            product = product + dot_tn(jnp.broadcast_to(own, (8, model)), pick_row)
        qkvt[rows, :] = product.astype(BF16)
    blocked = mask[...]
    for h in range(HEADS):
        q = qkvt[h * HEAD_DIM : (h + 1) * HEAD_DIM, :]
        k = qkvt[model + h * HEAD_DIM : model + (h + 1) * HEAD_DIM, :]
        v = qkvt[2 * model + h * HEAD_DIM : 2 * model + (h + 1) * HEAD_DIM, :]
        s = dot_tn(k, q) * HEAD_DIM ** (-0.5) + blocked
        top = jnp.max(s, 0, keepdims=True)
        p = jnp.exp(s - top)
        total = jnp.sum(p, 0, keepdims=True)
        p = (p * (1.0 / total)).astype(BF16)
        lse[0, h : h + 1, :] = top + jnp.log(total)
        ot[h * HEAD_DIM : (h + 1) * HEAD_DIM, :] = dot_nn(v, p).astype(BF16)
    projection = dot_tn(ot[...], wout[...]) + bout[...]
    proj[...] = projection
    middle = xg[...].astype(F32) + parts_of[2] * projection
    mid[...] = middle
    hat, _ = standardize(middle)
    low = (hat * (1.0 + parts_of[4]) + parts_of[3]).astype(BF16)
    nb[...] = low
    nbt[...] = low.T


def attend(cat, wt, biases, mask, wout, mod, xg, perm, half, at_qv, at_out, deps=()):
    model, tokens = cat.shape
    group = half * half
    sds = jax.ShapeDtypeStruct
    tall = lambda rows: pl.BlockSpec((rows, group), lambda i: (0, i))
    flat = pl.BlockSpec((group, model), lambda i: (i, 0))
    return ordered_call(
        functools.partial(attend_kernel, half),
        [
            tall(model), whole(wt.shape), pl.BlockSpec((1, 2 * model), lambda i: (0, at_qv)),
            whole(mask.shape), whole(wout.shape), pl.BlockSpec((1, model), lambda i: (0, at_out)),
            whole(mod.shape), flat, whole(perm.shape),
        ],
        deps,
        grid=(4,),
        out_specs=[tall(3 * model), pl.BlockSpec((1, 16, group), lambda i: (i, 0, 0)), tall(model),
                   flat, flat, flat, tall(model)],
        out_shape=[sds((3 * model, tokens), BF16), sds((4, 16, group), F32), sds((model, tokens), BF16),
                   sds((tokens, model), F32), sds((tokens, model), F32), sds((tokens, model), BF16),
                   sds((model, tokens), BF16)],
        micros=26,
        name="attend",
    )(cat, wt, biases, mask, wout, biases, mod, xg, perm)


def gate_kernel(half, own, r1, r2, r3, order, mod, perm, gg, db, dbt, small):
    group = half * half
    each = own.shape[1] // 4
    parts_of = mod_rows(mod)
    strip = my_strip()
    take_strip(strip, (own[strip], r1[...], r2[...], r3[...]), order[...], gg, group, each, 0)
    total = jnp.zeros((1, gg.shape[1]), F32)
    for g in range(4):
        rows = pl.ds(g * group, group)
        low = (parts_of[5] * gg[rows, :].astype(F32)).astype(BF16)
        db[rows, :] = low
        total = total + jnp.sum(low.astype(F32), 0, keepdims=True)
        dbt[:, rows] = low.T
    small[...] = total


def gate(own, r1, r2, r3, order, mod, perm, half, deps=()):
    tokens, model = 4 * half * half, own.shape[2]
    sds = jax.ShapeDtypeStruct
    args = (own, r1, r2, r3, order, mod, perm)
    return ordered_call(
        functools.partial(gate_kernel, half),
        [whole(v.shape) for v in args],
        deps,
        grid=(1,),
        out_specs=[whole((tokens, model)), whole((tokens, model)), whole((model, tokens)), whole((1, model))],
        out_shape=[sds((tokens, model), BF16), sds((tokens, model), BF16), sds((model, tokens), BF16), sds((1, model), F32)],
        micros=5,
        name="gate",
    )(*args)


def give_strip(strip, store, order_back, outs, group, each):
    for k, out in enumerate(outs):
        target = jnp.bitwise_xor(strip, k)
        rows = [store[pl.ds(pl.multiple_of(g * group + target * each, each), each), :] for g in range(4)]
        out[...] = dot_nn(order_back, jnp.concatenate(rows, 0)).astype(out.dtype)


def middle_kernel(half, branch, dnb, mid, proj, gg, wout, bfc2, mod, back, perm,
                  o0, o1, o2, o3, dmid, dot_, dpt, small, res):
    step = pl.program_id(0)
    group = half * half
    parts_of = mod_rows(mod)

    @pl.when(step == 0)
    def _():
        small[...] = jnp.zeros_like(small)

    full = branch[...] + bfc2[...]
    middle = mid[...]
    g = gg[...].astype(F32)
    res[pl.ds(pl.multiple_of(step * group, group), group), :] = (middle + parts_of[5] * full).astype(BF16)
    hat, inv = standardize(middle)
    d = dnb[...]
    d_mid = g + norm_reverse(d * (1.0 + parts_of[4]), hat, inv)
    dmid[...] = d_mid
    low = (parts_of[2] * d_mid).astype(BF16)
    rows = (
        d_mid * proj[...], d, d * hat, g * full, low.astype(F32),
    )
    for at, value in enumerate(rows):
        small[at : at + 1, :] += jnp.sum(value, 0, keepdims=True)
    dot_[...] = dot_nt(wout[...], low).astype(BF16)
    dpt[...] = dot_nt(perm[...], low).astype(BF16)

    @pl.when(step == pl.num_programs(0) - 1)
    def _():
        give_strip(my_strip(), res, back[...], (o0, o1, o2, o3), group, back.shape[0] // 4)


def middle(branch, dnb, mid, proj, gg, wout, biases, mod, back, perm, half, at, deps=()):
    tokens, model = mid.shape
    group = half * half
    sds = jax.ShapeDtypeStruct
    tall = pl.BlockSpec((model, group), lambda i: (0, i))
    flat = pl.BlockSpec((group, model), lambda i: (i, 0))
    strip = back.shape[0]
    return ordered_call(
        functools.partial(middle_kernel, half),
        [flat, flat, flat, flat, flat, whole(wout.shape), pl.BlockSpec((1, model), lambda i: (0, at)),
         whole(mod.shape), whole(back.shape), whole(perm.shape)],
        deps,
        grid=(4,),
        out_specs=[whole((strip, model))] * 4 + [flat, tall, tall, whole((8, model))],
        out_shape=[sds((strip, model), BF16)] * 4 + [sds((tokens, model), F32), sds((model, tokens), BF16),
                   sds((model, tokens), BF16), sds((8, model), F32)],
        scratch_shapes=[pltpu.VMEM((tokens, model), BF16)],
        micros=12,
        name="middle",
    )(branch, dnb, mid, proj, gg, wout, biases, mod, back, perm)


def attend_back_kernel(half, span, q, k, v, do, ot, lse, mask, cat, dpt, perm, wt,
                       gk1, gk2, gs1, gs2, dct, small, catp, acc):
    group = half * half
    step = pl.program_id(0)
    model = cat.shape[0]

    @pl.when(step == 0)
    def _():
        catp[...] = dot_nn(perm[...], cat[...]).astype(BF16)
        acc[...] = jnp.zeros_like(acc)

    blocked = mask[...]
    scale = HEAD_DIM ** (-0.5)
    parts = [[], [], []]
    for h in range(span // HEAD_DIM):
        rows = slice(h * HEAD_DIM, (h + 1) * HEAD_DIM)
        lists = [[], [], []]
        for g in range(4):
            cols = slice(g * group, (g + 1) * group)
            qh, kh, vh, dh = q[rows, cols], k[rows, cols], v[rows, cols], do[rows, cols]
            s = dot_tn(kh, qh) * scale + blocked
            p = jnp.exp(s - lse[g, pl.ds(step * (span // HEAD_DIM) + h, 1), :])
            dp = dot_tn(vh, dh)
            delta = jnp.sum(p * dp, 0, keepdims=True)
            ds = (p * (dp - delta)).astype(BF16)
            lists[0].append((dot_nn(kh, ds) * scale).astype(BF16))
            lists[1].append((dot_nt(qh, ds) * scale).astype(BF16))
            lists[2].append(dot_nt(dh, p.astype(BF16)).astype(BF16))
        for part in range(3):
            parts[part].append(jnp.concatenate(lists[part], 1))
    total = acc[...]
    for part in range(3):
        grads = jnp.concatenate(parts[part], 0)
        if part != 1:
            small[part // 2 : part // 2 + 1, :] = jnp.sum(grads.astype(F32).T, 0, keepdims=True)
        product = dot_nt(catp[...], grads).astype(BF16)
        (gk1, gk2)[part // 2][part % 2] = product[: model // 2]
        (gs1, gs2)[part // 2][part % 2] = product[model // 2 :]
        total = total + dot_tn(wt[part], grads)
    acc[...] = total
    product = dot_nt(dpt[...], ot[...]).astype(BF16)
    gk2[1] = product[: model // 2]
    gs2[1] = product[model // 2 :]

    @pl.when(step == pl.num_programs(0) - 1)
    def _():
        dct[...] = acc[...].astype(BF16)


def attend_back(qkvt, dot_, ot, lse, mask, cat, dpt, perm, wt, half, span, deps=()):
    model, tokens = cat.shape
    steps = model // span
    sds = jax.ShapeDtypeStruct
    part = lambda n: pl.BlockSpec((span, tokens), lambda i: (n * steps + i, 0))
    return ordered_call(
        functools.partial(attend_back_kernel, half, span),
        [
            part(0), part(1), part(2), part(0), part(0), whole(lse.shape), whole(mask.shape), whole(cat.shape),
            whole(dpt.shape), whole(perm.shape), pl.BlockSpec((3, span, model), lambda i: (0, i, 0)),
        ],
        deps,
        grid=(steps,),
        out_specs=[pl.BlockSpec((2, model // 2, span), lambda i: (0, 0, i))] * 4
        + [whole((model, tokens)), pl.BlockSpec((2, span), lambda i: (0, i))],
        out_shape=[sds((2, model // 2, model), BF16)] * 4 + [sds((model, tokens), BF16), sds((2, model), F32)],
        scratch_shapes=[pltpu.VMEM((model, tokens), BF16), pltpu.VMEM((model, tokens), F32)],
        micros=30,
        name="attend_back",
    )(qkvt, qkvt, qkvt, dot_, ot, lse, mask, cat, dpt, perm, wt.reshape(3, model, model))


def conv_back_kernel(half, dct, na, xg, wd, sides, seams, dna, small, D):
    group = half * half
    width = xg.shape[1]
    clear_rims(D, half, width)
    mid_rows = group // 2
    for g in range(4):
        a, e = g // 2, g % 2
        rows = pl.ds(g * group, group)
        h = dct[:, rows].T.astype(F32)
        for part in range(2):
            D[a, e, pl.ds(half + part * (mid_rows + half), mid_rows), :] = h[part * mid_rows : (part + 1) * mid_rows]
        shifted = pltpu.roll(h, 1 if e == 1 else group - 1, 0)
        for lb in range(width // LANES):
            lanes = pl.ds(lb * LANES, LANES)
            moved = shifted[:, lb * LANES : (lb + 1) * LANES] * sides[0 if e == 1 else 1]
            for part in range(2):
                D[a, 2 if e == 1 else 3, pl.ds(half + part * (mid_rows + half), mid_rows), lanes] = (
                    moved[part * mid_rows : (part + 1) * mid_rows]
                )

    def block(lb, carry):
        lanes = pl.ds(pl.multiple_of(lb * LANES, LANES), LANES)
        fill_seam(D, seams, half, lanes)
        wide_taps = wd[:, lanes].astype(F32)
        taps = [wide_taps[t : t + 1] for t in range(9)]

        def backward(step, sums):
            sums = list(sums)
            at = store_row(step, half)
            sources = row_sources(D, at, half, lanes)
            fold = lambda v: v.reshape(-1, 8, LANES).sum(0)
            for a in range(2):
                for e in range(2):
                    token = pl.ds(pl.multiple_of((2 * a + e) * group + step * half, half), half)
                    hid = na[token, lanes].astype(F32)
                    total = None
                    for t in range(9):
                        x = tap_source(sources, a, e, t)
                        term = taps[8 - t] * x
                        total = term if total is None else total + term
                        sums[8 - t] = sums[8 - t] + fold(hid * x)
                    dna[token, lanes] = total
                    sums[9] = sums[9] + fold(sources[a + 1][e])
                    sums[10] = sums[10] + fold(total)
            return tuple(sums)

        sums = lax.fori_loop(0, half, backward, tuple(jnp.zeros((8, LANES), F32) for _ in range(11)))
        for at, total in enumerate(sums):
            small[at : at + 1, lanes] = jnp.sum(total, 0, keepdims=True)
        return carry

    lax.fori_loop(0, width // LANES, block, 0)
    scale_sum = jnp.zeros((1, width), F32)
    for g in range(4):
        rows = pl.ds(g * group, group)
        hat, _ = standardize(xg[rows, :].astype(F32))
        scale_sum = scale_sum + jnp.sum(dna[rows, :] * hat, 0, keepdims=True)
    small[11:12, :] = scale_sum


def conv_back(dct, na, xg, wd, sides, seams, half, deps=()):
    tokens, model = xg.shape
    sds = jax.ShapeDtypeStruct
    args = (dct, na, xg, wd, sides, seams)
    return ordered_call(
        functools.partial(conv_back_kernel, half),
        [whole(v.shape) for v in args],
        deps,
        grid=(1,),
        out_specs=[whole((tokens, model)), whole((16, model))],
        out_shape=[sds((tokens, model), F32), sds((16, model), F32)],
        scratch_shapes=[pltpu.VMEM((2, 4, (half + 3) * half, model), F32)],
        micros=11,
        name="conv_back",
    )(*args)


def last_kernel(half, dna, xg, dmid, mod, back, o0, o1, o2, o3, tig):
    group = half * half
    parts_of = mod_rows(mod)
    for g in range(4):
        rows = pl.ds(g * group, group)
        hat, inv = standardize(xg[rows, :].astype(F32))
        change = norm_reverse(dna[rows, :] * (1.0 + parts_of[1]), hat, inv)
        tig[rows, :] = (dmid[rows, :] + change).astype(BF16)
    give_strip(my_strip(), tig, back[...], (o0, o1, o2, o3), group, back.shape[0] // 4)


def last(dna, xg, dmid, mod, back, half, deps=()):
    tokens, model = xg.shape
    args = (dna, xg, dmid, mod, back)
    strip = back.shape[0]
    return ordered_call(
        functools.partial(last_kernel, half),
        [whole(v.shape) for v in args],
        deps,
        grid=(1,),
        out_specs=[whole((strip, model))] * 4,
        out_shape=[jax.ShapeDtypeStruct((strip, model), BF16)] * 4,
        scratch_shapes=[pltpu.VMEM((tokens, model), BF16)],
        micros=5,
        name="last",
    )(*args)


def cut_kernel(source, o1, o2, o3):
    strip = my_strip()
    for k, out in enumerate((o1, o2, o3)):
        out[...] = source[jnp.bitwise_xor(strip, k + 1)]


def cut_strips(values, deps=()):
    shape = jax.ShapeDtypeStruct(values.shape[1:], values.dtype)
    return ordered_call(
        cut_kernel,
        [whole(values.shape)],
        deps,
        grid=(1,),
        out_specs=[whole(shape.shape)] * 3,
        out_shape=[shape] * 3,
        micros=2,
        name="cut_strips",
    )(values)


def gather_kernel(own, c1, c2, c3, out):
    strip = my_strip()
    for k, piece in enumerate((own, c1, c2, c3)):
        out[jnp.bitwise_xor(strip, k)] = piece[...].astype(out.dtype)


def gather_strips(own, c1, c2, c3, dtype, deps=()):
    rows, model = own.shape
    return ordered_call(
        gather_kernel,
        [whole(own.shape)] * 4,
        deps,
        grid=(1,),
        out_specs=whole((4, rows, model)),
        out_shape=jax.ShapeDtypeStruct((4, rows, model), dtype),
        micros=3,
        name="gather_strips",
    )(own, c1, c2, c3)


def swap(values, axis):
    return lax.ppermute(values, axis, [(0, 1), (1, 0)])


def fold_kernel(count, *refs):
    ins, outs = refs[: 2 * count], refs[2 * count :]
    for at, out in enumerate(outs):
        total = ins[at * count][...].astype(F32)
        for term in ins[at * count + 1 : (at + 1) * count]:
            total = total + term[...].astype(F32)
        out[...] = total.astype(BF16)


def spread_kernel(count, z_count, *refs):
    ins, out = refs[: 2 * count], refs[2 * count]
    for at in range(2):
        total = ins[at * count][0].astype(F32)
        for term in ins[at * count + 1 : (at + 1) * count]:
            total = total + term[0].astype(F32)
        shard = total.shape[0] // z_count
        for z in range(z_count):
            out[z, at, 0] = total[z * shard : (z + 1) * shard].astype(BF16)


def close_kernel(together, got, *outs):
    z_count, _, mine, _, width = got.shape
    part = 0
    for count, out in zip(together, outs):
        for at in range(count):
            total = got[0, part // mine, part % mine].astype(F32)
            for z in range(1, z_count):
                total = total + got[z, part // mine, part % mine].astype(F32)
            out[:, at * width : (at + 1) * width] = total
            part += 1


class SumOverAll:
    def __init__(self, place, keep, send, z_count):
        keep = [v.reshape((-1,) + v.shape[-2:]) for v in keep]
        self.place, self.z_count, self.keep = place, z_count, keep
        self.mine_parts, self.rows, self.width = keep[0].shape
        self.quarter = self.rows // 4
        self.block = min(1536, self.width)
        self.other = [swap(v.reshape((-1,) + v.shape[-2:]), "core") for v in send]

    def fold(self, terms, halves, name, spread=False, deps=()):
        first = len(terms[0])
        specs, args = [], []
        for side in terms:
            for array, row in side:
                def index(p, h, n, place, row=row):
                    return p, row(h, place[0], place[1]), n

                specs.append(pl.BlockSpec((1, self.quarter, self.block), index))
                args.append(array)
        mine = self.mine_parts
        if spread:
            shard = self.quarter // self.z_count
            out_specs = pl.BlockSpec(
                (self.z_count, 2, 1, shard, self.block), lambda p, h, n, place: (0, 0, p, 0, n)
            )
            out_shape = jax.ShapeDtypeStruct((self.z_count, 2, mine, shard, self.width), BF16)
            kernel = functools.partial(spread_kernel, first, self.z_count)
        else:
            out_specs = [pl.BlockSpec((1, self.quarter, self.block), lambda p, h, n, place: (p, h, n))] * 2
            out_shape = [jax.ShapeDtypeStruct((mine, halves * self.quarter, self.width), BF16)] * 2
            kernel = functools.partial(fold_kernel, first)
        return ordered_call(
            kernel,
            specs,
            deps,
            grid=(mine, halves, self.width // self.block),
            out_specs=out_specs,
            out_shape=out_shape,
            prefetch=self.place,
            micros=2,
            name=name,
        )(*args)

    def second(self):
        (k1, k2), (r1, r2) = self.keep, self.other
        away_x = lambda h, x, y: 2 * (1 - x) + h
        away_y = lambda h, x, y: 2 * h + (1 - y)
        a, b = self.fold([[(k1, away_x), (r1, away_x)], [(k2, away_y), (r2, away_y)]], 2, "fold_second")
        self.got_a, self.got_b = swap(a, "x"), swap(b, "y")
        return a, b

    def third(self):
        (k1, k2), (r1, r2) = self.keep, self.other
        near = lambda h, x, y: 2 * x + (1 - y)
        far = lambda h, x, y: 2 * (1 - x) + y
        a, b = self.fold(
            [
                [(k1, near), (r1, near), (self.got_a, lambda h, x, y: 1 - y)],
                [(k2, far), (r2, far), (self.got_b, lambda h, x, y: 1 - x)],
            ],
            1, "fold_third",
        )
        self.last_a, self.last_b = swap(a, "y"), swap(b, "x")
        return a, b

    def fourth(self, deps=()):
        (k1, k2), (r1, r2) = self.keep, self.other
        own = lambda h, x, y: 2 * x + y
        zero = lambda h, x, y: 0
        self.mine = self.fold(
            [
                [(k1, own), (r1, own), (self.got_a, lambda h, x, y: y), (self.last_a, zero)],
                [(k2, own), (r2, own), (self.got_b, lambda h, x, y: x), (self.last_b, zero)],
            ],
            1, "fold_fourth", True, deps,
        )
        return (self.mine,)

    def finish(self, together, deps=()):
        got = lax.all_to_all(self.mine, "z", split_axis=0, concat_axis=0, tiled=True)
        shard = got.shape[3]
        shapes = [jax.ShapeDtypeStruct((shard, count * self.width), F32) for count in together]
        return ordered_call(
            functools.partial(close_kernel, together),
            [whole(got.shape)],
            deps,
            grid=(1,),
            out_specs=[whole(v.shape) for v in shapes],
            out_shape=shapes,
            micros=2,
            name="close_sums",
        )(got)


MODS = 6


def pack_kernel(groups, ff, fc2, mid, qv, last, o0, o1, o2, o3, work):
    work[...] = jnp.zeros_like(work)
    model = last.shape[1]
    strip_width = model // 4
    d_mod = [last[10:11, :], last[11:12, :]] + [mid[k : k + 1, :] for k in range(4)]
    short = [last[k : k + 1, :] for k in range(10)] + [mid[4:5, :], fc2[...]]
    for t in range(4):
        work[t, 0:11, :] = ff[0:11, t * model : (t + 1) * model]
        for k, row in enumerate(d_mod):
            work[t, 11 + k : 12 + k, :] = row
        for k, row in enumerate(short):
            work[t, 17 + k : 18 + k, 0:strip_width] = row[:, t * strip_width : (t + 1) * strip_width]
        at = (2 * t * strip_width) % model
        work[t, 29:30, 0 : 2 * strip_width] = qv[t // 2 : t // 2 + 1, at : at + 2 * strip_width]
    for k, out in enumerate((o0, o1, o2, o3)):
        out[...] = work[jnp.bitwise_xor(my_strip(), k)].astype(BF16)


def pack(ff, fc2, mid, qv, last, groups, deps=()):
    args = (ff, fc2, mid, qv, last)
    model = last.shape[1]
    return ordered_call(
        functools.partial(pack_kernel, groups),
        [whole(v.shape) for v in args],
        deps,
        grid=(1,),
        out_specs=[whole((32, model))] * 4,
        out_shape=[jax.ShapeDtypeStruct((32, model), BF16)] * 4,
        scratch_shapes=[pltpu.VMEM((4, 32, model), F32)],
        micros=2,
        name="pack_small",
    )(*args)


def repack_kernel(groups, g0, g1, g2, g3, cond, out, mods, work, common):
    model = g0.shape[1]
    work[...] = jnp.zeros_like(work)
    values = [g[...].astype(F32) for g in (g0, g1, g2, g3)]
    total = values[0] + values[1] + values[2] + values[3]
    lanes = model // LANES
    head = MODS * lanes * 4
    for part in range(MODS):
        for lb in range(lanes):
            for k in range(4):
                at = (part * lanes + lb) * 4 + jnp.bitwise_xor(my_strip(), k)
                row = values[k][11 + part : 12 + part, lb * LANES : (lb + 1) * LANES]
                common[pl.ds(at, 1), :] = row
    for part in range(MODS):
        for lb in range(lanes):
            at = (part * lanes + lb) * 4
            mods[:, (part * lanes + lb) * LANES : (part * lanes + lb + 1) * LANES] = common[at : at + 4, :].astype(BF16)
    wide, thin = model // groups, model // 4 // groups
    for u in range(groups):
        work[u, 0:11, 0:wide] = total[0:11, u * wide : (u + 1) * wide]
        work[u, 17:29, 0:thin] = total[17:29, u * thin : (u + 1) * thin]
        work[u, 29:30, 0 : 2 * thin] = total[29:30, 2 * u * thin : 2 * (u + 1) * thin]
        work[u, 32:36, 0:thin] = cond[:, u * thin : (u + 1) * thin].astype(F32)
        out[u, 0:head, :] = common[...].astype(BF16)
        out[u, head:, :] = work[u].astype(BF16)


def repack(got, cond, groups, deps=()):
    model = got[0].shape[1]
    head = MODS * (model // LANES) * 4
    args = (*got, cond)
    shapes = [(groups, head + 48, LANES), (4, MODS * model)]
    return ordered_call(
        functools.partial(repack_kernel, groups),
        [whole(v.shape) for v in args],
        deps,
        grid=(1,),
        out_specs=[whole(v) for v in shapes],
        out_shape=[jax.ShapeDtypeStruct(v, BF16) for v in shapes],
        scratch_shapes=[pltpu.VMEM((groups, 48, LANES), F32), pltpu.VMEM((head, LANES), F32)],
        micros=2,
        name="repack_small",
    )(*args)


def unpack_kernel(groups, got, wada, bada, *refs):
    outs, (mods, conds) = refs[:-2], refs[-2:]
    head = got.shape[1] - 48
    total = jnp.sum(got[:, head:, :].astype(F32), 0)
    rows = ((0, 9), (9, 10), (10, 11), (17, 26), (26, 27), (27, 28), (28, 29), (29, 30))
    for (first, end), out in zip(rows, outs):
        out[...] = total[first:end, 0 : out.shape[1]]
    for u in range(groups):
        values = got[u].astype(F32)
        conds[u * 4 : (u + 1) * 4, :] = values[head + 32 : head + 36]
        for block in range(head // 4):
            mods[u * 4 : (u + 1) * 4, block * LANES : (block + 1) * LANES] = values[block * 4 : block * 4 + 4]
    shard, own = wada.shape[0], bada.shape[1]
    wada[...] = dot_tn(conds[...].astype(BF16), mods[...].astype(BF16))[0:shard]
    index = my_strip() * groups + lax.axis_index("z") * 2 + lax.axis_index("y")
    summed = jnp.broadcast_to(jnp.sum(mods[...], 0, keepdims=True), (8, mods.shape[1]))
    bada[...] = pltpu.roll(summed, mods.shape[1] - own * index, 1)[0:1, 0:own]


def unpack(got, model, groups, deps=()):
    wide, thin = model // groups, model // 4 // groups
    shapes = [(thin, MODS * model), (1, MODS * thin)]
    shapes += [(9, wide), (1, wide), (1, wide), (9, thin), (1, thin), (1, thin), (1, thin), (1, 2 * thin)]
    return ordered_call(
        functools.partial(unpack_kernel, groups),
        [whole(got.shape)],
        deps,
        grid=(1,),
        out_specs=[whole(v) for v in shapes],
        out_shape=[jax.ShapeDtypeStruct(v, F32) for v in shapes],
        scratch_shapes=[pltpu.VMEM((4 * groups, MODS * model), F32), pltpu.VMEM((4 * groups, LANES), F32)],
        micros=2,
        name="unpack_small",
    )(got)


def split_kernel(chunk, got, w1, w2):
    for at in range(w1.shape[1] // chunk):
        w1[:, at * chunk : (at + 1) * chunk] = got[:, 2 * at * chunk : (2 * at + 1) * chunk].astype(F32)
        w2[:, at * chunk : (at + 1) * chunk] = got[:, (2 * at + 1) * chunk : 2 * (at + 1) * chunk].astype(F32)


def split_parts(got, chunk, deps=()):
    shape = jax.ShapeDtypeStruct((got.shape[0], got.shape[1] // 2), F32)
    return ordered_call(
        functools.partial(split_kernel, chunk),
        [whole(got.shape)],
        deps,
        grid=(1,),
        out_specs=[whole(shape.shape)] * 2,
        out_shape=[shape] * 2,
        micros=2,
        name="split_parts",
    )(got)


def cond_back_kernel(mods, wada, cond, out):
    change = dot_nt(wada[...], mods[...]).T
    values = cond[...].astype(F32)
    gain = 1.0 / (1.0 + jnp.exp(-values))
    out[...] = change * gain * (1.0 + values * (1.0 - gain))


def cond_back(mods, wada, cond, deps=()):
    canvases, model = cond.shape
    tile = model // 3
    return ordered_call(
        cond_back_kernel,
        [whole(mods.shape), pl.BlockSpec((tile, wada.shape[1]), lambda i: (i, 0)),
         pl.BlockSpec((canvases, tile), lambda i: (0, i))],
        deps,
        grid=(3,),
        out_specs=pl.BlockSpec((canvases, tile), lambda i: (0, i)),
        out_shape=jax.ShapeDtypeStruct((canvases, model), F32),
        micros=3,
        name="cond_back",
    )(mods, wada, cond)


def row_order(model, z_count):
    rows = jnp.arange(model, dtype=jnp.int32).reshape(2, 2, z_count, 2, -1)
    rows = jnp.transpose(rows, (1, 0, 3, 2, 4)).reshape(2, -1)
    rows = jnp.where(lax.axis_index("core") == 0, rows, rows[::-1]).reshape(-1)
    return (rows[:, None] == jnp.arange(model, dtype=jnp.int32)[None]).astype(BF16)


def shards(
    tokens, conditioning, latent_ids, w_ada, b_ada, w_dw1, b_dw1, w_qkv, b_qv, w_out, b_out,
    w_fc1, b_fc1, w_dw2, b_dw2, w_fc2, b_fc2, out_grad,
):
    canvases, rows, cols, model = tokens.shape
    half = cols // 2
    hidden = w_fc1.shape[1]
    z_count = lax.axis_size("z")
    groups = 2 * z_count
    devices = 4 * groups
    strip = my_strip()
    strips, every = ("x", "core"), ("x", "core", "z", "y")
    span = 256
    Order.last = ()

    def exchange(pieces):
        return [lax.ppermute(piece, strips, [(i, i ^ (k + 1)) for i in range(4)]) for k, piece in enumerate(pieces)]

    token_rows = tokens.reshape(canvases, rows * cols, model)
    grad_rows = out_grad.reshape(canvases, rows * cols, model)
    token_pieces = exchange(cut_strips(token_rows))

    cond_vals = conditioning.astype(F32)
    cond_act = jax.nn.silu(cond_vals).astype(BF16)
    mod = jnp.dot(cond_act, w_ada, preferred_element_type=F32) + b_ada.astype(F32)
    cond_cols = lax.dynamic_slice_in_dim(cond_act, strip * (model // 4), model // 4, 1)
    place = jnp.stack([lax.axis_index("x"), lax.axis_index("y")]).astype(jnp.int32)
    perm = row_order(model, z_count)

    ids = lax.dynamic_slice_in_dim(latent_ids, strip, 1, 0)
    sides, seams, mask, order, back = prep(ids, half, rows * cols)
    listed = (b_fc1, b_dw2, b_qv, b_dw1, b_out, b_fc2)
    biases = jnp.concatenate(listed).astype(F32)[None]
    places = [sum(v.shape[0] for v in listed[:n]) // listed[n].shape[0] for n in range(6)]
    wt = w_qkv.T

    xg, na, cat = first_norm(
        token_rows, *token_pieces, order, mod, w_dw1, biases, sides, seams, half, places[3], (wt, cond_cols, perm, place)
    )
    grad_pieces = exchange(cut_strips(grad_rows, token_pieces))
    qkvt, lse, ot, proj, mid, nb, nbt = attend(
        cat, wt, biases, mask, w_out, mod, xg, perm, half, places[2], places[4]
    )
    gg, db, dbt, small_fc2 = gate(grad_rows, *grad_pieces, order, mod, perm, half)
    ff_grads, small_ff, branch, dnb = feed_forward(
        nb, nbt, db, dbt, w_fc1, w_dw2, w_fc2, biases, sides, seams, half, 256
    )
    ff_sum = lax.psum_scatter(ff_grads, every, scatter_dimension=0, tiled=True)
    *res, dmid, dot_, dpt, small_mid = middle(
        branch, dnb, mid, proj, gg, w_out, biases, mod, back, perm, half, places[5]
    )
    res = [res[0]] + exchange(res[1:])
    at_k1, at_k2, at_s1, at_s2, dct, small_qv = attend_back(
        qkvt, dot_, ot, lse, mask, cat, dpt, perm, wt, half, span
    )
    at = SumOverAll(place, (at_k1, at_k2), (at_s1, at_s2), z_count)
    at.second()
    dna, small_last = conv_back(dct, na, xg, w_dw1, sides, seams, half)
    tig = last(dna, xg, dmid, mod, back, half, (at.got_a, at.got_b))
    tig = [tig[0]] + exchange(tig[1:])
    message = pack(small_ff, small_fc2, small_mid, small_qv, small_last, groups)
    got = [message[0]] + exchange(message[1:])
    at.third()
    message, d_mod = repack(got, cond_cols, groups)
    token_grad = gather_strips(*tig, F32).reshape(tokens.shape)
    got = lax.all_to_all(message, ("z", "y"), split_axis=0, concat_axis=0, tiled=True)
    at.fourth()
    grad_cond = cond_back(d_mod, w_ada, conditioning)
    g_w_ada, g_b_ada, g_w_dw2, g_b_dw2, g_b_fc1, g_w_dw1, g_b_dw1, g_b_out, g_b_fc2, g_b_qv = unpack(
        got, model, groups
    )
    result = gather_strips(*res, BF16).reshape(tokens.shape)
    g_w_qkv, g_w_out = at.finish((3, 1))
    g_w_fc1, g_w_fc2 = split_parts(ff_sum, 256)
    return (
        result, token_grad, grad_cond, g_w_ada, g_b_ada[0],
        g_w_dw1, g_b_dw1[0], g_w_qkv, g_b_qv[0], g_w_out.T, g_b_out[0],
        g_w_fc1, g_b_fc1[0], g_w_dw2, g_b_dw2[0], g_w_fc2.T, g_b_fc2[0],
    )


def solution(mesh):
    strip, canvas = mesh.devices.shape
    finer = Mesh(mesh.devices.reshape(strip // 2, 2, canvas // 2, 2), ("x", "core", "z", "y"))
    strips, groups, every = ("x", "core"), ("z", "y"), ("x", "core", "z", "y")
    block = P(groups, strips, None, None)
    return jax.shard_map(
        shards,
        mesh=finer,
        in_specs=(block, P(groups, None), P(groups, None)) + (P(),) * 14 + (block,),
        out_specs=(
            block, block, P(groups, None), P(every, None), P(every),
            P(None, every), P(every), P(every, None), P(every),
            P(None, every), P(every), P(every, None), P(every),
            P(None, every), P(every), P(None, every), P(every),
        ),
        check_vma=False,
    )
```

```python
import functools
import jax, jax.numpy as jnp
from jax import lax
from jax.sharding import Mesh, PartitionSpec as P
from jax.experimental import pallas as pl
from jax.experimental.pallas import tpu as pltpu

LANES = 128
F32 = jnp.float32
BF16 = jnp.bfloat16


class Order:
    last = ()

    @classmethod
    def passed(cls, outputs):
        cls.last = (outputs[0] if isinstance(outputs, (list, tuple)) else outputs,)
        return outputs


def ordered_call(kernel, in_specs, deps=(), micros=1, vmem=60, prefetch=None, **kw):
    deps = tuple(deps) + Order.last
    front = 0 if prefetch is None else 1
    skip, first = len(deps), front + len(in_specs)

    def body(*refs):
        return kernel(*refs[front:first], *refs[first + skip :])

    in_specs = list(in_specs) + [pl.BlockSpec(memory_space=pl.ANY)] * skip
    if prefetch is None:
        kw["in_specs"] = in_specs
    else:
        inner = {name: kw.pop(name) for name in ("grid", "out_specs")}
        kw["grid_spec"] = pltpu.PrefetchScalarGridSpec(num_scalar_prefetch=1, in_specs=in_specs, **inner)
    call = pl.pallas_call(
        body,
        compiler_params=pltpu.CompilerParams(vmem_limit_bytes=vmem << 20),
        cost_estimate=cost(micros),
        **kw,
    )
    given = () if prefetch is None else (prefetch,)
    return lambda *args: Order.passed(call(*given, *args, *deps))


def my_core():
    return lax.axis_index("core")


def my_strip():
    return 2 * lax.axis_index("x") + lax.axis_index("core")


def dot_nn(left, right):
    return jnp.dot(left, right, preferred_element_type=F32)


def dot_nt(left, right):
    return lax.dot_general(left, right, (((1,), (1,)), ((), ())), preferred_element_type=F32)


def cost(micros):
    return pl.CostEstimate(flops=int(micros * 5e6), bytes_accessed=int(micros * 5e3), transcendentals=0)


KINDS = ((2, 0, 1), (0, 1, 3))


def prep_kernel(half, ids, sides, seams, mask, order, back):
    mid, group = half // 2, half * half
    same = lambda p, q: (ids[0, p] == ids[0, q]).astype(F32)
    shape = (group, LANES)
    spot = lax.broadcasted_iota(jnp.int32, shape, 0)
    place, line = spot % half, spot // half
    top = line < mid
    col = jnp.where(top, same(0, 1), same(2, 3))
    sides[0] = jnp.where(place == 0, 0.0, jnp.where(place == mid, col, 1.0))
    sides[1] = jnp.where(place == half - 1, 0.0, jnp.where(place == mid - 1, col, 1.0))
    place = lax.broadcasted_iota(jnp.int32, (half, LANES), 0)
    rows = jnp.where(place < mid, same(0, 2), same(1, 3))
    down, up = same(0, 3), same(1, 2)
    seams[0] = rows
    seams[1] = jnp.where(place == 0, 0.0, jnp.where(place == mid, down, rows))
    seams[2] = jnp.where(place == half - 1, 0.0, jnp.where(place == mid - 1, up, rows))
    seams[3] = jnp.where(place == 0, 0.0, jnp.where(place == mid, up, rows))
    seams[4] = jnp.where(place == half - 1, 0.0, jnp.where(place == mid - 1, down, rows))

    def named(axis):
        spot = lax.broadcasted_iota(jnp.int32, (group, group), axis)
        upper, left = spot // half < mid, spot % half < mid
        return jnp.where(
            upper, jnp.where(left, ids[0, 0], ids[0, 1]), jnp.where(left, ids[0, 2], ids[0, 3])
        )

    mask[...] = jnp.where(named(0) == named(1), 0.0, -1e30)

    def source(axis):
        n = order.shape[0]
        m = lax.broadcasted_iota(jnp.int32, (n, n), axis)
        each = n // 4
        a, e = m // (2 * each), (m // each) % 2
        i, j = (m % each) // half, m % half
        return (2 * i + a) * 2 * half + 2 * j + e, lax.broadcasted_iota(jnp.int32, (n, n), 1 - axis)

    wanted, here = source(0)
    order[...] = jnp.where(wanted == here, 1.0, 0.0).astype(BF16)
    wanted, here = source(1)
    back[...] = jnp.where(wanted == here, 1.0, 0.0).astype(BF16)


def prep(ids, half, strip_rows):
    group = half * half
    sds = jax.ShapeDtypeStruct
    shapes = [sds((2, group, LANES), F32), sds((5, half, LANES), F32), sds((group, group), F32),
              sds((strip_rows, strip_rows), BF16), sds((strip_rows, strip_rows), BF16)]
    return ordered_call(
        functools.partial(prep_kernel, half),
        [pl.BlockSpec(memory_space=pltpu.SMEM)],
        out_specs=[pl.BlockSpec(v.shape) for v in shapes],
        out_shape=shapes,
        micros=3,
        name="prep",
    )(ids)


def clear_rims(store, half, width):
    zero = jnp.zeros((half, width), F32)
    for a in range(2):
        for kind in range(4):
            store[a, kind, 0:half, :] = zero
            store[a, kind, (half + 2) * half : (half + 3) * half, :] = zero


def fill_seam(store, seams, half, lanes):
    mid = half // 2
    seam_at = pl.ds((mid + 1) * half, half)
    for a, source, left_id, right_id in ((1, mid, 1, 2), (0, mid + 2, 3, 4)):
        rows = pl.ds(source * half, half)
        even = store[a, 0, rows, lanes]
        odd = store[a, 1, rows, lanes]
        store[a, 0, seam_at, lanes] = even * seams[0]
        store[a, 1, seam_at, lanes] = odd * seams[0]
        store[a, 2, seam_at, lanes] = pltpu.roll(odd, 1, 0) * seams[left_id]
        store[a, 3, seam_at, lanes] = pltpu.roll(even, half - 1, 0) * seams[right_id]


def put_row(store, a, e, place, lanes, value, sides, rows, half):
    store[a, e, place, lanes] = value
    if e == 1:
        store[a, 2, place, lanes] = pltpu.roll(value, 1, 0) * sides[0, rows, :]
    else:
        store[a, 3, place, lanes] = pltpu.roll(value, half - 1, 0) * sides[1, rows, :]


def row_sources(store, at, half, lanes):
    spots = ((1, -1), (0, 0), (1, 0), (0, 1))
    return [
        [store[a, kind, pl.ds(pl.multiple_of((at + off) * half, half), half), lanes] for kind in range(4)]
        for a, off in spots
    ]


def tap_source(sources, a, e, tap):
    return sources[a + tap // 3][KINDS[e][tap % 3]]


def store_row(step, half):
    return step + 1 + (step >= half // 2).astype(jnp.int32)


def gelu_pair(u):
    size = jnp.abs(u)
    decay = jnp.exp2((u * u) * -0.7213475204444817)
    base = 1.0 + 0.23164190 * size
    guess = pl.reciprocal(base, approx=True)
    t = guess * (2.0 - base * guess)
    poly = t * (0.127414796 + t * (-0.142248368 + t * (0.710706870 + t * (-0.726576013 + t * 0.530702714))))
    tail = poly * decay
    share = jnp.where(u >= 0.0, 1.0 - tail, tail)
    return u * share, share + u * (decay * 0.3989422804014327)


def ff_kernel(half, nb, nbt, db, dbt, w1_next, w1_last, w2, w2_next, b1, b1_next, wd, bd, sides, seams,
              gk1, gs1, gk2, gs2, small, branch_out, dnb_out, S, D, dact, act, dh, branch, dnb):
    step_at, steps = pl.program_id(0), pl.num_programs(0) - 1
    width = w2.shape[0]
    group, mid = half * half, half // 2
    blocks = [pl.ds(lb * LANES, LANES) for lb in range(width // LANES)]
    half_rows = nbt.shape[0] // 2
    now = step_at % 2
    later = 1 - now

    def put_hidden(store, a, w1, bias, which=(0, 1)):
        for e in which:
            rows = pl.ds(pl.multiple_of((2 * a + e) * group, group), group)
            h = dot_nn(nb[rows, :], w1[...]) + bias[...]
            h = h.astype(BF16).astype(F32)
            shifted = pltpu.roll(h, 1 if e == 1 else group - 1, 0)
            for part in range(2):
                cut = slice(part * group // 2, (part + 1) * group // 2)
                place = pl.ds(half + part * (group // 2 + half), group // 2)
                store[a, e, place, :] = h[cut]
                for lb, lanes in enumerate(blocks):
                    moved = shifted[cut, lb * LANES : (lb + 1) * LANES] * sides[1 - e, cut, :]
                    store[a, 3 - e, place, lanes] = moved

    def put_dact(a, weights, which=(0, 1)):
        for e in which:
            rows = pl.ds(pl.multiple_of((2 * a + e) * group, group), group)
            dact[rows, :] = dot_nt(db[rows, :], weights[...])

    tile = 256

    def add_rows(total, left, weights, n, transposed):
        cols = pl.ds(n * tile, tile)
        if transposed:
            total[:, cols] += dot_nt(left[...], weights[cols, :])
        else:
            total[:, cols] += dot_nn(left[...], weights[:, cols])

    def add_gradient(acc, left, right, k):
        cols = pl.ds(k * tile, tile)
        acc[...] += dot_nn(left[:, cols], right[cols, :])

    def set_gradient(left, right, keep, send):
        keep[...] = dot_nn(left[0:half_rows, :], right[...]).astype(BF16)
        send[...] = dot_nn(left[half_rows:, :], right[...]).astype(BF16)

    def post_back():
        units = [functools.partial(add_rows, dnb, dh, w1_last, n, True) for n in range(nbt.shape[0] // tile)]
        return units + [functools.partial(set_gradient, nbt, dh, gk1, gs1)]

    def woven(lines, units):
        done = 0
        for at, line in enumerate(lines):
            line()
            while done < len(units) and (done + 1) * len(lines) <= (at + 1) * len(units):
                units[done]()
                done += 1

    @pl.when(step_at == 0)
    def _():
        for parity in range(2):
            clear_rims(S.at[parity], half, width)
        clear_rims(D, half, width)
        branch[...] = jnp.zeros_like(branch)
        dnb[...] = jnp.zeros_like(dnb)
        dh[...] = jnp.zeros_like(dh)
        for a in range(2):
            put_hidden(S.at[0], a, w1_last, b1)
            put_dact(a, w2)
        for lanes in blocks:
            fill_seam(S.at[0], seams, half, lanes)

    @pl.when(step_at < steps)
    def _():
        here, there = S.at[now], S.at[later]
        wide_taps = wd[...].astype(F32)
        lane_taps = lambda lb: [wide_taps[t : t + 1, lb * LANES : (lb + 1) * LANES] for t in range(9)]

        def forward():
            def line_of(lb, a_now, line):
                lanes = blocks[lb]
                taps, bias = lane_taps(lb), bd[:, lanes]
                step = a_now * mid + line
                at = step + 1 + a_now
                rows = pl.ds(pl.multiple_of(step * half, half), half)
                place = pl.ds(pl.multiple_of(at * half, half), half)
                sources = row_sources(here, at, half, lanes)
                for a in range(2):
                    for e in range(2):
                        pre = bias + taps[0] * tap_source(sources, a, e, 0)
                        for t in range(1, 9):
                            pre = pre + taps[t] * tap_source(sources, a, e, t)
                        value, slope = gelu_pair(pre)
                        token = pl.ds(pl.multiple_of((2 * a + e) * group + step * half, half), half)
                        act[token, lanes] = value.astype(BF16)
                        d_pre = (dact[token, lanes] * slope).astype(BF16).astype(F32)
                        put_row(D, a, e, place, lanes, d_pre, sides, rows, half)

            units = [functools.partial(put_hidden, there, a, w1_next, b1_next) for a in range(2)] + post_back()
            woven([functools.partial(line_of, lb, a, line) for lb in range(len(blocks)) for a in range(2)
                   for line in range(mid)], units)

        forward()
        for lanes in blocks:
            fill_seam(D, seams, half, lanes)
            fill_seam(there, seams, half, lanes)

        def backward(sums):
            sums = [list(v) for v in sums]
            fold = lambda v: v.reshape(-1, 8, LANES).sum(0)

            def line_of(lb, a_now, line):
                lanes = blocks[lb]
                taps, total_of = lane_taps(lb), sums[lb]
                step = a_now * mid + line
                at = step + 1 + a_now
                place = pl.ds(pl.multiple_of(at * half, half), half)
                sources = row_sources(D, at, half, lanes)
                for a in range(2):
                    for e in range(2):
                        hid = here[a, e, place, lanes]
                        total = None
                        for t in range(9):
                            x = tap_source(sources, a, e, t)
                            term = taps[8 - t] * x
                            total = term if total is None else total + term
                            total_of[8 - t] = total_of[8 - t] + fold(hid * x)
                        d_hid = total.astype(BF16)
                        token = pl.ds(pl.multiple_of((2 * a + e) * group + step * half, half), half)
                        dh[token, lanes] = d_hid
                        total_of[9] = total_of[9] + fold(sources[a + 1][e])
                        total_of[10] = total_of[10] + fold(d_hid.astype(F32))

            units = [functools.partial(add_rows, branch, act, w2, n, False) for n in range(nbt.shape[0] // tile)]
            units += [functools.partial(set_gradient, dbt, act, gk2, gs2)]
            units += [functools.partial(put_dact, a, w2_next) for a in range(2)]
            woven([functools.partial(line_of, lb, a, line) for lb in range(len(blocks)) for a in range(2)
                   for line in range(mid)], units)
            return tuple(tuple(v) for v in sums)

        zero = jnp.zeros((8, LANES), F32)
        sums = backward(tuple((zero,) * 11 for _ in blocks))
        for lanes, total_of in zip(blocks, sums):
            for at, total in enumerate(total_of):
                small[at : at + 1, lanes] = jnp.sum(total, 0, keepdims=True)

    @pl.when(step_at == steps)
    def _():
        for unit in post_back():
            unit()
        branch_out[...] = branch[...].astype(BF16)
        dnb_out[...] = dnb[...].astype(BF16)


def feed_forward(nb, nbt, db, dbt, w1, wd, w2, biases, sides, seams, half, chunk, deps=()):
    tokens, model = nb.shape
    hidden = w1.shape[1]
    padded = (half + 3) * half
    steps = hidden // chunk
    last = lambda i: jnp.maximum(i - 1, 0)
    this = lambda i: jnp.minimum(i, steps - 1)
    ahead = lambda i: jnp.minimum(i + 1, steps - 1)
    column = lambda rows, when, at=0: pl.BlockSpec((rows, chunk), lambda i: (0, at + when(i)))
    flat = lambda when: pl.BlockSpec((chunk, model), lambda i: (when(i), 0))
    sds = jax.ShapeDtypeStruct
    return ordered_call(
        functools.partial(ff_kernel, half),
        [
            whole((tokens, model)), whole((model, tokens)), whole((tokens, model)), whole((model, tokens)),
            column(model, ahead), column(model, last), flat(this), flat(ahead),
            column(1, this), column(1, ahead), column(9, this), column(1, this, steps),
            whole(sides.shape), whole(seams.shape),
        ],
        deps,
        grid=(steps + 1,),
        out_specs=[column(model // 2, last)] * 2 + [column(model // 2, this)] * 2
        + [column(16, this), whole((tokens, model)), whole((tokens, model))],
        out_shape=[sds((model // 2, hidden), BF16)] * 4
        + [sds((16, hidden), F32), sds((tokens, model), BF16), sds((tokens, model), BF16)],
        scratch_shapes=[
            pltpu.VMEM((2, 2, 4, padded, chunk), F32),
            pltpu.VMEM((2, 4, padded, chunk), F32),
            pltpu.VMEM((tokens, chunk), F32),
            pltpu.VMEM((tokens, chunk), BF16),
            pltpu.VMEM((tokens, chunk), BF16),
            pltpu.VMEM((tokens, model), F32),
            pltpu.VMEM((tokens, model), F32),
        ],
        micros=70,
        name="feed_forward",
    )(nb, nbt, db, dbt, w1, w1, w2, w2, biases, biases, wd, biases, sides, seams)


HEADS = 12
STRIP = 128
HEAD_DIM = 64
norm_eps = 1e-06


def dot_tn(left, right):
    return lax.dot_general(left, right, (((0,), (0,)), ((), ())), preferred_element_type=F32)


def whole(shape):
    return pl.BlockSpec(shape, lambda *_: (0,) * len(shape))


def mod_rows(mod):
    width = mod.shape[1] // 6
    return [mod[pl.ds(my_strip(), 1), part * width : (part + 1) * width] for part in range(6)]


def standardize(values):
    centred = values - jnp.mean(values, -1, keepdims=True)
    inv_std = lax.rsqrt(jnp.mean(centred * centred, -1, keepdims=True) + norm_eps)
    return centred * inv_std, inv_std


def norm_reverse(grad_hat, normed_hat, inv_std):
    mean_grad = jnp.mean(grad_hat, -1, keepdims=True)
    mean_cross = jnp.mean(grad_hat * normed_hat, -1, keepdims=True)
    return inv_std * (grad_hat - mean_grad - normed_hat * mean_cross)


def take_strip(strip, pieces, order, store, group, each, part):
    for k, piece in enumerate(pieces):
        source = jnp.bitwise_xor(strip, k)
        moved = dot_nn(order, piece)
        for g in range(4):
            at = pl.multiple_of(g * group + source * each, each)
            store[pl.ds(at, each), :] = moved[g * each : (g + 1) * each].astype(store.dtype)


def first_kernel(half, own, r1, r2, r3, order, mod, wd, bd, sides, seams,
                 xg, na, cat, S, conv):
    group = half * half
    each = own.shape[1] // 4
    strip = my_strip()
    parts_of = mod_rows(mod)
    take_strip(strip, (own[strip], r1[...], r2[...], r3[...]), order[...], xg, group, each, 0)
    width = xg.shape[1]
    clear_rims(S, half, width)
    mid_rows = group // 2
    for g in range(4):
        a, e = g // 2, g % 2
        rows = pl.ds(g * group, group)
        hat, _ = standardize(xg[rows, :].astype(F32))
        low = (hat * (1.0 + parts_of[1]) + parts_of[0]).astype(BF16)
        na[rows, :] = low
        h = low.astype(F32)
        for part in range(2):
            S[a, e, pl.ds(half + part * (mid_rows + half), mid_rows), :] = h[part * mid_rows : (part + 1) * mid_rows]
        shifted = pltpu.roll(h, 1 if e == 1 else group - 1, 0)
        for lb in range(width // LANES):
            lanes = pl.ds(lb * LANES, LANES)
            moved = shifted[:, lb * LANES : (lb + 1) * LANES] * sides[0 if e == 1 else 1]
            for part in range(2):
                S[a, 2 if e == 1 else 3, pl.ds(half + part * (mid_rows + half), mid_rows), lanes] = (
                    moved[part * mid_rows : (part + 1) * mid_rows]
                )

    def block(lb, carry):
        lanes = pl.ds(pl.multiple_of(lb * LANES, LANES), LANES)
        fill_seam(S, seams, half, lanes)
        wide_taps = wd[:, lanes].astype(F32)
        taps = [wide_taps[t : t + 1] for t in range(9)]
        bias = bd[:, lanes]

        def forward(step, inner):
            at = store_row(step, half)
            sources = row_sources(S, at, half, lanes)
            for a in range(2):
                for e in range(2):
                    pre = bias + taps[0] * tap_source(sources, a, e, 0)
                    for t in range(1, 9):
                        pre = pre + taps[t] * tap_source(sources, a, e, t)
                    token = pl.ds(pl.multiple_of((2 * a + e) * group + step * half, half), half)
                    conv[token, lanes] = pre.astype(BF16)
            return inner

        return lax.fori_loop(0, half, forward, carry)

    lax.fori_loop(0, width // LANES, block, 0)
    for g in range(4):
        rows = pl.ds(g * group, group)
        cat[:, rows] = conv[rows, :].T


def first_norm(own, r1, r2, r3, order, mod, wd, biases, sides, seams, half, at, deps=()):
    tokens, model = 4 * half * half, own.shape[2]
    sds = jax.ShapeDtypeStruct
    return ordered_call(
        functools.partial(first_kernel, half),
        [
            whole(own.shape), whole(r1.shape), whole(r2.shape), whole(r3.shape), whole(order.shape),
            whole(mod.shape), whole(wd.shape), pl.BlockSpec((1, model), lambda i: (0, at)),
            whole(sides.shape), whole(seams.shape),
        ],
        deps,
        grid=(1,),
        out_specs=[whole((tokens, model)), whole((tokens, model)), whole((model, tokens))],
        scratch_shapes=[
            pltpu.VMEM((2, 4, (half + 3) * half, model), F32),
            pltpu.VMEM((tokens, model), BF16),
        ],
        out_shape=[sds((tokens, model), BF16), sds((tokens, model), BF16), sds((model, tokens), BF16)],
        micros=10,
        name="first_norm",
    )(own, r1, r2, r3, order, mod, wd, biases, sides, seams)


def attend_kernel(half, cat, wt, bias, mask, wout, bout, mod, xg, perm,
                  qkvt, lse, ot, proj, mid, nb, nbt, scores, probs):
    group = half * half
    model = cat.shape[0]
    parts_of = mod_rows(mod)
    pick_row = (lax.broadcasted_iota(jnp.int32, (8, group), 0) == 0).astype(BF16)
    for part in range(3):
        rows = pl.ds(part * model, model)
        product = dot_nn(wt[rows, :], cat[...])
        if part != 1:
            own = bias[:, (part // 2) * model : (part // 2 + 1) * model].astype(BF16)
            product = product + dot_tn(jnp.broadcast_to(own, (8, model)), pick_row)
        qkvt[rows, :] = product.astype(BF16)
    rows_of = lambda part, h: slice(part * model + h * HEAD_DIM, part * model + (h + 1) * HEAD_DIM)
    for h in range(HEADS):
        q = qkvt[rows_of(0, h), :] * HEAD_DIM ** (-0.5)
        scores[h] = dot_tn(qkvt[rows_of(1, h), :], q)
    for h in range(HEADS):
        s = scores[h] + mask[...]
        top = jnp.max(s, 0, keepdims=True)
        p = jnp.exp(s - top)
        total = jnp.sum(p, 0, keepdims=True)
        probs[h] = (p * (1.0 / total)).astype(BF16)
        lse[0, h : h + 1, :] = top + jnp.log(total)
    for h in range(HEADS):
        ot[rows_of(0, h), :] = dot_nn(qkvt[rows_of(2, h), :], probs[h]).astype(BF16)
    projection = dot_tn(ot[...], wout[...]) + bout[...]
    proj[...] = projection.astype(BF16)
    middle = xg[...].astype(F32) + parts_of[2] * projection
    mid[...] = middle
    hat, _ = standardize(middle)
    low = (hat * (1.0 + parts_of[4]) + parts_of[3]).astype(BF16)
    nb[...] = low
    nbt[...] = dot_nt(perm[...], low).astype(BF16)


def attend(cat, wt, biases, mask, wout, mod, xg, perm, half, at_qv, at_out, deps=()):
    model, tokens = cat.shape
    group = half * half
    sds = jax.ShapeDtypeStruct
    tall = lambda rows: pl.BlockSpec((rows, group), lambda i: (0, i))
    flat = pl.BlockSpec((group, model), lambda i: (i, 0))
    return ordered_call(
        functools.partial(attend_kernel, half),
        [
            tall(model), whole(wt.shape), pl.BlockSpec((1, 2 * model), lambda i: (0, at_qv)),
            whole(mask.shape), whole(wout.shape), pl.BlockSpec((1, model), lambda i: (0, at_out)),
            whole(mod.shape), flat, whole(perm.shape),
        ],
        deps,
        grid=(4,),
        out_specs=[tall(3 * model), pl.BlockSpec((1, 16, group), lambda i: (i, 0, 0)), tall(model),
                   flat, flat, flat, tall(model)],
        out_shape=[sds((3 * model, tokens), BF16), sds((4, 16, group), F32), sds((model, tokens), BF16),
                   sds((tokens, model), BF16), sds((tokens, model), F32), sds((tokens, model), BF16),
                   sds((model, tokens), BF16)],
        scratch_shapes=[pltpu.VMEM((HEADS, group, group), F32), pltpu.VMEM((HEADS, group, group), BF16)],
        micros=26,
        name="attend",
    )(cat, wt, biases, mask, wout, biases, mod, xg, perm)


def gate_kernel(half, own, r1, r2, r3, order, mod, perm, gg, db, dbt, small):
    group = half * half
    each = own.shape[1] // 4
    parts_of = mod_rows(mod)
    strip = my_strip()
    take_strip(strip, (own[strip], r1[...], r2[...], r3[...]), order[...], gg, group, each, 0)
    total = jnp.zeros((1, gg.shape[1]), F32)
    for g in range(4):
        rows = pl.ds(g * group, group)
        low = (parts_of[5] * gg[rows, :].astype(F32)).astype(BF16)
        db[rows, :] = low
        total = total + jnp.sum(low.astype(F32), 0, keepdims=True)
        dbt[:, rows] = dot_nt(perm[...], low).astype(BF16)
    small[...] = total


def gate(own, r1, r2, r3, order, mod, perm, half, deps=()):
    tokens, model = 4 * half * half, own.shape[2]
    sds = jax.ShapeDtypeStruct
    args = (own, r1, r2, r3, order, mod, perm)
    return ordered_call(
        functools.partial(gate_kernel, half),
        [whole(v.shape) for v in args],
        deps,
        grid=(1,),
        out_specs=[whole((tokens, model)), whole((tokens, model)), whole((model, tokens)), whole((1, model))],
        out_shape=[sds((tokens, model), BF16), sds((tokens, model), BF16), sds((model, tokens), BF16), sds((1, model), F32)],
        micros=5,
        name="gate",
    )(*args)


def give_strip(strip, store, order_back, outs, group, each):
    for k, out in enumerate(outs):
        target = jnp.bitwise_xor(strip, k)
        rows = [store[pl.ds(pl.multiple_of(g * group + target * each, each), each), :] for g in range(4)]
        out[...] = dot_nn(order_back, jnp.concatenate(rows, 0)).astype(out.dtype)


def middle_kernel(half, branch, dnb, mid, proj, gg, wout, bfc2, mod, back, perm,
                  o0, o1, o2, o3, dmid, dot_, dpt, small, res):
    step = pl.program_id(0)
    group = half * half
    parts_of = mod_rows(mod)

    @pl.when(step == 0)
    def _():
        small[...] = jnp.zeros_like(small)

    full = branch[...].astype(F32) + bfc2[...]
    middle = mid[...]
    g = gg[...].astype(F32)
    res[pl.ds(pl.multiple_of(step * group, group), group), :] = (middle + parts_of[5] * full).astype(BF16)
    hat, inv = standardize(middle)
    d = dnb[...].astype(F32)
    d_mid = g + norm_reverse(d * (1.0 + parts_of[4]), hat, inv)
    dmid[...] = d_mid.astype(BF16)
    low = (parts_of[2] * d_mid).astype(BF16)
    rows = (
        d_mid * proj[...].astype(F32), d, d * hat, g * full, low.astype(F32),
    )
    for at, value in enumerate(rows):
        small[at : at + 1, :] += jnp.sum(value, 0, keepdims=True)
    dot_[...] = dot_nt(wout[...], low).astype(BF16)
    dpt[...] = dot_nt(perm[...], low).astype(BF16)

    @pl.when(step == pl.num_programs(0) - 1)
    def _():
        give_strip(my_strip(), res, back[...], (o0, o1, o2, o3), group, back.shape[0] // 4)


def middle(branch, dnb, mid, proj, gg, wout, biases, mod, back, perm, half, at, deps=()):
    tokens, model = mid.shape
    group = half * half
    sds = jax.ShapeDtypeStruct
    tall = pl.BlockSpec((model, group), lambda i: (0, i))
    flat = pl.BlockSpec((group, model), lambda i: (i, 0))
    strip = back.shape[0]
    return ordered_call(
        functools.partial(middle_kernel, half),
        [flat, flat, flat, flat, flat, whole(wout.shape), pl.BlockSpec((1, model), lambda i: (0, at)),
         whole(mod.shape), whole(back.shape), whole(perm.shape)],
        deps,
        grid=(4,),
        out_specs=[whole((strip, model))] * 4 + [flat, tall, tall, whole((8, model))],
        out_shape=[sds((strip, model), BF16)] * 4 + [sds((tokens, model), BF16), sds((model, tokens), BF16),
                   sds((model, tokens), BF16), sds((8, model), F32)],
        scratch_shapes=[pltpu.VMEM((tokens, model), BF16)],
        micros=12,
        name="middle",
    )(branch, dnb, mid, proj, gg, wout, biases, mod, back, perm)


def attend_back_kernel(half, span, q, k, v, do, ot, lse, mask, cat, dpt, perm, wq, wk, wv,
                       gk1, gk2, gs1, gs2, dct, small, catp, acc, grads, scores, changes, low_ds, low_p):
    group = half * half
    step = pl.program_id(0)
    model = cat.shape[0]

    @pl.when(step == 0)
    def _():
        catp[...] = dot_nn(perm[...], cat[...]).astype(BF16)
        acc[...] = jnp.zeros_like(acc)

    scale = HEAD_DIM ** (-0.5)
    heads = span // HEAD_DIM
    pairs = [(h, g) for h in range(heads) for g in range(4)]
    spot = lambda h, g: (slice(h * HEAD_DIM, (h + 1) * HEAD_DIM), slice(g * group, (g + 1) * group))
    for n, (h, g) in enumerate(pairs):
        at = spot(h, g)
        scores[n] = dot_tn(k[at], q[at] * scale)
        changes[n] = dot_tn(v[at], do[at])
    for n, (h, g) in enumerate(pairs):
        p = jnp.exp(scores[n] + mask[...] - lse[g, pl.ds(step * heads + h, 1), :])
        dp = changes[n]
        delta = jnp.sum(p * dp, 0, keepdims=True)
        low_ds[n] = (p * (dp - delta)).astype(BF16)
        low_p[n] = p.astype(BF16)
    for n, (h, g) in enumerate(pairs):
        rows, cols = spot(h, g)
        part_rows = lambda part: slice(part * span + h * HEAD_DIM, part * span + (h + 1) * HEAD_DIM)
        grads[part_rows(0), cols] = (dot_nn(k[rows, cols], low_ds[n]) * scale).astype(BF16)
        grads[part_rows(1), cols] = (dot_nt(q[rows, cols], low_ds[n]) * scale).astype(BF16)
        grads[part_rows(2), cols] = dot_nt(do[rows, cols], low_p[n]).astype(BF16)
    ones = jnp.ones((8, grads.shape[1]), BF16)
    outs = ((gk1, gs1, 0), (gk1, gs1, 1), (gk2, gs2, 0))
    for part in range(3):
        mine = grads[part * span : (part + 1) * span, :]
        if part != 1:
            small[part // 2 : part // 2 + 1, :] = dot_nt(ones, mine)[0:1]
        product = dot_nt(catp[...], mine).astype(BF16)
        keep, send, at = outs[part]
        keep[at] = product[: model // 2]
        send[at] = product[model // 2 :]
    weights = jnp.concatenate([wq[...], wk[...], wv[...]], 1)
    acc[...] += dot_nn(weights, grads[...])
    product = dot_nt(dpt[...], ot[...]).astype(BF16)
    gk2[1] = product[: model // 2]
    gs2[1] = product[model // 2 :]

    @pl.when(step == pl.num_programs(0) - 1)
    def _():
        dct[...] = acc[...].astype(BF16)


def attend_back(qkvt, dot_, ot, lse, mask, cat, dpt, perm, w, half, span, deps=()):
    model, tokens = cat.shape
    group = half * half
    steps = model // span
    sds = jax.ShapeDtypeStruct
    part = lambda n: pl.BlockSpec((span, tokens), lambda i: (n * steps + i, 0))
    return ordered_call(
        functools.partial(attend_back_kernel, half, span),
        [
            part(0), part(1), part(2), part(0), part(0), whole(lse.shape), whole(mask.shape), whole(cat.shape),
            whole(dpt.shape), whole(perm.shape),
            *[pl.BlockSpec((model, span), lambda i, n=n: (0, n * steps + i)) for n in range(3)],
        ],
        deps,
        grid=(steps,),
        out_specs=[pl.BlockSpec((2, model // 2, span), lambda i: (0, 0, i))] * 4
        + [whole((model, tokens)), pl.BlockSpec((2, span), lambda i: (0, i))],
        out_shape=[sds((2, model // 2, model), BF16)] * 4 + [sds((model, tokens), BF16), sds((2, model), F32)],
        scratch_shapes=[pltpu.VMEM((model, tokens), BF16), pltpu.VMEM((model, tokens), F32),
                        pltpu.VMEM((3 * span, tokens), BF16),
                        *[pltpu.VMEM((4 * span // HEAD_DIM, group, group), kind) for kind in (F32, F32, BF16, BF16)]],
        micros=30,
        name="attend_back",
    )(qkvt, qkvt, qkvt, dot_, ot, lse, mask, cat, dpt, perm, w, w, w)


def conv_back_kernel(half, dct, na, xg, wd, sides, seams, dna, small, D):
    group = half * half
    width = xg.shape[1]
    clear_rims(D, half, width)
    mid_rows = group // 2
    for g in range(4):
        a, e = g // 2, g % 2
        rows = pl.ds(g * group, group)
        h = dct[:, rows].T.astype(F32)
        for part in range(2):
            D[a, e, pl.ds(half + part * (mid_rows + half), mid_rows), :] = h[part * mid_rows : (part + 1) * mid_rows]
        shifted = pltpu.roll(h, 1 if e == 1 else group - 1, 0)
        for lb in range(width // LANES):
            lanes = pl.ds(lb * LANES, LANES)
            moved = shifted[:, lb * LANES : (lb + 1) * LANES] * sides[0 if e == 1 else 1]
            for part in range(2):
                D[a, 2 if e == 1 else 3, pl.ds(half + part * (mid_rows + half), mid_rows), lanes] = (
                    moved[part * mid_rows : (part + 1) * mid_rows]
                )

    def block(lb, carry):
        lanes = pl.ds(pl.multiple_of(lb * LANES, LANES), LANES)
        fill_seam(D, seams, half, lanes)
        wide_taps = wd[:, lanes].astype(F32)
        taps = [wide_taps[t : t + 1] for t in range(9)]

        def backward(step, sums):
            sums = list(sums)
            at = store_row(step, half)
            sources = row_sources(D, at, half, lanes)
            fold = lambda v: v.reshape(-1, 8, LANES).sum(0)
            for a in range(2):
                for e in range(2):
                    token = pl.ds(pl.multiple_of((2 * a + e) * group + step * half, half), half)
                    hid = na[token, lanes].astype(F32)
                    total = None
                    for t in range(9):
                        x = tap_source(sources, a, e, t)
                        term = taps[8 - t] * x
                        total = term if total is None else total + term
                        sums[8 - t] = sums[8 - t] + fold(hid * x)
                    dna[token, lanes] = total.astype(BF16)
                    sums[9] = sums[9] + fold(sources[a + 1][e])
                    sums[10] = sums[10] + fold(total)
            return tuple(sums)

        sums = lax.fori_loop(0, half, backward, tuple(jnp.zeros((8, LANES), F32) for _ in range(11)))
        for at, total in enumerate(sums):
            small[at : at + 1, lanes] = jnp.sum(total, 0, keepdims=True)
        return carry

    lax.fori_loop(0, width // LANES, block, 0)
    scale_sum = jnp.zeros((1, width), F32)
    for g in range(4):
        rows = pl.ds(g * group, group)
        hat, _ = standardize(xg[rows, :].astype(F32))
        scale_sum = scale_sum + jnp.sum(dna[rows, :].astype(F32) * hat, 0, keepdims=True)
    small[11:12, :] = scale_sum


def conv_back(dct, na, xg, wd, sides, seams, half, deps=()):
    tokens, model = xg.shape
    sds = jax.ShapeDtypeStruct
    args = (dct, na, xg, wd, sides, seams)
    return ordered_call(
        functools.partial(conv_back_kernel, half),
        [whole(v.shape) for v in args],
        deps,
        grid=(1,),
        out_specs=[whole((tokens, model)), whole((16, model))],
        out_shape=[sds((tokens, model), BF16), sds((16, model), F32)],
        scratch_shapes=[pltpu.VMEM((2, 4, (half + 3) * half, model), F32)],
        micros=11,
        name="conv_back",
    )(*args)


def last_kernel(half, dna, xg, dmid, mod, back, o0, o1, o2, o3, tig):
    group = half * half
    parts_of = mod_rows(mod)
    for g in range(4):
        rows = pl.ds(g * group, group)
        hat, inv = standardize(xg[rows, :].astype(F32))
        change = norm_reverse(dna[rows, :].astype(F32) * (1.0 + parts_of[1]), hat, inv)
        tig[rows, :] = (dmid[rows, :].astype(F32) + change).astype(BF16)
    give_strip(my_strip(), tig, back[...], (o0, o1, o2, o3), group, back.shape[0] // 4)


def last(dna, xg, dmid, mod, back, half, deps=()):
    tokens, model = xg.shape
    args = (dna, xg, dmid, mod, back)
    strip = back.shape[0]
    return ordered_call(
        functools.partial(last_kernel, half),
        [whole(v.shape) for v in args],
        deps,
        grid=(1,),
        out_specs=[whole((strip, model))] * 4,
        out_shape=[jax.ShapeDtypeStruct((strip, model), BF16)] * 4,
        scratch_shapes=[pltpu.VMEM((tokens, model), BF16)],
        micros=5,
        name="last",
    )(*args)


def cut_kernel(source, o1, o2, o3):
    strip = my_strip()
    for k, out in enumerate((o1, o2, o3)):
        out[...] = source[jnp.bitwise_xor(strip, k + 1)]


def cut_strips(values, deps=()):
    shape = jax.ShapeDtypeStruct(values.shape[1:], values.dtype)
    return ordered_call(
        cut_kernel,
        [whole(values.shape)],
        deps,
        grid=(1,),
        out_specs=[whole(shape.shape)] * 3,
        out_shape=[shape] * 3,
        micros=2,
        name="cut_strips",
    )(values)


def gather_kernel(own, c1, c2, c3, out):
    strip = my_strip()
    for k, piece in enumerate((own, c1, c2, c3)):
        out[jnp.bitwise_xor(strip, k)] = piece[...].astype(out.dtype)


def gather_strips(own, c1, c2, c3, dtype, deps=()):
    rows, model = own.shape
    return ordered_call(
        gather_kernel,
        [whole(own.shape)] * 4,
        deps,
        grid=(1,),
        out_specs=whole((4, rows, model)),
        out_shape=jax.ShapeDtypeStruct((4, rows, model), dtype),
        micros=3,
        name="gather_strips",
    )(own, c1, c2, c3)


def swap(values, axis):
    return lax.ppermute(values, axis, [(0, 1), (1, 0)])


def fold_kernel(count, *refs):
    ins, outs = refs[: 2 * count], refs[2 * count :]
    for at, out in enumerate(outs):
        total = ins[at * count][...].astype(F32)
        for term in ins[at * count + 1 : (at + 1) * count]:
            total = total + term[...].astype(F32)
        out[...] = total.astype(BF16)


def spread_kernel(count, z_count, *refs):
    ins, outs = refs[: 2 * count], refs[2 * count :]
    z = lax.axis_index("z")
    for at in range(2):
        total = ins[at * count][0].astype(F32)
        for term in ins[at * count + 1 : (at + 1) * count]:
            total = total + term[0].astype(F32)
        total = total.astype(BF16)
        rows = total.shape[0]
        shard = rows // z_count
        line = lax.broadcasted_iota(jnp.int32, (shard, rows), 0)
        place = lax.broadcasted_iota(jnp.int32, (shard, rows), 1)
        for k, out in enumerate(outs):
            wanted = (place == line + jnp.bitwise_xor(z, k) * shard).astype(F32).astype(BF16)
            out[at, 0] = dot_nn(wanted, total).astype(BF16)


def close_kernel(together, *refs):
    outs, got = refs[-len(together) :], refs[: -len(together)]
    _, mine, _, width = got[0].shape
    part = 0
    for count, out in zip(together, outs):
        for at in range(count):
            total = got[0][part // mine, part % mine].astype(F32)
            for more in got[1:]:
                total = total + more[part // mine, part % mine].astype(F32)
            out[:, at * width : (at + 1) * width] = total
            part += 1


class SumOverAll:
    def __init__(self, place, keep, send, z_count):
        keep = [v.reshape((-1,) + v.shape[-2:]) for v in keep]
        self.place, self.z_count, self.keep = place, z_count, keep
        self.mine_parts, self.rows, self.width = keep[0].shape
        self.quarter = self.rows // 4
        self.block = min(1536, self.width)
        self.other = [swap(v.reshape((-1,) + v.shape[-2:]), "core") for v in send]

    def fold(self, terms, halves, name, spread=False, deps=()):
        first = len(terms[0])
        specs, args = [], []
        for side in terms:
            for array, row in side:
                def index(p, h, n, place, row=row):
                    return p, row(h, place[0], place[1]), n

                specs.append(pl.BlockSpec((1, self.quarter, self.block), index))
                args.append(array)
        mine = self.mine_parts
        if spread:
            shard = self.quarter // self.z_count
            out_specs = [
                pl.BlockSpec((2, 1, shard, self.block), lambda p, h, n, place: (0, p, 0, n))
            ] * self.z_count
            out_shape = [jax.ShapeDtypeStruct((2, mine, shard, self.width), BF16)] * self.z_count
            kernel = functools.partial(spread_kernel, first, self.z_count)
        else:
            out_specs = [pl.BlockSpec((1, self.quarter, self.block), lambda p, h, n, place: (p, h, n))] * 2
            out_shape = [jax.ShapeDtypeStruct((mine, halves * self.quarter, self.width), BF16)] * 2
            kernel = functools.partial(fold_kernel, first)
        return ordered_call(
            kernel,
            specs,
            deps,
            grid=(mine, halves, self.width // self.block),
            out_specs=out_specs,
            out_shape=out_shape,
            prefetch=self.place,
            micros=2,
            name=name,
        )(*args)

    def second(self):
        (k1, k2), (r1, r2) = self.keep, self.other
        away_x = lambda h, x, y: 2 * (1 - x) + h
        away_y = lambda h, x, y: 2 * h + (1 - y)
        a, b = self.fold([[(k1, away_x), (r1, away_x)], [(k2, away_y), (r2, away_y)]], 2, "fold_second")
        self.got_a, self.got_b = swap(a, "x"), swap(b, "y")
        return a, b

    def third(self):
        (k1, k2), (r1, r2) = self.keep, self.other
        near = lambda h, x, y: 2 * x + (1 - y)
        far = lambda h, x, y: 2 * (1 - x) + y
        a, b = self.fold(
            [
                [(k1, near), (r1, near), (self.got_a, lambda h, x, y: 1 - y)],
                [(k2, far), (r2, far), (self.got_b, lambda h, x, y: 1 - x)],
            ],
            1, "fold_third",
        )
        self.last_a, self.last_b = swap(a, "y"), swap(b, "x")
        return a, b

    def fourth(self, deps=()):
        (k1, k2), (r1, r2) = self.keep, self.other
        own = lambda h, x, y: 2 * x + y
        zero = lambda h, x, y: 0
        self.mine = self.fold(
            [
                [(k1, own), (r1, own), (self.got_a, lambda h, x, y: y), (self.last_a, zero)],
                [(k2, own), (r2, own), (self.got_b, lambda h, x, y: x), (self.last_b, zero)],
            ],
            1, "fold_fourth", True, deps,
        )
        pairs = lambda k: [(i, i ^ k) for i in range(self.z_count)]
        self.mine = [v if k == 0 else lax.ppermute(v, "z", pairs(k)) for k, v in enumerate(self.mine)]

    def finish(self, together, deps=()):
        shard = self.mine[0].shape[2]
        shapes = [jax.ShapeDtypeStruct((shard, count * self.width), F32) for count in together]
        return ordered_call(
            functools.partial(close_kernel, together),
            [whole(v.shape) for v in self.mine],
            deps,
            grid=(1,),
            out_specs=[whole(v.shape) for v in shapes],
            out_shape=shapes,
            micros=2,
            name="close_sums",
        )(*self.mine)


MODS = 6


def pack_kernel(groups, ff, fc2, mid, qv, last, o0, o1, o2, o3, work):
    work[...] = jnp.zeros_like(work)
    model = last.shape[1]
    strip_width = model // 4
    d_mod = [last[10:11, :], last[11:12, :]] + [mid[k : k + 1, :] for k in range(4)]
    short = [last[k : k + 1, :] for k in range(10)] + [mid[4:5, :], fc2[...]]
    for t in range(4):
        work[t, 0:11, :] = ff[0:11, t * model : (t + 1) * model]
        for k, row in enumerate(d_mod):
            work[t, 11 + k : 12 + k, :] = row
        for k, row in enumerate(short):
            work[t, 17 + k : 18 + k, 0:strip_width] = row[:, t * strip_width : (t + 1) * strip_width]
        at = (2 * t * strip_width) % model
        work[t, 29:30, 0 : 2 * strip_width] = qv[t // 2 : t // 2 + 1, at : at + 2 * strip_width]
    for k, out in enumerate((o0, o1, o2, o3)):
        out[...] = work[jnp.bitwise_xor(my_strip(), k)].astype(BF16)


def pack(ff, fc2, mid, qv, last, groups, deps=()):
    args = (ff, fc2, mid, qv, last)
    model = last.shape[1]
    return ordered_call(
        functools.partial(pack_kernel, groups),
        [whole(v.shape) for v in args],
        deps,
        grid=(1,),
        out_specs=[whole((32, model))] * 4,
        out_shape=[jax.ShapeDtypeStruct((32, model), BF16)] * 4,
        scratch_shapes=[pltpu.VMEM((4, 32, model), F32)],
        micros=2,
        name="pack_small",
    )(*args)


def repack_kernel(groups, g0, g1, g2, g3, cond, out, mods, work, common):
    model = g0.shape[1]
    work[...] = jnp.zeros_like(work)
    values = [g[...].astype(F32) for g in (g0, g1, g2, g3)]
    total = values[0] + values[1] + values[2] + values[3]
    lanes = model // LANES
    head = MODS * lanes * 4
    for part in range(MODS):
        for lb in range(lanes):
            for k in range(4):
                at = (part * lanes + lb) * 4 + jnp.bitwise_xor(my_strip(), k)
                row = values[k][11 + part : 12 + part, lb * LANES : (lb + 1) * LANES]
                common[pl.ds(at, 1), :] = row
    for part in range(MODS):
        for lb in range(lanes):
            at = (part * lanes + lb) * 4
            mods[:, (part * lanes + lb) * LANES : (part * lanes + lb + 1) * LANES] = common[at : at + 4, :].astype(BF16)
    wide, thin = model // groups, model // 4 // groups
    for u in range(groups):
        work[u, 0:11, 0:wide] = total[0:11, u * wide : (u + 1) * wide]
        work[u, 17:29, 0:thin] = total[17:29, u * thin : (u + 1) * thin]
        work[u, 29:30, 0 : 2 * thin] = total[29:30, 2 * u * thin : 2 * (u + 1) * thin]
        work[u, 32:36, 0:thin] = cond[:, u * thin : (u + 1) * thin].astype(F32)
        out[u, 0:head, :] = common[...].astype(BF16)
        out[u, head:, :] = work[u].astype(BF16)


def repack(got, cond, groups, deps=()):
    model = got[0].shape[1]
    head = MODS * (model // LANES) * 4
    args = (*got, cond)
    shapes = [(groups, head + 48, LANES), (4, MODS * model)]
    return ordered_call(
        functools.partial(repack_kernel, groups),
        [whole(v.shape) for v in args],
        deps,
        grid=(1,),
        out_specs=[whole(v) for v in shapes],
        out_shape=[jax.ShapeDtypeStruct(v, BF16) for v in shapes],
        scratch_shapes=[pltpu.VMEM((groups, 48, LANES), F32), pltpu.VMEM((head, LANES), F32)],
        micros=2,
        name="repack_small",
    )(*args)


def unpack_kernel(groups, got, wada, bada, *refs):
    outs, (mods, conds) = refs[:-2], refs[-2:]
    head = got.shape[1] - 48
    total = jnp.sum(got[:, head:, :].astype(F32), 0)
    rows = ((0, 9), (9, 10), (10, 11), (17, 26), (26, 27), (27, 28), (28, 29), (29, 30))
    for (first, end), out in zip(rows, outs):
        out[...] = total[first:end, 0 : out.shape[1]]
    for u in range(groups):
        values = got[u].astype(F32)
        conds[u * 4 : (u + 1) * 4, :] = values[head + 32 : head + 36]
        for block in range(head // 4):
            mods[u * 4 : (u + 1) * 4, block * LANES : (block + 1) * LANES] = values[block * 4 : block * 4 + 4]
    shard, own = wada.shape[0], bada.shape[1]
    wada[...] = dot_tn(conds[...].astype(BF16), mods[...].astype(BF16))[0:shard]
    index = my_strip() * groups + lax.axis_index("z") * 2 + lax.axis_index("y")
    summed = jnp.broadcast_to(jnp.sum(mods[...], 0, keepdims=True), (8, mods.shape[1]))
    bada[...] = pltpu.roll(summed, mods.shape[1] - own * index, 1)[0:1, 0:own]


def unpack(got, model, groups, deps=()):
    wide, thin = model // groups, model // 4 // groups
    shapes = [(thin, MODS * model), (1, MODS * thin)]
    shapes += [(9, wide), (1, wide), (1, wide), (9, thin), (1, thin), (1, thin), (1, thin), (1, 2 * thin)]
    return ordered_call(
        functools.partial(unpack_kernel, groups),
        [whole(got.shape)],
        deps,
        grid=(1,),
        out_specs=[whole(v) for v in shapes],
        out_shape=[jax.ShapeDtypeStruct(v, F32) for v in shapes],
        scratch_shapes=[pltpu.VMEM((4 * groups, MODS * model), F32), pltpu.VMEM((4 * groups, LANES), F32)],
        micros=2,
        name="unpack_small",
    )(got)


def cond_back_kernel(mods, wada, cond, out):
    change = dot_nt(wada[...], mods[...]).T
    values = cond[...].astype(F32)
    gain = 1.0 / (1.0 + jnp.exp(-values))
    out[...] = change * gain * (1.0 + values * (1.0 - gain))


def cond_back(mods, wada, cond, deps=()):
    canvases, model = cond.shape
    tile = model // 3
    return ordered_call(
        cond_back_kernel,
        [whole(mods.shape), pl.BlockSpec((tile, wada.shape[1]), lambda i: (i, 0)),
         pl.BlockSpec((canvases, tile), lambda i: (0, i))],
        deps,
        grid=(3,),
        out_specs=pl.BlockSpec((canvases, tile), lambda i: (0, i)),
        out_shape=jax.ShapeDtypeStruct((canvases, model), F32),
        micros=3,
        name="cond_back",
    )(mods, wada, cond)


def row_order(model, z_count):
    rows = jnp.arange(model, dtype=jnp.int32).reshape(2, 2, z_count, 2, -1)
    rows = jnp.transpose(rows, (1, 0, 3, 2, 4)).reshape(2, -1)
    rows = jnp.where(lax.axis_index("core") == 0, rows, rows[::-1]).reshape(-1)
    return (rows[:, None] == jnp.arange(model, dtype=jnp.int32)[None]).astype(BF16)


def shards(
    tokens, conditioning, latent_ids, w_ada, b_ada, w_dw1, b_dw1, w_qkv, b_qv, w_out, b_out,
    w_fc1, b_fc1, w_dw2, b_dw2, w_fc2, b_fc2, out_grad,
):
    canvases, rows, cols, model = tokens.shape
    half = cols // 2
    hidden = w_fc1.shape[1]
    z_count = lax.axis_size("z")
    groups = 2 * z_count
    devices = 4 * groups
    strip = my_strip()
    strips = ("x", "core")
    span = 256
    Order.last = ()

    def exchange(pieces):
        return [lax.ppermute(piece, strips, [(i, i ^ (k + 1)) for i in range(4)]) for k, piece in enumerate(pieces)]

    token_rows = tokens.reshape(canvases, rows * cols, model)
    grad_rows = out_grad.reshape(canvases, rows * cols, model)
    token_pieces = exchange(cut_strips(token_rows))

    cond_vals = conditioning.astype(F32)
    cond_act = jax.nn.silu(cond_vals).astype(BF16)
    mod = jnp.dot(cond_act, w_ada, preferred_element_type=F32) + b_ada.astype(F32)
    cond_cols = lax.dynamic_slice_in_dim(cond_act, strip * (model // 4), model // 4, 1)
    place = jnp.stack([lax.axis_index("x"), lax.axis_index("y")]).astype(jnp.int32)
    perm = row_order(model, z_count)

    ids = lax.dynamic_slice_in_dim(latent_ids, strip, 1, 0)
    sides, seams, mask, order, back = prep(ids, half, rows * cols)
    listed = (b_fc1, b_dw2, b_qv, b_dw1, b_out, b_fc2)
    biases = jnp.concatenate(listed).astype(F32)[None]
    places = [sum(v.shape[0] for v in listed[:n]) // listed[n].shape[0] for n in range(6)]
    wt = w_qkv.T

    xg, na, cat = first_norm(
        token_rows, *token_pieces, order, mod, w_dw1, biases, sides, seams, half, places[3], (wt, cond_cols, perm, place)
    )
    grad_pieces = exchange(cut_strips(grad_rows, token_pieces))
    qkvt, lse, ot, proj, mid, nb, nbt = attend(
        cat, wt, biases, mask, w_out, mod, xg, perm, half, places[2], places[4]
    )
    gg, db, dbt, small_fc2 = gate(grad_rows, *grad_pieces, order, mod, perm, half)
    ff_k1, ff_s1, ff_k2, ff_s2, small_ff, branch, dnb = feed_forward(
        nb, nbt, db, dbt, w_fc1, w_dw2, w_fc2, biases, sides, seams, half, 256
    )
    ff = SumOverAll(place, (ff_k1, ff_k2), (ff_s1, ff_s2), z_count)
    *res, dmid, dot_, dpt, small_mid = middle(
        branch, dnb, mid, proj, gg, w_out, biases, mod, back, perm, half, places[5]
    )
    res = [res[0]] + exchange(res[1:])
    ff.second()
    at_k1, at_k2, at_s1, at_s2, dct, small_qv = attend_back(
        qkvt, dot_, ot, lse, mask, cat, dpt, perm, w_qkv, half, span
    )
    at = SumOverAll(place, (at_k1, at_k2), (at_s1, at_s2), z_count)
    ff.third()
    at.second()
    dna, small_last = conv_back(dct, na, xg, w_dw1, sides, seams, half)
    ff.fourth()
    tig = last(dna, xg, dmid, mod, back, half)
    tig = [tig[0]] + exchange(tig[1:])
    message = pack(small_ff, small_fc2, small_mid, small_qv, small_last, groups)
    got = [message[0]] + exchange(message[1:])
    at.third()
    token_grad = gather_strips(*tig, F32).reshape(tokens.shape)
    g_w_fc1, g_w_fc2 = ff.finish((1, 1))
    at.fourth()
    message, d_mod = repack(got, cond_cols, groups)
    got = lax.all_to_all(message, ("z", "y"), split_axis=0, concat_axis=0, tiled=True)
    grad_cond = cond_back(d_mod, w_ada, conditioning)
    g_w_ada, g_b_ada, g_w_dw2, g_b_dw2, g_b_fc1, g_w_dw1, g_b_dw1, g_b_out, g_b_fc2, g_b_qv = unpack(
        got, model, groups
    )
    result = gather_strips(*res, BF16).reshape(tokens.shape)
    g_w_qkv, g_w_out = at.finish((3, 1))
    return (
        result, token_grad, grad_cond, g_w_ada, g_b_ada[0],
        g_w_dw1, g_b_dw1[0], g_w_qkv, g_b_qv[0], g_w_out.T, g_b_out[0],
        g_w_fc1, g_b_fc1[0], g_w_dw2, g_b_dw2[0], g_w_fc2.T, g_b_fc2[0],
    )


def solution(mesh):
    strip, canvas = mesh.devices.shape
    finer = Mesh(mesh.devices.reshape(strip // 2, 2, canvas // 2, 2), ("x", "core", "z", "y"))
    strips, groups, every = ("x", "core"), ("z", "y"), ("x", "core", "z", "y")
    block = P(groups, strips, None, None)
    return jax.shard_map(
        shards,
        mesh=finer,
        in_specs=(block, P(groups, None), P(groups, None)) + (P(),) * 14 + (block,),
        out_specs=(
            block, block, P(groups, None), P(every, None), P(every),
            P(None, every), P(every), P(every, None), P(every),
            P(None, every), P(every), P(every, None), P(every),
            P(None, every), P(every), P(None, every), P(every),
        ),
        check_vma=False,
    )
```

```python
import functools
import jax, jax.numpy as jnp
from jax import lax
from jax.sharding import Mesh, PartitionSpec as P
from jax.experimental import pallas as pl
from jax.experimental.pallas import tpu as pltpu

LANES = 128
F32 = jnp.float32
BF16 = jnp.bfloat16


class Order:
    last = ()

    @classmethod
    def passed(cls, outputs):
        cls.last = (outputs[0] if isinstance(outputs, (list, tuple)) else outputs,)
        return outputs


def ordered_call(kernel, in_specs, deps=(), micros=1, vmem=60, prefetch=None, **kw):
    deps = tuple(deps) + Order.last
    front = 0 if prefetch is None else 1
    skip, first = len(deps), front + len(in_specs)

    def body(*refs):
        return kernel(*refs[front:first], *refs[first + skip :])

    in_specs = list(in_specs) + [pl.BlockSpec(memory_space=pl.ANY)] * skip
    if prefetch is None:
        kw["in_specs"] = in_specs
    else:
        inner = {name: kw.pop(name) for name in ("grid", "out_specs")}
        kw["grid_spec"] = pltpu.PrefetchScalarGridSpec(num_scalar_prefetch=1, in_specs=in_specs, **inner)
    call = pl.pallas_call(
        body,
        compiler_params=pltpu.CompilerParams(vmem_limit_bytes=vmem << 20),
        cost_estimate=cost(micros),
        **kw,
    )
    given = () if prefetch is None else (prefetch,)
    return lambda *args: Order.passed(call(*given, *args, *deps))


def my_core():
    return lax.axis_index("core")


def my_strip():
    return 2 * lax.axis_index("x") + lax.axis_index("core")


def dot_nn(left, right):
    return jnp.dot(left, right, preferred_element_type=F32)


def dot_nt(left, right):
    return lax.dot_general(left, right, (((1,), (1,)), ((), ())), preferred_element_type=F32)


def cost(micros):
    return pl.CostEstimate(flops=int(micros * 5e6), bytes_accessed=int(micros * 5e3), transcendentals=0)


KINDS = ((2, 0, 1), (0, 1, 3))


def prep_kernel(half, ids, sides, seams, mask, order, back):
    mid, group = half // 2, half * half
    same = lambda p, q: (ids[0, p] == ids[0, q]).astype(F32)
    shape = (group, LANES)
    spot = lax.broadcasted_iota(jnp.int32, shape, 0)
    place, line = spot % half, spot // half
    top = line < mid
    col = jnp.where(top, same(0, 1), same(2, 3))
    sides[0] = jnp.where(place == 0, 0.0, jnp.where(place == mid, col, 1.0))
    sides[1] = jnp.where(place == half - 1, 0.0, jnp.where(place == mid - 1, col, 1.0))
    place = lax.broadcasted_iota(jnp.int32, (half, LANES), 0)
    rows = jnp.where(place < mid, same(0, 2), same(1, 3))
    down, up = same(0, 3), same(1, 2)
    seams[0] = rows
    seams[1] = jnp.where(place == 0, 0.0, jnp.where(place == mid, down, rows))
    seams[2] = jnp.where(place == half - 1, 0.0, jnp.where(place == mid - 1, up, rows))
    seams[3] = jnp.where(place == 0, 0.0, jnp.where(place == mid, up, rows))
    seams[4] = jnp.where(place == half - 1, 0.0, jnp.where(place == mid - 1, down, rows))

    def named(axis):
        spot = lax.broadcasted_iota(jnp.int32, (group, group), axis)
        upper, left = spot // half < mid, spot % half < mid
        return jnp.where(
            upper, jnp.where(left, ids[0, 0], ids[0, 1]), jnp.where(left, ids[0, 2], ids[0, 3])
        )

    mask[...] = jnp.where(named(0) == named(1), 0.0, -1e30)

    def source(axis):
        n = order.shape[0]
        m = lax.broadcasted_iota(jnp.int32, (n, n), axis)
        each = n // 4
        a, e = m // (2 * each), (m // each) % 2
        i, j = (m % each) // half, m % half
        return (2 * i + a) * 2 * half + 2 * j + e, lax.broadcasted_iota(jnp.int32, (n, n), 1 - axis)

    wanted, here = source(0)
    order[...] = jnp.where(wanted == here, 1.0, 0.0).astype(BF16)
    wanted, here = source(1)
    back[...] = jnp.where(wanted == here, 1.0, 0.0).astype(BF16)


def prep(ids, half, strip_rows):
    group = half * half
    sds = jax.ShapeDtypeStruct
    shapes = [sds((2, group, LANES), F32), sds((5, half, LANES), F32), sds((group, group), F32),
              sds((strip_rows, strip_rows), BF16), sds((strip_rows, strip_rows), BF16)]
    return ordered_call(
        functools.partial(prep_kernel, half),
        [pl.BlockSpec(memory_space=pltpu.SMEM)],
        out_specs=[pl.BlockSpec(v.shape) for v in shapes],
        out_shape=shapes,
        micros=3,
        name="prep",
    )(ids)


def clear_rims(store, half, width):
    zero = jnp.zeros((half, width), F32)
    for a in range(2):
        for kind in range(4):
            store[a, kind, 0:half, :] = zero
            store[a, kind, (half + 2) * half : (half + 3) * half, :] = zero


def fill_seam(store, seams, half, lanes):
    mid = half // 2
    seam_at = pl.ds((mid + 1) * half, half)
    for a, source, left_id, right_id in ((1, mid, 1, 2), (0, mid + 2, 3, 4)):
        rows = pl.ds(source * half, half)
        even = store[a, 0, rows, lanes]
        odd = store[a, 1, rows, lanes]
        store[a, 0, seam_at, lanes] = even * seams[0]
        store[a, 1, seam_at, lanes] = odd * seams[0]
        store[a, 2, seam_at, lanes] = pltpu.roll(odd, 1, 0) * seams[left_id]
        store[a, 3, seam_at, lanes] = pltpu.roll(even, half - 1, 0) * seams[right_id]


def put_row(store, a, e, place, lanes, value, sides, rows, half):
    store[a, e, place, lanes] = value
    if e == 1:
        store[a, 2, place, lanes] = pltpu.roll(value, 1, 0) * sides[0, rows, :]
    else:
        store[a, 3, place, lanes] = pltpu.roll(value, half - 1, 0) * sides[1, rows, :]


def row_sources(store, at, half, lanes):
    spots = ((1, -1), (0, 0), (1, 0), (0, 1))
    return [
        [store[a, kind, pl.ds(pl.multiple_of((at + off) * half, half), half), lanes] for kind in range(4)]
        for a, off in spots
    ]


def tap_source(sources, a, e, tap):
    return sources[a + tap // 3][KINDS[e][tap % 3]]


def store_row(step, half):
    return step + 1 + (step >= half // 2).astype(jnp.int32)


def gelu_pair(u):
    size = jnp.abs(u)
    decay = jnp.exp2((u * u) * -0.7213475204444817)
    base = 1.0 + 0.23164190 * size
    guess = pl.reciprocal(base, approx=True)
    t = guess * (2.0 - base * guess)
    poly = t * (0.127414796 + t * (-0.142248368 + t * (0.710706870 + t * (-0.726576013 + t * 0.530702714))))
    tail = poly * decay
    share = jnp.where(u >= 0.0, 1.0 - tail, tail)
    return u * share, share + u * (decay * 0.3989422804014327)


def ff_kernel(half, nb, nbt, db, dbt, w1_next, w1_last, w2, w2_next, b1, b1_next, wd, bd, sides, seams,
              gk1, gs1, gk2, gs2, small, branch_out, dnb_out, S, D, dact, act, dh, branch, dnb):
    step_at, steps = pl.program_id(0), pl.num_programs(0) - 1
    width = w2.shape[0]
    group, mid = half * half, half // 2
    blocks = [pl.ds(lb * LANES, LANES) for lb in range(width // LANES)]
    half_rows = nbt.shape[0] // 2
    now = step_at % 2
    later = 1 - now

    def put_hidden(store, a, w1, bias, which=(0, 1)):
        for e in which:
            rows = pl.ds(pl.multiple_of((2 * a + e) * group, group), group)
            h = dot_nn(nb[rows, :], w1[...]) + bias[...]
            h = h.astype(BF16).astype(F32)
            shifted = pltpu.roll(h, 1 if e == 1 else group - 1, 0)
            for part in range(2):
                cut = slice(part * group // 2, (part + 1) * group // 2)
                place = pl.ds(half + part * (group // 2 + half), group // 2)
                store[a, e, place, :] = h[cut]
                for lb, lanes in enumerate(blocks):
                    moved = shifted[cut, lb * LANES : (lb + 1) * LANES] * sides[1 - e, cut, :]
                    store[a, 3 - e, place, lanes] = moved

    def put_dact(a, weights, which=(0, 1)):
        for e in which:
            rows = pl.ds(pl.multiple_of((2 * a + e) * group, group), group)
            dact[rows, :] = dot_nt(db[rows, :], weights[...])

    tile = 256

    def add_rows(total, left, weights, n, transposed):
        cols = pl.ds(n * tile, tile)
        if transposed:
            total[:, cols] += dot_nt(left[...], weights[cols, :])
        else:
            total[:, cols] += dot_nn(left[...], weights[:, cols])

    def add_gradient(acc, left, right, k):
        cols = pl.ds(k * tile, tile)
        acc[...] += dot_nn(left[:, cols], right[cols, :])

    def set_gradient(left, right, keep, send):
        keep[...] = dot_nn(left[0:half_rows, :], right[...]).astype(BF16)
        send[...] = dot_nn(left[half_rows:, :], right[...]).astype(BF16)

    def post_back():
        units = [functools.partial(add_rows, dnb, dh, w1_last, n, True) for n in range(nbt.shape[0] // tile)]
        return units + [functools.partial(set_gradient, nbt, dh, gk1, gs1)]

    def woven(lines, units):
        done = 0
        for at, line in enumerate(lines):
            line()
            while done < len(units) and (done + 1) * len(lines) <= (at + 1) * len(units):
                units[done]()
                done += 1

    @pl.when(step_at == 0)
    def _():
        for parity in range(2):
            clear_rims(S.at[parity], half, width)
        clear_rims(D, half, width)
        branch[...] = jnp.zeros_like(branch)
        dnb[...] = jnp.zeros_like(dnb)
        dh[...] = jnp.zeros_like(dh)
        for a in range(2):
            put_hidden(S.at[0], a, w1_last, b1)
            put_dact(a, w2)
        for lanes in blocks:
            fill_seam(S.at[0], seams, half, lanes)

    @pl.when(step_at < steps)
    def _():
        here, there = S.at[now], S.at[later]
        wide_taps = wd[...].astype(F32)
        lane_taps = lambda lb: [wide_taps[t : t + 1, lb * LANES : (lb + 1) * LANES] for t in range(9)]

        def forward():
            def line_of(lb, a_now, line):
                lanes = blocks[lb]
                taps, bias = lane_taps(lb), bd[:, lanes]
                step = a_now * mid + line
                at = step + 1 + a_now
                rows = pl.ds(pl.multiple_of(step * half, half), half)
                place = pl.ds(pl.multiple_of(at * half, half), half)
                sources = row_sources(here, at, half, lanes)
                for a in range(2):
                    for e in range(2):
                        pre = bias + taps[0] * tap_source(sources, a, e, 0)
                        for t in range(1, 9):
                            pre = pre + taps[t] * tap_source(sources, a, e, t)
                        value, slope = gelu_pair(pre)
                        token = pl.ds(pl.multiple_of((2 * a + e) * group + step * half, half), half)
                        act[token, lanes] = value.astype(BF16)
                        d_pre = (dact[token, lanes] * slope).astype(BF16).astype(F32)
                        put_row(D, a, e, place, lanes, d_pre, sides, rows, half)

            units = [functools.partial(put_hidden, there, a, w1_next, b1_next) for a in range(2)] + post_back()
            woven([functools.partial(line_of, lb, a, line) for lb in range(len(blocks)) for a in range(2)
                   for line in range(mid)], units)

        forward()
        for lanes in blocks:
            fill_seam(D, seams, half, lanes)
            fill_seam(there, seams, half, lanes)

        def backward(sums):
            sums = [list(v) for v in sums]
            fold = lambda v: v.reshape(-1, 8, LANES).sum(0)

            def line_of(lb, a_now, line):
                lanes = blocks[lb]
                taps, total_of = lane_taps(lb), sums[lb]
                step = a_now * mid + line
                at = step + 1 + a_now
                place = pl.ds(pl.multiple_of(at * half, half), half)
                sources = row_sources(D, at, half, lanes)
                for a in range(2):
                    for e in range(2):
                        hid = here[a, e, place, lanes]
                        total = None
                        for t in range(9):
                            x = tap_source(sources, a, e, t)
                            term = taps[8 - t] * x
                            total = term if total is None else total + term
                            total_of[8 - t] = total_of[8 - t] + fold(hid * x)
                        d_hid = total.astype(BF16)
                        token = pl.ds(pl.multiple_of((2 * a + e) * group + step * half, half), half)
                        dh[token, lanes] = d_hid
                        total_of[9] = total_of[9] + fold(sources[a + 1][e])
                        total_of[10] = total_of[10] + fold(d_hid.astype(F32))

            units = [functools.partial(add_rows, branch, act, w2, n, False) for n in range(nbt.shape[0] // tile)]
            units += [functools.partial(set_gradient, dbt, act, gk2, gs2)]
            units += [functools.partial(put_dact, a, w2_next) for a in range(2)]
            woven([functools.partial(line_of, lb, a, line) for lb in range(len(blocks)) for a in range(2)
                   for line in range(mid)], units)
            return tuple(tuple(v) for v in sums)

        zero = jnp.zeros((8, LANES), F32)
        sums = backward(tuple((zero,) * 11 for _ in blocks))
        for lanes, total_of in zip(blocks, sums):
            for at, total in enumerate(total_of):
                small[at : at + 1, lanes] = jnp.sum(total, 0, keepdims=True)

    @pl.when(step_at == steps)
    def _():
        for unit in post_back():
            unit()
        branch_out[...] = branch[...].astype(BF16)
        dnb_out[...] = dnb[...].astype(BF16)


def feed_forward(nb, nbt, db, dbt, w1, wd, w2, biases, sides, seams, half, chunk, deps=()):
    tokens, model = nb.shape
    hidden = w1.shape[1]
    padded = (half + 3) * half
    steps = hidden // chunk
    last = lambda i: jnp.maximum(i - 1, 0)
    this = lambda i: jnp.minimum(i, steps - 1)
    ahead = lambda i: jnp.minimum(i + 1, steps - 1)
    column = lambda rows, when, at=0: pl.BlockSpec((rows, chunk), lambda i: (0, at + when(i)))
    flat = lambda when: pl.BlockSpec((chunk, model), lambda i: (when(i), 0))
    sds = jax.ShapeDtypeStruct
    return ordered_call(
        functools.partial(ff_kernel, half),
        [
            whole((tokens, model)), whole((model, tokens)), whole((tokens, model)), whole((model, tokens)),
            column(model, ahead), column(model, last), flat(this), flat(ahead),
            column(1, this), column(1, ahead), column(9, this), column(1, this, steps),
            whole(sides.shape), whole(seams.shape),
        ],
        deps,
        grid=(steps + 1,),
        out_specs=[column(model // 2, last)] * 2 + [column(model // 2, this)] * 2
        + [column(16, this), whole((tokens, model)), whole((tokens, model))],
        out_shape=[sds((model // 2, hidden), BF16)] * 4
        + [sds((16, hidden), F32), sds((tokens, model), BF16), sds((tokens, model), BF16)],
        scratch_shapes=[
            pltpu.VMEM((2, 2, 4, padded, chunk), F32),
            pltpu.VMEM((2, 4, padded, chunk), F32),
            pltpu.VMEM((tokens, chunk), F32),
            pltpu.VMEM((tokens, chunk), BF16),
            pltpu.VMEM((tokens, chunk), BF16),
            pltpu.VMEM((tokens, model), F32),
            pltpu.VMEM((tokens, model), F32),
        ],
        micros=70,
        name="feed_forward",
    )(nb, nbt, db, dbt, w1, w1, w2, w2, biases, biases, wd, biases, sides, seams)


HEADS = 12
STRIP = 128
HEAD_DIM = 64
norm_eps = 1e-06


def dot_tn(left, right):
    return lax.dot_general(left, right, (((0,), (0,)), ((), ())), preferred_element_type=F32)


def whole(shape):
    return pl.BlockSpec(shape, lambda *_: (0,) * len(shape))


def mod_rows(mod):
    width = mod.shape[1] // 6
    return [mod[pl.ds(my_strip(), 1), part * width : (part + 1) * width] for part in range(6)]


def standardize(values):
    centred = values - jnp.mean(values, -1, keepdims=True)
    inv_std = lax.rsqrt(jnp.mean(centred * centred, -1, keepdims=True) + norm_eps)
    return centred * inv_std, inv_std


def norm_reverse(grad_hat, normed_hat, inv_std):
    mean_grad = jnp.mean(grad_hat, -1, keepdims=True)
    mean_cross = jnp.mean(grad_hat * normed_hat, -1, keepdims=True)
    return inv_std * (grad_hat - mean_grad - normed_hat * mean_cross)


def take_strip(strip, pieces, order, store, group, each, part):
    for k, piece in enumerate(pieces):
        source = jnp.bitwise_xor(strip, k)
        moved = dot_nn(order, piece)
        for g in range(4):
            at = pl.multiple_of(g * group + source * each, each)
            store[pl.ds(at, each), :] = moved[g * each : (g + 1) * each].astype(store.dtype)


def first_kernel(half, own, r1, r2, r3, order, mod, wd, bd, sides, seams, later,
                 xg, na, cat, c1, c2, c3, S, conv, held, sems):
    group = half * half
    each = own.shape[1] // 4
    strip = my_strip()
    fetch = [
        pltpu.make_async_copy(later.at[jnp.bitwise_xor(strip, n + 1)], held.at[n], sems.at[0, n]) for n in range(3)
    ]
    for copy in fetch:
        copy.start()
    parts_of = mod_rows(mod)
    take_strip(strip, (own[strip], r1[...], r2[...], r3[...]), order[...], xg, group, each, 0)
    width = xg.shape[1]
    clear_rims(S, half, width)
    mid_rows = group // 2
    for g in range(4):
        a, e = g // 2, g % 2
        rows = pl.ds(g * group, group)
        hat, _ = standardize(xg[rows, :].astype(F32))
        low = (hat * (1.0 + parts_of[1]) + parts_of[0]).astype(BF16)
        na[rows, :] = low
        h = low.astype(F32)
        for part in range(2):
            S[a, e, pl.ds(half + part * (mid_rows + half), mid_rows), :] = h[part * mid_rows : (part + 1) * mid_rows]
        shifted = pltpu.roll(h, 1 if e == 1 else group - 1, 0)
        for lb in range(width // LANES):
            lanes = pl.ds(lb * LANES, LANES)
            moved = shifted[:, lb * LANES : (lb + 1) * LANES] * sides[0 if e == 1 else 1]
            for part in range(2):
                S[a, 2 if e == 1 else 3, pl.ds(half + part * (mid_rows + half), mid_rows), lanes] = (
                    moved[part * mid_rows : (part + 1) * mid_rows]
                )

    for copy in fetch:
        copy.wait()
    give = [pltpu.make_async_copy(held.at[n], out, sems.at[1, n]) for n, out in enumerate((c1, c2, c3))]
    for copy in give:
        copy.start()

    def block(lb, carry):
        lanes = pl.ds(pl.multiple_of(lb * LANES, LANES), LANES)
        fill_seam(S, seams, half, lanes)
        wide_taps = wd[:, lanes].astype(F32)
        taps = [wide_taps[t : t + 1] for t in range(9)]
        bias = bd[:, lanes]

        def forward(step, inner):
            at = store_row(step, half)
            sources = row_sources(S, at, half, lanes)
            for a in range(2):
                for e in range(2):
                    pre = bias + taps[0] * tap_source(sources, a, e, 0)
                    for t in range(1, 9):
                        pre = pre + taps[t] * tap_source(sources, a, e, t)
                    token = pl.ds(pl.multiple_of((2 * a + e) * group + step * half, half), half)
                    conv[token, lanes] = pre.astype(BF16)
            return inner

        return lax.fori_loop(0, half, forward, carry, unroll=4)

    lax.fori_loop(0, width // LANES, block, 0)
    for g in range(4):
        rows = pl.ds(g * group, group)
        cat[:, rows] = conv[rows, :].T
    for copy in give:
        copy.wait()


def first_norm(own, r1, r2, r3, order, mod, wd, biases, sides, seams, later, half, at, deps=()):
    tokens, model = 4 * half * half, own.shape[2]
    sds = jax.ShapeDtypeStruct
    return ordered_call(
        functools.partial(first_kernel, half),
        [
            whole(own.shape), whole(r1.shape), whole(r2.shape), whole(r3.shape), whole(order.shape),
            whole(mod.shape), whole(wd.shape), pl.BlockSpec((1, model), lambda i: (0, at)),
            whole(sides.shape), whole(seams.shape), pl.BlockSpec(memory_space=pl.ANY),
        ],
        deps,
        grid=(1,),
        out_specs=[whole((tokens, model)), whole((tokens, model)), whole((model, tokens))]
        + [pl.BlockSpec(memory_space=pl.ANY)] * 3,
        scratch_shapes=[
            pltpu.VMEM((2, 4, (half + 3) * half, model), F32),
            pltpu.VMEM((tokens, model), BF16),
            pltpu.VMEM((3,) + later.shape[1:], later.dtype),
            pltpu.SemaphoreType.DMA((2, 3)),
        ],
        out_shape=[sds((tokens, model), BF16), sds((tokens, model), BF16), sds((model, tokens), BF16)]
        + [sds(later.shape[1:], later.dtype)] * 3,
        micros=10,
        name="first_norm",
    )(own, r1, r2, r3, order, mod, wd, biases, sides, seams, later)


def attend_kernel(half, cat, wt, bias, mask, wout, bout, mod, xg, perm,
                  qkvt, lse, ot, proj, mid, nb, nbt, scores, probs):
    group = half * half
    model = cat.shape[0]
    parts_of = mod_rows(mod)
    pick_row = (lax.broadcasted_iota(jnp.int32, (8, group), 0) == 0).astype(BF16)
    for part in range(3):
        rows = pl.ds(part * model, model)
        product = dot_nn(wt[rows, :], cat[...])
        if part != 1:
            own = bias[:, (part // 2) * model : (part // 2 + 1) * model].astype(BF16)
            product = product + dot_tn(jnp.broadcast_to(own, (8, model)), pick_row)
        qkvt[rows, :] = product.astype(BF16)
    rows_of = lambda part, h: slice(part * model + h * HEAD_DIM, part * model + (h + 1) * HEAD_DIM)
    for h in range(HEADS):
        q = qkvt[rows_of(0, h), :] * HEAD_DIM ** (-0.5)
        scores[h] = dot_tn(qkvt[rows_of(1, h), :], q)
    for h in range(HEADS):
        s = scores[h] + mask[...]
        top = jnp.max(s, 0, keepdims=True)
        p = jnp.exp(s - top)
        total = jnp.sum(p, 0, keepdims=True)
        probs[h] = (p * (1.0 / total)).astype(BF16)
        lse[0, h : h + 1, :] = top + jnp.log(total)
    for h in range(HEADS):
        ot[rows_of(0, h), :] = dot_nn(qkvt[rows_of(2, h), :], probs[h]).astype(BF16)
    projection = dot_tn(ot[...], wout[...]) + bout[...]
    proj[...] = projection.astype(BF16)
    middle = xg[...].astype(F32) + parts_of[2] * projection
    mid[...] = middle
    hat, _ = standardize(middle)
    low = (hat * (1.0 + parts_of[4]) + parts_of[3]).astype(BF16)
    nb[...] = low
    nbt[...] = dot_nt(perm[...], low).astype(BF16)


def attend(cat, wt, biases, mask, wout, mod, xg, perm, half, at_qv, at_out, deps=()):
    model, tokens = cat.shape
    group = half * half
    sds = jax.ShapeDtypeStruct
    tall = lambda rows: pl.BlockSpec((rows, group), lambda i: (0, i))
    flat = pl.BlockSpec((group, model), lambda i: (i, 0))
    return ordered_call(
        functools.partial(attend_kernel, half),
        [
            tall(model), whole(wt.shape), pl.BlockSpec((1, 2 * model), lambda i: (0, at_qv)),
            whole(mask.shape), whole(wout.shape), pl.BlockSpec((1, model), lambda i: (0, at_out)),
            whole(mod.shape), flat, whole(perm.shape),
        ],
        deps,
        grid=(4,),
        out_specs=[tall(3 * model), pl.BlockSpec((1, 16, group), lambda i: (i, 0, 0)), tall(model),
                   flat, flat, flat, tall(model)],
        out_shape=[sds((3 * model, tokens), BF16), sds((4, 16, group), F32), sds((model, tokens), BF16),
                   sds((tokens, model), BF16), sds((tokens, model), F32), sds((tokens, model), BF16),
                   sds((model, tokens), BF16)],
        scratch_shapes=[pltpu.VMEM((HEADS, group, group), F32), pltpu.VMEM((HEADS, group, group), BF16)],
        micros=26,
        name="attend",
    )(cat, wt, biases, mask, wout, biases, mod, xg, perm)


def gate_kernel(half, own, r1, r2, r3, order, mod, perm, gg, db, dbt, small):
    group = half * half
    each = own.shape[1] // 4
    parts_of = mod_rows(mod)
    strip = my_strip()
    take_strip(strip, (own[strip], r1[...], r2[...], r3[...]), order[...], gg, group, each, 0)
    total = jnp.zeros((1, gg.shape[1]), F32)
    for g in range(4):
        rows = pl.ds(g * group, group)
        low = (parts_of[5] * gg[rows, :].astype(F32)).astype(BF16)
        db[rows, :] = low
        total = total + jnp.sum(low.astype(F32), 0, keepdims=True)
        dbt[:, rows] = dot_nt(perm[...], low).astype(BF16)
    small[...] = total


def gate(own, r1, r2, r3, order, mod, perm, half, deps=()):
    tokens, model = 4 * half * half, own.shape[2]
    sds = jax.ShapeDtypeStruct
    args = (own, r1, r2, r3, order, mod, perm)
    return ordered_call(
        functools.partial(gate_kernel, half),
        [whole(v.shape) for v in args],
        deps,
        grid=(1,),
        out_specs=[whole((tokens, model)), whole((tokens, model)), whole((model, tokens)), whole((1, model))],
        out_shape=[sds((tokens, model), BF16), sds((tokens, model), BF16), sds((model, tokens), BF16), sds((1, model), F32)],
        micros=5,
        name="gate",
    )(*args)


def give_strip(strip, store, order_back, outs, group, each):
    for k, out in enumerate(outs):
        target = jnp.bitwise_xor(strip, k)
        rows = [store[pl.ds(pl.multiple_of(g * group + target * each, each), each), :] for g in range(4)]
        out[...] = dot_nn(order_back, jnp.concatenate(rows, 0)).astype(out.dtype)


def middle_kernel(half, branch, dnb, mid, proj, gg, wout, bfc2, mod, back, perm,
                  o0, o1, o2, o3, dmid, dot_, dpt, small, res):
    step = pl.program_id(0)
    group = half * half
    parts_of = mod_rows(mod)

    @pl.when(step == 0)
    def _():
        small[...] = jnp.zeros_like(small)

    full = branch[...].astype(F32) + bfc2[...]
    middle = mid[...]
    g = gg[...].astype(F32)
    res[pl.ds(pl.multiple_of(step * group, group), group), :] = (middle + parts_of[5] * full).astype(BF16)
    hat, inv = standardize(middle)
    d = dnb[...].astype(F32)
    d_mid = g + norm_reverse(d * (1.0 + parts_of[4]), hat, inv)
    dmid[...] = d_mid.astype(BF16)
    low = (parts_of[2] * d_mid).astype(BF16)
    rows = (
        d_mid * proj[...].astype(F32), d, d * hat, g * full, low.astype(F32),
    )
    for at, value in enumerate(rows):
        small[at : at + 1, :] += jnp.sum(value, 0, keepdims=True)
    dot_[...] = dot_nt(wout[...], low).astype(BF16)
    dpt[...] = dot_nt(perm[...], low).astype(BF16)

    @pl.when(step == pl.num_programs(0) - 1)
    def _():
        give_strip(my_strip(), res, back[...], (o0, o1, o2, o3), group, back.shape[0] // 4)


def middle(branch, dnb, mid, proj, gg, wout, biases, mod, back, perm, half, at, deps=()):
    tokens, model = mid.shape
    group = half * half
    sds = jax.ShapeDtypeStruct
    tall = pl.BlockSpec((model, group), lambda i: (0, i))
    flat = pl.BlockSpec((group, model), lambda i: (i, 0))
    strip = back.shape[0]
    return ordered_call(
        functools.partial(middle_kernel, half),
        [flat, flat, flat, flat, flat, whole(wout.shape), pl.BlockSpec((1, model), lambda i: (0, at)),
         whole(mod.shape), whole(back.shape), whole(perm.shape)],
        deps,
        grid=(4,),
        out_specs=[whole((strip, model))] * 4 + [flat, tall, tall, whole((8, model))],
        out_shape=[sds((strip, model), BF16)] * 4 + [sds((tokens, model), BF16), sds((model, tokens), BF16),
                   sds((model, tokens), BF16), sds((8, model), F32)],
        scratch_shapes=[pltpu.VMEM((tokens, model), BF16)],
        micros=12,
        name="middle",
    )(branch, dnb, mid, proj, gg, wout, biases, mod, back, perm)


def attend_back_kernel(half, span, q, k, v, do, ot, lse, mask, cat, dpt, perm, wq, wk, wv,
                       gk1, gk2, gs1, gs2, dct, small, catp, acc, grads, scores, changes, low_ds, low_p):
    group = half * half
    step = pl.program_id(0)
    model = cat.shape[0]

    @pl.when(step == 0)
    def _():
        catp[...] = dot_nn(perm[...], cat[...]).astype(BF16)
        acc[...] = jnp.zeros_like(acc)

    scale = HEAD_DIM ** (-0.5)
    heads = span // HEAD_DIM
    pairs = [(h, g) for h in range(heads) for g in range(4)]
    spot = lambda h, g: (slice(h * HEAD_DIM, (h + 1) * HEAD_DIM), slice(g * group, (g + 1) * group))
    for n, (h, g) in enumerate(pairs):
        at = spot(h, g)
        scores[n] = dot_tn(k[at], q[at] * scale)
        changes[n] = dot_tn(v[at], do[at])
    for n, (h, g) in enumerate(pairs):
        p = jnp.exp(scores[n] + mask[...] - lse[g, pl.ds(step * heads + h, 1), :])
        dp = changes[n]
        delta = jnp.sum(p * dp, 0, keepdims=True)
        low_ds[n] = (p * (dp - delta)).astype(BF16)
        low_p[n] = p.astype(BF16)
    for n, (h, g) in enumerate(pairs):
        rows, cols = spot(h, g)
        part_rows = lambda part: slice(part * span + h * HEAD_DIM, part * span + (h + 1) * HEAD_DIM)
        grads[part_rows(0), cols] = (dot_nn(k[rows, cols], low_ds[n]) * scale).astype(BF16)
        grads[part_rows(1), cols] = (dot_nt(q[rows, cols], low_ds[n]) * scale).astype(BF16)
        grads[part_rows(2), cols] = dot_nt(do[rows, cols], low_p[n]).astype(BF16)
    ones = jnp.ones((8, grads.shape[1]), BF16)
    outs = ((gk1, gs1, 0), (gk1, gs1, 1), (gk2, gs2, 0))
    for part in range(3):
        mine = grads[part * span : (part + 1) * span, :]
        if part != 1:
            small[part // 2 : part // 2 + 1, :] = dot_nt(ones, mine)[0:1]
        product = dot_nt(catp[...], mine).astype(BF16)
        keep, send, at = outs[part]
        keep[at] = product[: model // 2]
        send[at] = product[model // 2 :]
    weights = jnp.concatenate([wq[...], wk[...], wv[...]], 1)
    acc[...] += dot_nn(weights, grads[...])
    product = dot_nt(dpt[...], ot[...]).astype(BF16)
    gk2[1] = product[: model // 2]
    gs2[1] = product[model // 2 :]

    @pl.when(step == pl.num_programs(0) - 1)
    def _():
        dct[...] = acc[...].astype(BF16)


def attend_back(qkvt, dot_, ot, lse, mask, cat, dpt, perm, w, half, span, deps=()):
    model, tokens = cat.shape
    group = half * half
    steps = model // span
    sds = jax.ShapeDtypeStruct
    part = lambda n: pl.BlockSpec((span, tokens), lambda i: (n * steps + i, 0))
    return ordered_call(
        functools.partial(attend_back_kernel, half, span),
        [
            part(0), part(1), part(2), part(0), part(0), whole(lse.shape), whole(mask.shape), whole(cat.shape),
            whole(dpt.shape), whole(perm.shape),
            *[pl.BlockSpec((model, span), lambda i, n=n: (0, n * steps + i)) for n in range(3)],
        ],
        deps,
        grid=(steps,),
        out_specs=[pl.BlockSpec((2, model // 2, span), lambda i: (0, 0, i))] * 4
        + [whole((model, tokens)), pl.BlockSpec((2, span), lambda i: (0, i))],
        out_shape=[sds((2, model // 2, model), BF16)] * 4 + [sds((model, tokens), BF16), sds((2, model), F32)],
        scratch_shapes=[pltpu.VMEM((model, tokens), BF16), pltpu.VMEM((model, tokens), F32),
                        pltpu.VMEM((3 * span, tokens), BF16),
                        *[pltpu.VMEM((4 * span // HEAD_DIM, group, group), kind) for kind in (F32, F32, BF16, BF16)]],
        micros=30,
        name="attend_back",
    )(qkvt, qkvt, qkvt, dot_, ot, lse, mask, cat, dpt, perm, w, w, w)


def conv_back_kernel(half, dct, na, xg, wd, sides, seams, dna, small, D):
    group = half * half
    width = xg.shape[1]
    clear_rims(D, half, width)
    mid_rows = group // 2
    for g in range(4):
        a, e = g // 2, g % 2
        rows = pl.ds(g * group, group)
        h = dct[:, rows].T.astype(F32)
        for part in range(2):
            D[a, e, pl.ds(half + part * (mid_rows + half), mid_rows), :] = h[part * mid_rows : (part + 1) * mid_rows]
        shifted = pltpu.roll(h, 1 if e == 1 else group - 1, 0)
        for lb in range(width // LANES):
            lanes = pl.ds(lb * LANES, LANES)
            moved = shifted[:, lb * LANES : (lb + 1) * LANES] * sides[0 if e == 1 else 1]
            for part in range(2):
                D[a, 2 if e == 1 else 3, pl.ds(half + part * (mid_rows + half), mid_rows), lanes] = (
                    moved[part * mid_rows : (part + 1) * mid_rows]
                )

    def block(lb, carry):
        lanes = pl.ds(pl.multiple_of(lb * LANES, LANES), LANES)
        fill_seam(D, seams, half, lanes)
        wide_taps = wd[:, lanes].astype(F32)
        taps = [wide_taps[t : t + 1] for t in range(9)]

        def backward(step, sums):
            sums = list(sums)
            at = store_row(step, half)
            sources = row_sources(D, at, half, lanes)
            fold = lambda v: v.reshape(-1, 8, LANES).sum(0)
            for a in range(2):
                for e in range(2):
                    token = pl.ds(pl.multiple_of((2 * a + e) * group + step * half, half), half)
                    hid = na[token, lanes].astype(F32)
                    total = None
                    for t in range(9):
                        x = tap_source(sources, a, e, t)
                        term = taps[8 - t] * x
                        total = term if total is None else total + term
                        sums[8 - t] = sums[8 - t] + fold(hid * x)
                    dna[token, lanes] = total.astype(BF16)
                    sums[9] = sums[9] + fold(sources[a + 1][e])
                    sums[10] = sums[10] + fold(total)
            return tuple(sums)

        sums = lax.fori_loop(0, half, backward, tuple(jnp.zeros((8, LANES), F32) for _ in range(11)), unroll=4)
        for at, total in enumerate(sums):
            small[at : at + 1, lanes] = jnp.sum(total, 0, keepdims=True)
        return carry

    lax.fori_loop(0, width // LANES, block, 0)
    scale_sum = jnp.zeros((1, width), F32)
    for g in range(4):
        rows = pl.ds(g * group, group)
        hat, _ = standardize(xg[rows, :].astype(F32))
        scale_sum = scale_sum + jnp.sum(dna[rows, :].astype(F32) * hat, 0, keepdims=True)
    small[11:12, :] = scale_sum


def conv_back(dct, na, xg, wd, sides, seams, half, deps=()):
    tokens, model = xg.shape
    sds = jax.ShapeDtypeStruct
    args = (dct, na, xg, wd, sides, seams)
    return ordered_call(
        functools.partial(conv_back_kernel, half),
        [whole(v.shape) for v in args],
        deps,
        grid=(1,),
        out_specs=[whole((tokens, model)), whole((16, model))],
        out_shape=[sds((tokens, model), BF16), sds((16, model), F32)],
        scratch_shapes=[pltpu.VMEM((2, 4, (half + 3) * half, model), F32)],
        micros=11,
        name="conv_back",
    )(*args)


def last_kernel(half, dna, xg, dmid, mod, back, o0, o1, o2, o3, tig):
    group = half * half
    parts_of = mod_rows(mod)
    for g in range(4):
        rows = pl.ds(g * group, group)
        hat, inv = standardize(xg[rows, :].astype(F32))
        change = norm_reverse(dna[rows, :].astype(F32) * (1.0 + parts_of[1]), hat, inv)
        tig[rows, :] = (dmid[rows, :].astype(F32) + change).astype(BF16)
    give_strip(my_strip(), tig, back[...], (o0, o1, o2, o3), group, back.shape[0] // 4)


def last(dna, xg, dmid, mod, back, half, deps=()):
    tokens, model = xg.shape
    args = (dna, xg, dmid, mod, back)
    strip = back.shape[0]
    return ordered_call(
        functools.partial(last_kernel, half),
        [whole(v.shape) for v in args],
        deps,
        grid=(1,),
        out_specs=[whole((strip, model))] * 4,
        out_shape=[jax.ShapeDtypeStruct((strip, model), BF16)] * 4,
        scratch_shapes=[pltpu.VMEM((tokens, model), BF16)],
        micros=5,
        name="last",
    )(*args)


def cut_kernel(source, o1, o2, o3):
    strip = my_strip()
    for k, out in enumerate((o1, o2, o3)):
        out[...] = source[jnp.bitwise_xor(strip, k + 1)]


def cut_strips(values, deps=()):
    shape = jax.ShapeDtypeStruct(values.shape[1:], values.dtype)
    return ordered_call(
        cut_kernel,
        [whole(values.shape)],
        deps,
        grid=(1,),
        out_specs=[whole(shape.shape)] * 3,
        out_shape=[shape] * 3,
        micros=2,
        name="cut_strips",
    )(values)


def gather_kernel(own, c1, c2, c3, out):
    strip = my_strip()
    for k, piece in enumerate((own, c1, c2, c3)):
        out[jnp.bitwise_xor(strip, k)] = piece[...].astype(out.dtype)


def gather_strips(own, c1, c2, c3, dtype, deps=()):
    rows, model = own.shape
    return ordered_call(
        gather_kernel,
        [whole(own.shape)] * 4,
        deps,
        grid=(1,),
        out_specs=whole((4, rows, model)),
        out_shape=jax.ShapeDtypeStruct((4, rows, model), dtype),
        vmem=20,
        micros=3,
        name="gather_strips",
    )(own, c1, c2, c3)


def swap(values, axis):
    return lax.ppermute(values, axis, [(0, 1), (1, 0)])


def fold_kernel(count, *refs):
    ins, outs = refs[: 2 * count], refs[2 * count :]
    for at, out in enumerate(outs):
        total = ins[at * count][...].astype(F32)
        for term in ins[at * count + 1 : (at + 1) * count]:
            total = total + term[...].astype(F32)
        out[...] = total.astype(BF16)


def spread_kernel(count, z_count, *refs):
    ins, outs = refs[: 2 * count], refs[2 * count :]
    z = lax.axis_index("z")
    for at in range(2):
        total = ins[at * count][0].astype(F32)
        for term in ins[at * count + 1 : (at + 1) * count]:
            total = total + term[0].astype(F32)
        total = total.astype(BF16)
        rows = total.shape[0]
        shard = rows // z_count
        line = lax.broadcasted_iota(jnp.int32, (shard, rows), 0)
        place = lax.broadcasted_iota(jnp.int32, (shard, rows), 1)
        for k, out in enumerate(outs):
            wanted = (place == line + jnp.bitwise_xor(z, k) * shard).astype(F32).astype(BF16)
            out[at, 0] = dot_nn(wanted, total).astype(BF16)


def close_kernel(together, *refs):
    outs, got = refs[-len(together) :], refs[: -len(together)]
    _, mine, _, width = got[0].shape
    part = 0
    for count, out in zip(together, outs):
        for at in range(count):
            total = got[0][part // mine, part % mine].astype(F32)
            for more in got[1:]:
                total = total + more[part // mine, part % mine].astype(F32)
            out[:, at * width : (at + 1) * width] = total
            part += 1


class SumOverAll:
    def __init__(self, place, keep, send, z_count):
        keep = [v.reshape((-1,) + v.shape[-2:]) for v in keep]
        self.place, self.z_count, self.keep = place, z_count, keep
        self.mine_parts, self.rows, self.width = keep[0].shape
        self.quarter = self.rows // 4
        self.block = min(1536, self.width)
        self.other = [swap(v.reshape((-1,) + v.shape[-2:]), "core") for v in send]

    def fold(self, terms, halves, name, spread=False, deps=()):
        first = len(terms[0])
        specs, args = [], []
        for side in terms:
            for array, row in side:
                def index(p, h, n, place, row=row):
                    return p, row(h, place[0], place[1]), n

                specs.append(pl.BlockSpec((1, self.quarter, self.block), index))
                args.append(array)
        mine = self.mine_parts
        if spread:
            shard = self.quarter // self.z_count
            out_specs = [
                pl.BlockSpec((2, 1, shard, self.block), lambda p, h, n, place: (0, p, 0, n))
            ] * self.z_count
            out_shape = [jax.ShapeDtypeStruct((2, mine, shard, self.width), BF16)] * self.z_count
            kernel = functools.partial(spread_kernel, first, self.z_count)
        else:
            out_specs = [pl.BlockSpec((1, self.quarter, self.block), lambda p, h, n, place: (p, h, n))] * 2
            out_shape = [jax.ShapeDtypeStruct((mine, halves * self.quarter, self.width), BF16)] * 2
            kernel = functools.partial(fold_kernel, first)
        return ordered_call(
            kernel,
            specs,
            deps,
            grid=(mine, halves, self.width // self.block),
            out_specs=out_specs,
            out_shape=out_shape,
            prefetch=self.place,
            micros=2,
            name=name,
        )(*args)

    def second(self):
        (k1, k2), (r1, r2) = self.keep, self.other
        away_x = lambda h, x, y: 2 * (1 - x) + h
        away_y = lambda h, x, y: 2 * h + (1 - y)
        a, b = self.fold([[(k1, away_x), (r1, away_x)], [(k2, away_y), (r2, away_y)]], 2, "fold_second")
        self.got_a, self.got_b = swap(a, "x"), swap(b, "y")
        return a, b

    def third(self):
        (k1, k2), (r1, r2) = self.keep, self.other
        near = lambda h, x, y: 2 * x + (1 - y)
        far = lambda h, x, y: 2 * (1 - x) + y
        a, b = self.fold(
            [
                [(k1, near), (r1, near), (self.got_a, lambda h, x, y: 1 - y)],
                [(k2, far), (r2, far), (self.got_b, lambda h, x, y: 1 - x)],
            ],
            1, "fold_third",
        )
        self.last_a, self.last_b = swap(a, "y"), swap(b, "x")
        return a, b

    def fourth(self, deps=()):
        (k1, k2), (r1, r2) = self.keep, self.other
        own = lambda h, x, y: 2 * x + y
        zero = lambda h, x, y: 0
        self.mine = self.fold(
            [
                [(k1, own), (r1, own), (self.got_a, lambda h, x, y: y), (self.last_a, zero)],
                [(k2, own), (r2, own), (self.got_b, lambda h, x, y: x), (self.last_b, zero)],
            ],
            1, "fold_fourth", True, deps,
        )
        pairs = lambda k: [(i, i ^ k) for i in range(self.z_count)]
        self.mine = [v if k == 0 else lax.ppermute(v, "z", pairs(k)) for k, v in enumerate(self.mine)]

    def finish(self, together, deps=()):
        shard = self.mine[0].shape[2]
        shapes = [jax.ShapeDtypeStruct((shard, count * self.width), F32) for count in together]
        return ordered_call(
            functools.partial(close_kernel, together),
            [whole(v.shape) for v in self.mine],
            deps,
            grid=(1,),
            out_specs=[whole(v.shape) for v in shapes],
            out_shape=shapes,
            vmem=20,
        micros=2,
            name="close_sums",
        )(*self.mine)


MODS = 6


def pack_kernel(groups, ff, fc2, mid, qv, last, o0, o1, o2, o3, work):
    work[...] = jnp.zeros_like(work)
    model = last.shape[1]
    strip_width = model // 4
    d_mod = [last[10:11, :], last[11:12, :]] + [mid[k : k + 1, :] for k in range(4)]
    short = [last[k : k + 1, :] for k in range(10)] + [mid[4:5, :], fc2[...]]
    for t in range(4):
        work[t, 0:11, :] = ff[0:11, t * model : (t + 1) * model]
        for k, row in enumerate(d_mod):
            work[t, 11 + k : 12 + k, :] = row
        for k, row in enumerate(short):
            work[t, 17 + k : 18 + k, 0:strip_width] = row[:, t * strip_width : (t + 1) * strip_width]
        at = (2 * t * strip_width) % model
        work[t, 29:30, 0 : 2 * strip_width] = qv[t // 2 : t // 2 + 1, at : at + 2 * strip_width]
    for k, out in enumerate((o0, o1, o2, o3)):
        out[...] = work[jnp.bitwise_xor(my_strip(), k)].astype(BF16)


def pack(ff, fc2, mid, qv, last, groups, deps=()):
    args = (ff, fc2, mid, qv, last)
    model = last.shape[1]
    return ordered_call(
        functools.partial(pack_kernel, groups),
        [whole(v.shape) for v in args],
        deps,
        grid=(1,),
        out_specs=[whole((32, model))] * 4,
        out_shape=[jax.ShapeDtypeStruct((32, model), BF16)] * 4,
        scratch_shapes=[pltpu.VMEM((4, 32, model), F32)],
        vmem=20,
        micros=2,
        name="pack_small",
    )(*args)


def repack_kernel(groups, g0, g1, g2, g3, cond, out, mods, work, common):
    model = g0.shape[1]
    work[...] = jnp.zeros_like(work)
    values = [g[...].astype(F32) for g in (g0, g1, g2, g3)]
    total = values[0] + values[1] + values[2] + values[3]
    lanes = model // LANES
    head = MODS * lanes * 4
    for part in range(MODS):
        for lb in range(lanes):
            for k in range(4):
                at = (part * lanes + lb) * 4 + jnp.bitwise_xor(my_strip(), k)
                row = values[k][11 + part : 12 + part, lb * LANES : (lb + 1) * LANES]
                common[pl.ds(at, 1), :] = row
    for part in range(MODS):
        for lb in range(lanes):
            at = (part * lanes + lb) * 4
            mods[:, (part * lanes + lb) * LANES : (part * lanes + lb + 1) * LANES] = common[at : at + 4, :].astype(BF16)
    wide, thin = model // groups, model // 4 // groups
    for u in range(groups):
        work[u, 0:11, 0:wide] = total[0:11, u * wide : (u + 1) * wide]
        work[u, 17:29, 0:thin] = total[17:29, u * thin : (u + 1) * thin]
        work[u, 29:30, 0 : 2 * thin] = total[29:30, 2 * u * thin : 2 * (u + 1) * thin]
        work[u, 32:36, 0:thin] = cond[:, u * thin : (u + 1) * thin].astype(F32)
        out[u, 0:head, :] = common[...].astype(BF16)
        out[u, head:, :] = work[u].astype(BF16)


def repack(got, cond, groups, deps=()):
    model = got[0].shape[1]
    head = MODS * (model // LANES) * 4
    args = (*got, cond)
    shapes = [(groups, head + 48, LANES), (4, MODS * model)]
    return ordered_call(
        functools.partial(repack_kernel, groups),
        [whole(v.shape) for v in args],
        deps,
        grid=(1,),
        out_specs=[whole(v) for v in shapes],
        out_shape=[jax.ShapeDtypeStruct(v, BF16) for v in shapes],
        scratch_shapes=[pltpu.VMEM((groups, 48, LANES), F32), pltpu.VMEM((head, LANES), F32)],
        vmem=20,
        micros=2,
        name="repack_small",
    )(*args)


def unpack_kernel(groups, got, wada, bada, *refs):
    outs, (mods, conds) = refs[:-2], refs[-2:]
    head = got.shape[1] - 48
    total = jnp.sum(got[:, head:, :].astype(F32), 0)
    rows = ((0, 9), (9, 10), (10, 11), (17, 26), (26, 27), (27, 28), (28, 29), (29, 30))
    for (first, end), out in zip(rows, outs):
        out[...] = total[first:end, 0 : out.shape[1]]
    for u in range(groups):
        values = got[u].astype(F32)
        conds[u * 4 : (u + 1) * 4, :] = values[head + 32 : head + 36]
        for block in range(head // 4):
            mods[u * 4 : (u + 1) * 4, block * LANES : (block + 1) * LANES] = values[block * 4 : block * 4 + 4]
    shard, own = wada.shape[0], bada.shape[1]
    wada[...] = dot_tn(conds[...].astype(BF16), mods[...].astype(BF16))[0:shard]
    index = my_strip() * groups + lax.axis_index("z") * 2 + lax.axis_index("y")
    summed = jnp.broadcast_to(jnp.sum(mods[...], 0, keepdims=True), (8, mods.shape[1]))
    bada[...] = pltpu.roll(summed, mods.shape[1] - own * index, 1)[0:1, 0:own]


def unpack(got, model, groups, deps=()):
    wide, thin = model // groups, model // 4 // groups
    shapes = [(thin, MODS * model), (1, MODS * thin)]
    shapes += [(9, wide), (1, wide), (1, wide), (9, thin), (1, thin), (1, thin), (1, thin), (1, 2 * thin)]
    return ordered_call(
        functools.partial(unpack_kernel, groups),
        [whole(got.shape)],
        deps,
        grid=(1,),
        out_specs=[whole(v) for v in shapes],
        out_shape=[jax.ShapeDtypeStruct(v, F32) for v in shapes],
        scratch_shapes=[pltpu.VMEM((4 * groups, MODS * model), F32), pltpu.VMEM((4 * groups, LANES), F32)],
        vmem=20,
        micros=2,
        name="unpack_small",
    )(got)


def cond_back_kernel(mods, wada, cond, out):
    change = dot_nt(wada[...], mods[...]).T
    values = cond[...].astype(F32)
    gain = 1.0 / (1.0 + jnp.exp(-values))
    out[...] = change * gain * (1.0 + values * (1.0 - gain))


def cond_back(mods, wada, cond, deps=()):
    canvases, model = cond.shape
    tile = model // 3
    return ordered_call(
        cond_back_kernel,
        [whole(mods.shape), pl.BlockSpec((tile, wada.shape[1]), lambda i: (i, 0)),
         pl.BlockSpec((canvases, tile), lambda i: (0, i))],
        deps,
        grid=(3,),
        out_specs=pl.BlockSpec((canvases, tile), lambda i: (0, i)),
        out_shape=jax.ShapeDtypeStruct((canvases, model), F32),
        micros=3,
        name="cond_back",
    )(mods, wada, cond)


def row_order(model, z_count):
    rows = jnp.arange(model, dtype=jnp.int32).reshape(2, 2, z_count, 2, -1)
    rows = jnp.transpose(rows, (1, 0, 3, 2, 4)).reshape(2, -1)
    rows = jnp.where(lax.axis_index("core") == 0, rows, rows[::-1]).reshape(-1)
    return (rows[:, None] == jnp.arange(model, dtype=jnp.int32)[None]).astype(BF16)


def shards(
    tokens, conditioning, latent_ids, w_ada, b_ada, w_dw1, b_dw1, w_qkv, b_qv, w_out, b_out,
    w_fc1, b_fc1, w_dw2, b_dw2, w_fc2, b_fc2, out_grad,
):
    canvases, rows, cols, model = tokens.shape
    half = cols // 2
    hidden = w_fc1.shape[1]
    z_count = lax.axis_size("z")
    groups = 2 * z_count
    devices = 4 * groups
    strip = my_strip()
    strips = ("x", "core")
    span = 256
    Order.last = ()

    def exchange(pieces):
        return [lax.ppermute(piece, strips, [(i, i ^ (k + 1)) for i in range(4)]) for k, piece in enumerate(pieces)]

    token_rows = tokens.reshape(canvases, rows * cols, model)
    grad_rows = out_grad.reshape(canvases, rows * cols, model)
    token_pieces = exchange(cut_strips(token_rows))

    cond_vals = conditioning.astype(F32)
    cond_act = jax.nn.silu(cond_vals).astype(BF16)
    mod = jnp.dot(cond_act, w_ada, preferred_element_type=F32) + b_ada.astype(F32)
    cond_cols = lax.dynamic_slice_in_dim(cond_act, strip * (model // 4), model // 4, 1)
    place = jnp.stack([lax.axis_index("x"), lax.axis_index("y")]).astype(jnp.int32)
    perm = row_order(model, z_count)

    ids = lax.dynamic_slice_in_dim(latent_ids, strip, 1, 0)
    sides, seams, mask, order, back = prep(ids, half, rows * cols)
    listed = (b_fc1, b_dw2, b_qv, b_dw1, b_out, b_fc2)
    biases = jnp.concatenate(listed).astype(F32)[None]
    places = [sum(v.shape[0] for v in listed[:n]) // listed[n].shape[0] for n in range(6)]
    wt = w_qkv.T

    xg, na, cat, *grad_cut = first_norm(
        token_rows, *token_pieces, order, mod, w_dw1, biases, sides, seams, grad_rows, half, places[3], (wt, cond_cols, perm, place)
    )
    grad_pieces = exchange(grad_cut)
    qkvt, lse, ot, proj, mid, nb, nbt = attend(
        cat, wt, biases, mask, w_out, mod, xg, perm, half, places[2], places[4]
    )
    gg, db, dbt, small_fc2 = gate(grad_rows, *grad_pieces, order, mod, perm, half)
    ff_k1, ff_s1, ff_k2, ff_s2, small_ff, branch, dnb = feed_forward(
        nb, nbt, db, dbt, w_fc1, w_dw2, w_fc2, biases, sides, seams, half, 256
    )
    ff = SumOverAll(place, (ff_k1, ff_k2), (ff_s1, ff_s2), z_count)
    *res, dmid, dot_, dpt, small_mid = middle(
        branch, dnb, mid, proj, gg, w_out, biases, mod, back, perm, half, places[5]
    )
    res = [res[0]] + exchange(res[1:])
    ff.second()
    at_k1, at_k2, at_s1, at_s2, dct, small_qv = attend_back(
        qkvt, dot_, ot, lse, mask, cat, dpt, perm, w_qkv, half, span
    )
    at = SumOverAll(place, (at_k1, at_k2), (at_s1, at_s2), z_count)
    ff.third()
    at.second()
    dna, small_last = conv_back(dct, na, xg, w_dw1, sides, seams, half)
    ff.fourth()
    tig = last(dna, xg, dmid, mod, back, half)
    tig = [tig[0]] + exchange(tig[1:])
    message = pack(small_ff, small_fc2, small_mid, small_qv, small_last, groups)
    got = [message[0]] + exchange(message[1:])
    at.third()
    token_grad = gather_strips(*tig, F32).reshape(tokens.shape)
    g_w_fc1, g_w_fc2 = ff.finish((1, 1))
    at.fourth()
    message, d_mod = repack(got, cond_cols, groups)
    got = lax.all_to_all(message, ("z", "y"), split_axis=0, concat_axis=0, tiled=True)
    grad_cond = cond_back(d_mod, w_ada, conditioning)
    g_w_ada, g_b_ada, g_w_dw2, g_b_dw2, g_b_fc1, g_w_dw1, g_b_dw1, g_b_out, g_b_fc2, g_b_qv = unpack(
        got, model, groups
    )
    result = gather_strips(*res, BF16).reshape(tokens.shape)
    g_w_qkv, g_w_out = at.finish((3, 1))
    return (
        result, token_grad, grad_cond, g_w_ada, g_b_ada[0],
        g_w_dw1, g_b_dw1[0], g_w_qkv, g_b_qv[0], g_w_out.T, g_b_out[0],
        g_w_fc1, g_b_fc1[0], g_w_dw2, g_b_dw2[0], g_w_fc2.T, g_b_fc2[0],
    )


def solution(mesh):
    strip, canvas = mesh.devices.shape
    finer = Mesh(mesh.devices.reshape(strip // 2, 2, canvas // 2, 2), ("x", "core", "z", "y"))
    strips, groups, every = ("x", "core"), ("z", "y"), ("x", "core", "z", "y")
    block = P(groups, strips, None, None)
    return jax.shard_map(
        shards,
        mesh=finer,
        in_specs=(block, P(groups, None), P(groups, None)) + (P(),) * 14 + (block,),
        out_specs=(
            block, block, P(groups, None), P(every, None), P(every),
            P(None, every), P(every), P(every, None), P(every),
            P(None, every), P(every), P(every, None), P(every),
            P(None, every), P(every), P(None, every), P(every),
        ),
        check_vma=False,
    )
```

```python
import functools
import jax, jax.numpy as jnp
from jax import lax
from jax.sharding import Mesh, PartitionSpec as P
from jax.experimental import pallas as pl
from jax.experimental.pallas import tpu as pltpu

LANES = 128
F32 = jnp.float32
BF16 = jnp.bfloat16


class Order:
    last = ()

    @classmethod
    def passed(cls, outputs):
        cls.last = (outputs[0] if isinstance(outputs, (list, tuple)) else outputs,)
        return outputs


def ordered_call(kernel, in_specs, deps=(), micros=1, vmem=60, prefetch=None, **kw):
    deps = tuple(deps) + Order.last
    front = 0 if prefetch is None else 1
    skip, first = len(deps), front + len(in_specs)

    def body(*refs):
        return kernel(*refs[front:first], *refs[first + skip :])

    in_specs = list(in_specs) + [pl.BlockSpec(memory_space=pl.ANY)] * skip
    if prefetch is None:
        kw["in_specs"] = in_specs
    else:
        inner = {name: kw.pop(name) for name in ("grid", "out_specs")}
        kw["grid_spec"] = pltpu.PrefetchScalarGridSpec(num_scalar_prefetch=1, in_specs=in_specs, **inner)
    call = pl.pallas_call(
        body,
        compiler_params=pltpu.CompilerParams(vmem_limit_bytes=vmem << 20),
        cost_estimate=cost(micros),
        **kw,
    )
    given = () if prefetch is None else (prefetch,)
    return lambda *args: Order.passed(call(*given, *args, *deps))


def my_core():
    return lax.axis_index("core")


def my_strip():
    return 2 * lax.axis_index("x") + lax.axis_index("core")


def dot_nn(left, right):
    return jnp.dot(left, right, preferred_element_type=F32)


def dot_nt(left, right):
    return lax.dot_general(left, right, (((1,), (1,)), ((), ())), preferred_element_type=F32)


def cost(micros):
    return pl.CostEstimate(flops=int(micros * 5e6), bytes_accessed=int(micros * 5e3), transcendentals=0)


KINDS = ((2, 0, 1), (0, 1, 3))


def prep_kernel(half, ids, sides, seams, mask, order, back):
    mid, group = half // 2, half * half
    same = lambda p, q: (ids[0, p] == ids[0, q]).astype(F32)
    shape = (group, LANES)
    spot = lax.broadcasted_iota(jnp.int32, shape, 0)
    place, line = spot % half, spot // half
    top = line < mid
    col = jnp.where(top, same(0, 1), same(2, 3))
    sides[0] = jnp.where(place == 0, 0.0, jnp.where(place == mid, col, 1.0))
    sides[1] = jnp.where(place == half - 1, 0.0, jnp.where(place == mid - 1, col, 1.0))
    place = lax.broadcasted_iota(jnp.int32, (half, LANES), 0)
    rows = jnp.where(place < mid, same(0, 2), same(1, 3))
    down, up = same(0, 3), same(1, 2)
    seams[0] = rows
    seams[1] = jnp.where(place == 0, 0.0, jnp.where(place == mid, down, rows))
    seams[2] = jnp.where(place == half - 1, 0.0, jnp.where(place == mid - 1, up, rows))
    seams[3] = jnp.where(place == 0, 0.0, jnp.where(place == mid, up, rows))
    seams[4] = jnp.where(place == half - 1, 0.0, jnp.where(place == mid - 1, down, rows))

    def named(axis):
        spot = lax.broadcasted_iota(jnp.int32, (group, group), axis)
        upper, left = spot // half < mid, spot % half < mid
        return jnp.where(
            upper, jnp.where(left, ids[0, 0], ids[0, 1]), jnp.where(left, ids[0, 2], ids[0, 3])
        )

    mask[...] = jnp.where(named(0) == named(1), 0.0, -1e30)

    def source(axis):
        n = order.shape[0]
        m = lax.broadcasted_iota(jnp.int32, (n, n), axis)
        each = n // 4
        a, e = m // (2 * each), (m // each) % 2
        i, j = (m % each) // half, m % half
        return (2 * i + a) * 2 * half + 2 * j + e, lax.broadcasted_iota(jnp.int32, (n, n), 1 - axis)

    wanted, here = source(0)
    order[...] = jnp.where(wanted == here, 1.0, 0.0).astype(BF16)
    wanted, here = source(1)
    back[...] = jnp.where(wanted == here, 1.0, 0.0).astype(BF16)


def prep(ids, half, strip_rows):
    group = half * half
    sds = jax.ShapeDtypeStruct
    shapes = [sds((2, group, LANES), F32), sds((5, half, LANES), F32), sds((group, group), F32),
              sds((strip_rows, strip_rows), BF16), sds((strip_rows, strip_rows), BF16)]
    return ordered_call(
        functools.partial(prep_kernel, half),
        [pl.BlockSpec(memory_space=pltpu.SMEM)],
        out_specs=[pl.BlockSpec(v.shape) for v in shapes],
        out_shape=shapes,
        micros=3,
        name="prep",
    )(ids)


def clear_rims(store, half, width):
    zero = jnp.zeros((half, width), F32)
    for a in range(2):
        for kind in range(4):
            store[a, kind, 0:half, :] = zero
            store[a, kind, (half + 2) * half : (half + 3) * half, :] = zero


def fill_seam(store, seams, half, lanes):
    mid = half // 2
    seam_at = pl.ds((mid + 1) * half, half)
    for a, source, left_id, right_id in ((1, mid, 1, 2), (0, mid + 2, 3, 4)):
        rows = pl.ds(source * half, half)
        even = store[a, 0, rows, lanes]
        odd = store[a, 1, rows, lanes]
        store[a, 0, seam_at, lanes] = even * seams[0]
        store[a, 1, seam_at, lanes] = odd * seams[0]
        store[a, 2, seam_at, lanes] = pltpu.roll(odd, 1, 0) * seams[left_id]
        store[a, 3, seam_at, lanes] = pltpu.roll(even, half - 1, 0) * seams[right_id]


def put_row(store, a, e, place, lanes, value, sides, rows, half):
    store[a, e, place, lanes] = value
    if e == 1:
        store[a, 2, place, lanes] = pltpu.roll(value, 1, 0) * sides[0, rows, :]
    else:
        store[a, 3, place, lanes] = pltpu.roll(value, half - 1, 0) * sides[1, rows, :]


def row_sources(store, at, half, lanes):
    spots = ((1, -1), (0, 0), (1, 0), (0, 1))
    return [
        [store[a, kind, pl.ds(pl.multiple_of((at + off) * half, half), half), lanes] for kind in range(4)]
        for a, off in spots
    ]


def tap_source(sources, a, e, tap):
    return sources[a + tap // 3][KINDS[e][tap % 3]]


def store_row(step, half):
    return step + 1 + (step >= half // 2).astype(jnp.int32)


def gelu_pair(u):
    size = jnp.abs(u)
    decay = jnp.exp2((u * u) * -0.7213475204444817)
    base = 1.0 + 0.23164190 * size
    guess = pl.reciprocal(base, approx=True)
    t = guess * (2.0 - base * guess)
    poly = t * (0.127414796 + t * (-0.142248368 + t * (0.710706870 + t * (-0.726576013 + t * 0.530702714))))
    tail = poly * decay
    share = jnp.where(u >= 0.0, 1.0 - tail, tail)
    return u * share, share + u * (decay * 0.3989422804014327)


def ff_kernel(half, nb, nbt, db, dbt, w1_next, w1_last, w2, w2_next, b1, b1_next, wd, bd, sides, seams,
              gk1, gs1, gk2, gs2, small, branch_out, dnb_out, S, D, dact, act, dh, branch, dnb):
    step_at, steps = pl.program_id(0), pl.num_programs(0) - 1
    width = w2.shape[0]
    group, mid = half * half, half // 2
    blocks = [pl.ds(lb * LANES, LANES) for lb in range(width // LANES)]
    half_rows = nbt.shape[0] // 2
    now = step_at % 2
    later = 1 - now

    def put_hidden(store, a, w1, bias, which=(0, 1)):
        for e in which:
            rows = pl.ds(pl.multiple_of((2 * a + e) * group, group), group)
            h = dot_nn(nb[rows, :], w1[...]) + bias[...]
            h = h.astype(BF16).astype(F32)
            shifted = pltpu.roll(h, 1 if e == 1 else group - 1, 0)
            for part in range(2):
                cut = slice(part * group // 2, (part + 1) * group // 2)
                place = pl.ds(half + part * (group // 2 + half), group // 2)
                store[a, e, place, :] = h[cut]
                for lb, lanes in enumerate(blocks):
                    moved = shifted[cut, lb * LANES : (lb + 1) * LANES] * sides[1 - e, cut, :]
                    store[a, 3 - e, place, lanes] = moved

    def put_dact(a, weights, which=(0, 1)):
        for e in which:
            rows = pl.ds(pl.multiple_of((2 * a + e) * group, group), group)
            dact[rows, :] = dot_nt(db[rows, :], weights[...])

    tile = 256

    def add_rows(total, left, weights, n, transposed):
        cols = pl.ds(n * tile, tile)
        if transposed:
            total[:, cols] += dot_nt(left[...], weights[cols, :])
        else:
            total[:, cols] += dot_nn(left[...], weights[:, cols])

    def add_gradient(acc, left, right, k):
        cols = pl.ds(k * tile, tile)
        acc[...] += dot_nn(left[:, cols], right[cols, :])

    def set_gradient(left, right, keep, send):
        keep[...] = dot_nn(left[0:half_rows, :], right[...]).astype(BF16)
        send[...] = dot_nn(left[half_rows:, :], right[...]).astype(BF16)

    def post_back():
        units = [functools.partial(add_rows, dnb, dh, w1_last, n, True) for n in range(nbt.shape[0] // tile)]
        return units + [functools.partial(set_gradient, nbt, dh, gk1, gs1)]

    def woven(lines, units):
        done = 0
        for at, line in enumerate(lines):
            line()
            while done < len(units) and (done + 1) * len(lines) <= (at + 1) * len(units):
                units[done]()
                done += 1

    @pl.when(step_at == 0)
    def _():
        for parity in range(2):
            clear_rims(S.at[parity], half, width)
        clear_rims(D, half, width)
        branch[...] = jnp.zeros_like(branch)
        dnb[...] = jnp.zeros_like(dnb)
        dh[...] = jnp.zeros_like(dh)
        for a in range(2):
            put_hidden(S.at[0], a, w1_last, b1)
            put_dact(a, w2)
        for lanes in blocks:
            fill_seam(S.at[0], seams, half, lanes)

    @pl.when(step_at < steps)
    def _():
        here, there = S.at[now], S.at[later]
        wide_taps = wd[...].astype(F32)
        lane_taps = lambda lb: [wide_taps[t : t + 1, lb * LANES : (lb + 1) * LANES] for t in range(9)]

        def forward():
            def line_of(lb, a_now, line):
                lanes = blocks[lb]
                taps, bias = lane_taps(lb), bd[:, lanes]
                step = a_now * mid + line
                at = step + 1 + a_now
                rows = pl.ds(pl.multiple_of(step * half, half), half)
                place = pl.ds(pl.multiple_of(at * half, half), half)
                sources = row_sources(here, at, half, lanes)
                for a in range(2):
                    for e in range(2):
                        pre = bias + taps[0] * tap_source(sources, a, e, 0)
                        for t in range(1, 9):
                            pre = pre + taps[t] * tap_source(sources, a, e, t)
                        value, slope = gelu_pair(pre)
                        token = pl.ds(pl.multiple_of((2 * a + e) * group + step * half, half), half)
                        act[token, lanes] = value.astype(BF16)
                        d_pre = (dact[token, lanes] * slope).astype(BF16).astype(F32)
                        put_row(D, a, e, place, lanes, d_pre, sides, rows, half)

            units = [functools.partial(put_hidden, there, a, w1_next, b1_next) for a in range(2)] + post_back()
            woven([functools.partial(line_of, lb, a, line) for lb in range(len(blocks)) for a in range(2)
                   for line in range(mid)], units)

        forward()
        for lanes in blocks:
            fill_seam(D, seams, half, lanes)
            fill_seam(there, seams, half, lanes)

        def backward(sums):
            sums = [list(v) for v in sums]
            fold = lambda v: v.reshape(-1, 8, LANES).sum(0)

            def line_of(lb, a_now, line):
                lanes = blocks[lb]
                taps, total_of = lane_taps(lb), sums[lb]
                step = a_now * mid + line
                at = step + 1 + a_now
                place = pl.ds(pl.multiple_of(at * half, half), half)
                sources = row_sources(D, at, half, lanes)
                for a in range(2):
                    for e in range(2):
                        hid = here[a, e, place, lanes]
                        total = None
                        for t in range(9):
                            x = tap_source(sources, a, e, t)
                            term = taps[8 - t] * x
                            total = term if total is None else total + term
                            total_of[8 - t] = total_of[8 - t] + fold(hid * x)
                        d_hid = total.astype(BF16)
                        token = pl.ds(pl.multiple_of((2 * a + e) * group + step * half, half), half)
                        dh[token, lanes] = d_hid
                        total_of[9] = total_of[9] + fold(sources[a + 1][e])
                        total_of[10] = total_of[10] + fold(d_hid.astype(F32))

            units = [functools.partial(add_rows, branch, act, w2, n, False) for n in range(nbt.shape[0] // tile)]
            units += [functools.partial(set_gradient, dbt, act, gk2, gs2)]
            units += [functools.partial(put_dact, a, w2_next) for a in range(2)]
            woven([functools.partial(line_of, lb, a, line) for lb in range(len(blocks)) for a in range(2)
                   for line in range(mid)], units)
            return tuple(tuple(v) for v in sums)

        zero = jnp.zeros((8, LANES), F32)
        sums = backward(tuple((zero,) * 11 for _ in blocks))
        for lanes, total_of in zip(blocks, sums):
            for at, total in enumerate(total_of):
                small[at : at + 1, lanes] = jnp.sum(total, 0, keepdims=True)

    @pl.when(step_at == steps)
    def _():
        for unit in post_back():
            unit()
        branch_out[...] = branch[...].astype(BF16)
        dnb_out[...] = dnb[...].astype(BF16)


def feed_forward(nb, nbt, db, dbt, w1, wd, w2, biases, sides, seams, half, chunk, deps=()):
    tokens, model = nb.shape
    hidden = w1.shape[1]
    padded = (half + 3) * half
    steps = hidden // chunk
    last = lambda i: jnp.maximum(i - 1, 0)
    this = lambda i: jnp.minimum(i, steps - 1)
    ahead = lambda i: jnp.minimum(i + 1, steps - 1)
    column = lambda rows, when, at=0: pl.BlockSpec((rows, chunk), lambda i: (0, at + when(i)))
    flat = lambda when: pl.BlockSpec((chunk, model), lambda i: (when(i), 0))
    sds = jax.ShapeDtypeStruct
    return ordered_call(
        functools.partial(ff_kernel, half),
        [
            whole((tokens, model)), whole((model, tokens)), whole((tokens, model)), whole((model, tokens)),
            column(model, ahead), column(model, last), flat(this), flat(ahead),
            column(1, this), column(1, ahead), column(9, this), column(1, this, steps),
            whole(sides.shape), whole(seams.shape),
        ],
        deps,
        grid=(steps + 1,),
        out_specs=[column(model // 2, last)] * 2 + [column(model // 2, this)] * 2
        + [column(16, this), whole((tokens, model)), whole((tokens, model))],
        out_shape=[sds((model // 2, hidden), BF16)] * 4
        + [sds((16, hidden), F32), sds((tokens, model), BF16), sds((tokens, model), BF16)],
        scratch_shapes=[
            pltpu.VMEM((2, 2, 4, padded, chunk), F32),
            pltpu.VMEM((2, 4, padded, chunk), F32),
            pltpu.VMEM((tokens, chunk), F32),
            pltpu.VMEM((tokens, chunk), BF16),
            pltpu.VMEM((tokens, chunk), BF16),
            pltpu.VMEM((tokens, model), F32),
            pltpu.VMEM((tokens, model), F32),
        ],
        micros=70,
        name="feed_forward",
    )(nb, nbt, db, dbt, w1, w1, w2, w2, biases, biases, wd, biases, sides, seams)


HEADS = 12
STRIP = 128
HEAD_DIM = 64
norm_eps = 1e-06


def dot_tn(left, right):
    return lax.dot_general(left, right, (((0,), (0,)), ((), ())), preferred_element_type=F32)


def whole(shape):
    return pl.BlockSpec(shape, lambda *_: (0,) * len(shape))


def mod_rows(mod):
    width = mod.shape[1] // 6
    return [mod[pl.ds(my_strip(), 1), part * width : (part + 1) * width] for part in range(6)]


def standardize(values):
    centred = values - jnp.mean(values, -1, keepdims=True)
    inv_std = lax.rsqrt(jnp.mean(centred * centred, -1, keepdims=True) + norm_eps)
    return centred * inv_std, inv_std


def norm_reverse(grad_hat, normed_hat, inv_std):
    mean_grad = jnp.mean(grad_hat, -1, keepdims=True)
    mean_cross = jnp.mean(grad_hat * normed_hat, -1, keepdims=True)
    return inv_std * (grad_hat - mean_grad - normed_hat * mean_cross)


def take_strip(strip, pieces, order, store, group, each, part):
    for k, piece in enumerate(pieces):
        source = jnp.bitwise_xor(strip, k)
        moved = dot_nn(order, piece)
        for g in range(4):
            at = pl.multiple_of(g * group + source * each, each)
            store[pl.ds(at, each), :] = moved[g * each : (g + 1) * each].astype(store.dtype)


def first_kernel(half, own, r1, r2, r3, order, mod, wd, bd, sides, seams, later,
                 xg, na, cat, c1, c2, c3, S, conv, held, sems):
    group = half * half
    each = own.shape[1] // 4
    strip = my_strip()
    fetch = [
        pltpu.make_async_copy(later.at[jnp.bitwise_xor(strip, n + 1)], held.at[n], sems.at[0, n]) for n in range(3)
    ]
    for copy in fetch:
        copy.start()
    parts_of = mod_rows(mod)
    take_strip(strip, (own[strip], r1[...], r2[...], r3[...]), order[...], xg, group, each, 0)
    width = xg.shape[1]
    clear_rims(S, half, width)
    mid_rows = group // 2
    for g in range(4):
        a, e = g // 2, g % 2
        rows = pl.ds(g * group, group)
        hat, _ = standardize(xg[rows, :].astype(F32))
        low = (hat * (1.0 + parts_of[1]) + parts_of[0]).astype(BF16)
        na[rows, :] = low
        h = low.astype(F32)
        for part in range(2):
            S[a, e, pl.ds(half + part * (mid_rows + half), mid_rows), :] = h[part * mid_rows : (part + 1) * mid_rows]
        shifted = pltpu.roll(h, 1 if e == 1 else group - 1, 0)
        for lb in range(width // LANES):
            lanes = pl.ds(lb * LANES, LANES)
            moved = shifted[:, lb * LANES : (lb + 1) * LANES] * sides[0 if e == 1 else 1]
            for part in range(2):
                S[a, 2 if e == 1 else 3, pl.ds(half + part * (mid_rows + half), mid_rows), lanes] = (
                    moved[part * mid_rows : (part + 1) * mid_rows]
                )

    for copy in fetch:
        copy.wait()
    give = [pltpu.make_async_copy(held.at[n], out, sems.at[1, n]) for n, out in enumerate((c1, c2, c3))]
    for copy in give:
        copy.start()

    def block(lb, carry):
        lanes = pl.ds(pl.multiple_of(lb * LANES, LANES), LANES)
        fill_seam(S, seams, half, lanes)
        wide_taps = wd[:, lanes].astype(F32)
        taps = [wide_taps[t : t + 1] for t in range(9)]
        bias = bd[:, lanes]

        def forward(step, inner):
            at = store_row(step, half)
            sources = row_sources(S, at, half, lanes)
            for a in range(2):
                for e in range(2):
                    pre = bias + taps[0] * tap_source(sources, a, e, 0)
                    for t in range(1, 9):
                        pre = pre + taps[t] * tap_source(sources, a, e, t)
                    token = pl.ds(pl.multiple_of((2 * a + e) * group + step * half, half), half)
                    conv[token, lanes] = pre.astype(BF16)
            return inner

        return lax.fori_loop(0, half, forward, carry, unroll=4)

    lax.fori_loop(0, width // LANES, block, 0)
    for g in range(4):
        rows = pl.ds(g * group, group)
        cat[:, rows] = conv[rows, :].T
    for copy in give:
        copy.wait()


def first_norm(own, r1, r2, r3, order, mod, wd, biases, sides, seams, later, half, at, deps=()):
    tokens, model = 4 * half * half, own.shape[2]
    sds = jax.ShapeDtypeStruct
    return ordered_call(
        functools.partial(first_kernel, half),
        [
            whole(own.shape), whole(r1.shape), whole(r2.shape), whole(r3.shape), whole(order.shape),
            whole(mod.shape), whole(wd.shape), pl.BlockSpec((1, model), lambda i: (0, at)),
            whole(sides.shape), whole(seams.shape), pl.BlockSpec(memory_space=pl.ANY),
        ],
        deps,
        grid=(1,),
        out_specs=[whole((tokens, model)), whole((tokens, model)), whole((model, tokens))]
        + [pl.BlockSpec(memory_space=pl.ANY)] * 3,
        scratch_shapes=[
            pltpu.VMEM((2, 4, (half + 3) * half, model), F32),
            pltpu.VMEM((tokens, model), BF16),
            pltpu.VMEM((3,) + later.shape[1:], later.dtype),
            pltpu.SemaphoreType.DMA((2, 3)),
        ],
        out_shape=[sds((tokens, model), BF16), sds((tokens, model), BF16), sds((model, tokens), BF16)]
        + [sds(later.shape[1:], later.dtype)] * 3,
        micros=10,
        name="first_norm",
    )(own, r1, r2, r3, order, mod, wd, biases, sides, seams, later)


def attend_kernel(half, cat, wt, bias, mask, wout, bout, mod, xg, perm,
                  qkvt, lse, ot, proj, mid, nb, nbt, scores, probs):
    group = half * half
    model = cat.shape[0]
    parts_of = mod_rows(mod)
    pick_row = (lax.broadcasted_iota(jnp.int32, (8, group), 0) == 0).astype(BF16)
    for part in range(3):
        rows = pl.ds(part * model, model)
        product = dot_nn(wt[rows, :], cat[...])
        if part != 1:
            own = bias[:, (part // 2) * model : (part // 2 + 1) * model].astype(BF16)
            product = product + dot_tn(jnp.broadcast_to(own, (8, model)), pick_row)
        qkvt[rows, :] = product.astype(BF16)
    rows_of = lambda part, h: slice(part * model + h * HEAD_DIM, part * model + (h + 1) * HEAD_DIM)
    for h in range(HEADS):
        q = qkvt[rows_of(0, h), :] * HEAD_DIM ** (-0.5)
        scores[h] = dot_tn(qkvt[rows_of(1, h), :], q)
    for h in range(HEADS):
        s = scores[h] + mask[...]
        top = jnp.max(s, 0, keepdims=True)
        p = jnp.exp(s - top)
        total = jnp.sum(p, 0, keepdims=True)
        probs[h] = (p * (1.0 / total)).astype(BF16)
        lse[0, h : h + 1, :] = top + jnp.log(total)
    for h in range(HEADS):
        ot[rows_of(0, h), :] = dot_nn(qkvt[rows_of(2, h), :], probs[h]).astype(BF16)
    projection = dot_tn(ot[...], wout[...]) + bout[...]
    proj[...] = projection.astype(BF16)
    middle = xg[...].astype(F32) + parts_of[2] * projection
    mid[...] = middle.astype(BF16)
    hat, _ = standardize(middle)
    low = (hat * (1.0 + parts_of[4]) + parts_of[3]).astype(BF16)
    nb[...] = low
    nbt[...] = dot_nt(perm[...], low).astype(BF16)


def attend(cat, wt, biases, mask, wout, mod, xg, perm, half, at_qv, at_out, deps=()):
    model, tokens = cat.shape
    group = half * half
    sds = jax.ShapeDtypeStruct
    tall = lambda rows: pl.BlockSpec((rows, group), lambda i: (0, i))
    flat = pl.BlockSpec((group, model), lambda i: (i, 0))
    return ordered_call(
        functools.partial(attend_kernel, half),
        [
            tall(model), whole(wt.shape), pl.BlockSpec((1, 2 * model), lambda i: (0, at_qv)),
            whole(mask.shape), whole(wout.shape), pl.BlockSpec((1, model), lambda i: (0, at_out)),
            whole(mod.shape), flat, whole(perm.shape),
        ],
        deps,
        grid=(4,),
        out_specs=[tall(3 * model), pl.BlockSpec((1, 16, group), lambda i: (i, 0, 0)), tall(model),
                   flat, flat, flat, tall(model)],
        out_shape=[sds((3 * model, tokens), BF16), sds((4, 16, group), F32), sds((model, tokens), BF16),
                   sds((tokens, model), BF16), sds((tokens, model), BF16), sds((tokens, model), BF16),
                   sds((model, tokens), BF16)],
        scratch_shapes=[pltpu.VMEM((HEADS, group, group), F32), pltpu.VMEM((HEADS, group, group), BF16)],
        micros=26,
        name="attend",
    )(cat, wt, biases, mask, wout, biases, mod, xg, perm)


def gate_kernel(half, own, r1, r2, r3, order, mod, perm, gg, db, dbt, small):
    group = half * half
    each = own.shape[1] // 4
    parts_of = mod_rows(mod)
    strip = my_strip()
    take_strip(strip, (own[strip], r1[...], r2[...], r3[...]), order[...], gg, group, each, 0)
    total = jnp.zeros((1, gg.shape[1]), F32)
    for g in range(4):
        rows = pl.ds(g * group, group)
        low = (parts_of[5] * gg[rows, :].astype(F32)).astype(BF16)
        db[rows, :] = low
        total = total + jnp.sum(low.astype(F32), 0, keepdims=True)
        dbt[:, rows] = dot_nt(perm[...], low).astype(BF16)
    small[...] = total


def gate(own, r1, r2, r3, order, mod, perm, half, deps=()):
    tokens, model = 4 * half * half, own.shape[2]
    sds = jax.ShapeDtypeStruct
    args = (own, r1, r2, r3, order, mod, perm)
    return ordered_call(
        functools.partial(gate_kernel, half),
        [whole(v.shape) for v in args],
        deps,
        grid=(1,),
        out_specs=[whole((tokens, model)), whole((tokens, model)), whole((model, tokens)), whole((1, model))],
        out_shape=[sds((tokens, model), BF16), sds((tokens, model), BF16), sds((model, tokens), BF16), sds((1, model), F32)],
        micros=5,
        name="gate",
    )(*args)


def give_strip(strip, store, order_back, outs, group, each):
    for k, out in enumerate(outs):
        target = jnp.bitwise_xor(strip, k)
        rows = [store[pl.ds(pl.multiple_of(g * group + target * each, each), each), :] for g in range(4)]
        out[...] = dot_nn(order_back, jnp.concatenate(rows, 0)).astype(out.dtype)


def middle_kernel(half, branch, dnb, mid, proj, gg, wout, bfc2, mod, back, perm,
                  o0, o1, o2, o3, dmid, dot_, dpt, small, res):
    step = pl.program_id(0)
    group = half * half
    parts_of = mod_rows(mod)

    @pl.when(step == 0)
    def _():
        small[...] = jnp.zeros_like(small)

    full = branch[...].astype(F32) + bfc2[...]
    middle = mid[...].astype(F32)
    g = gg[...].astype(F32)
    res[pl.ds(pl.multiple_of(step * group, group), group), :] = (middle + parts_of[5] * full).astype(BF16)
    hat, inv = standardize(middle)
    d = dnb[...].astype(F32)
    d_mid = g + norm_reverse(d * (1.0 + parts_of[4]), hat, inv)
    dmid[...] = d_mid.astype(BF16)
    low = (parts_of[2] * d_mid).astype(BF16)
    rows = (
        d_mid * proj[...].astype(F32), d, d * hat, g * full, low.astype(F32),
    )
    for at, value in enumerate(rows):
        small[at : at + 1, :] += jnp.sum(value, 0, keepdims=True)
    dot_[...] = dot_nt(wout[...], low).astype(BF16)
    dpt[...] = dot_nt(perm[...], low).astype(BF16)

    @pl.when(step == pl.num_programs(0) - 1)
    def _():
        give_strip(my_strip(), res, back[...], (o0, o1, o2, o3), group, back.shape[0] // 4)


def middle(branch, dnb, mid, proj, gg, wout, biases, mod, back, perm, half, at, deps=()):
    tokens, model = mid.shape
    group = half * half
    sds = jax.ShapeDtypeStruct
    tall = pl.BlockSpec((model, group), lambda i: (0, i))
    flat = pl.BlockSpec((group, model), lambda i: (i, 0))
    strip = back.shape[0]
    return ordered_call(
        functools.partial(middle_kernel, half),
        [flat, flat, flat, flat, flat, whole(wout.shape), pl.BlockSpec((1, model), lambda i: (0, at)),
         whole(mod.shape), whole(back.shape), whole(perm.shape)],
        deps,
        grid=(4,),
        out_specs=[whole((strip, model))] * 4 + [flat, tall, tall, whole((8, model))],
        out_shape=[sds((strip, model), BF16)] * 4 + [sds((tokens, model), BF16), sds((model, tokens), BF16),
                   sds((model, tokens), BF16), sds((8, model), F32)],
        scratch_shapes=[pltpu.VMEM((tokens, model), BF16)],
        micros=12,
        name="middle",
    )(branch, dnb, mid, proj, gg, wout, biases, mod, back, perm)


def attend_back_kernel(half, span, q, k, v, do, ot, lse, mask, cat, dpt, perm, wq, wk, wv,
                       gk1, gk2, gs1, gs2, dct, small, catp, acc, grads, scores, changes, low_ds, low_p):
    group = half * half
    step = pl.program_id(0)
    model = cat.shape[0]

    @pl.when(step == 0)
    def _():
        catp[...] = dot_nn(perm[...], cat[...]).astype(BF16)
        acc[...] = jnp.zeros_like(acc)

    scale = HEAD_DIM ** (-0.5)
    heads = span // HEAD_DIM
    pairs = [(h, g) for h in range(heads) for g in range(4)]
    spot = lambda h, g: (slice(h * HEAD_DIM, (h + 1) * HEAD_DIM), slice(g * group, (g + 1) * group))
    for n, (h, g) in enumerate(pairs):
        at = spot(h, g)
        scores[n] = dot_tn(k[at], q[at] * scale)
        changes[n] = dot_tn(v[at], do[at])
    for n, (h, g) in enumerate(pairs):
        p = jnp.exp(scores[n] + mask[...] - lse[g, pl.ds(step * heads + h, 1), :])
        dp = changes[n]
        delta = jnp.sum(p * dp, 0, keepdims=True)
        low_ds[n] = (p * (dp - delta)).astype(BF16)
        low_p[n] = p.astype(BF16)
    for n, (h, g) in enumerate(pairs):
        rows, cols = spot(h, g)
        part_rows = lambda part: slice(part * span + h * HEAD_DIM, part * span + (h + 1) * HEAD_DIM)
        grads[part_rows(0), cols] = (dot_nn(k[rows, cols], low_ds[n]) * scale).astype(BF16)
        grads[part_rows(1), cols] = (dot_nt(q[rows, cols], low_ds[n]) * scale).astype(BF16)
        grads[part_rows(2), cols] = dot_nt(do[rows, cols], low_p[n]).astype(BF16)
    ones = jnp.ones((8, grads.shape[1]), BF16)
    outs = ((gk1, gs1, 0), (gk1, gs1, 1), (gk2, gs2, 0))
    for part in range(3):
        mine = grads[part * span : (part + 1) * span, :]
        if part != 1:
            small[part // 2 : part // 2 + 1, :] = dot_nt(ones, mine)[0:1]
        product = dot_nt(catp[...], mine).astype(BF16)
        keep, send, at = outs[part]
        keep[at] = product[: model // 2]
        send[at] = product[model // 2 :]
    weights = jnp.concatenate([wq[...], wk[...], wv[...]], 1)
    acc[...] += dot_nn(weights, grads[...])
    product = dot_nt(dpt[...], ot[...]).astype(BF16)
    gk2[1] = product[: model // 2]
    gs2[1] = product[model // 2 :]

    @pl.when(step == pl.num_programs(0) - 1)
    def _():
        dct[...] = acc[...].astype(BF16)


def attend_back(qkvt, dot_, ot, lse, mask, cat, dpt, perm, w, half, span, deps=()):
    model, tokens = cat.shape
    group = half * half
    steps = model // span
    sds = jax.ShapeDtypeStruct
    part = lambda n: pl.BlockSpec((span, tokens), lambda i: (n * steps + i, 0))
    return ordered_call(
        functools.partial(attend_back_kernel, half, span),
        [
            part(0), part(1), part(2), part(0), part(0), whole(lse.shape), whole(mask.shape), whole(cat.shape),
            whole(dpt.shape), whole(perm.shape),
            *[pl.BlockSpec((model, span), lambda i, n=n: (0, n * steps + i)) for n in range(3)],
        ],
        deps,
        grid=(steps,),
        out_specs=[pl.BlockSpec((2, model // 2, span), lambda i: (0, 0, i))] * 4
        + [whole((model, tokens)), pl.BlockSpec((2, span), lambda i: (0, i))],
        out_shape=[sds((2, model // 2, model), BF16)] * 4 + [sds((model, tokens), BF16), sds((2, model), F32)],
        scratch_shapes=[pltpu.VMEM((model, tokens), BF16), pltpu.VMEM((model, tokens), F32),
                        pltpu.VMEM((3 * span, tokens), BF16),
                        *[pltpu.VMEM((4 * span // HEAD_DIM, group, group), kind) for kind in (F32, F32, BF16, BF16)]],
        micros=30,
        name="attend_back",
    )(qkvt, qkvt, qkvt, dot_, ot, lse, mask, cat, dpt, perm, w, w, w)


def conv_back_kernel(half, dct, na, xg, wd, sides, seams, dna, small, D):
    group = half * half
    width = xg.shape[1]
    clear_rims(D, half, width)
    mid_rows = group // 2
    for g in range(4):
        a, e = g // 2, g % 2
        rows = pl.ds(g * group, group)
        h = dct[:, rows].T.astype(F32)
        for part in range(2):
            D[a, e, pl.ds(half + part * (mid_rows + half), mid_rows), :] = h[part * mid_rows : (part + 1) * mid_rows]
        shifted = pltpu.roll(h, 1 if e == 1 else group - 1, 0)
        for lb in range(width // LANES):
            lanes = pl.ds(lb * LANES, LANES)
            moved = shifted[:, lb * LANES : (lb + 1) * LANES] * sides[0 if e == 1 else 1]
            for part in range(2):
                D[a, 2 if e == 1 else 3, pl.ds(half + part * (mid_rows + half), mid_rows), lanes] = (
                    moved[part * mid_rows : (part + 1) * mid_rows]
                )

    def block(lb, carry):
        lanes = pl.ds(pl.multiple_of(lb * LANES, LANES), LANES)
        fill_seam(D, seams, half, lanes)
        wide_taps = wd[:, lanes].astype(F32)
        taps = [wide_taps[t : t + 1] for t in range(9)]

        def backward(step, sums):
            sums = list(sums)
            at = store_row(step, half)
            sources = row_sources(D, at, half, lanes)
            fold = lambda v: v.reshape(-1, 8, LANES).sum(0)
            for a in range(2):
                for e in range(2):
                    token = pl.ds(pl.multiple_of((2 * a + e) * group + step * half, half), half)
                    hid = na[token, lanes].astype(F32)
                    total = None
                    for t in range(9):
                        x = tap_source(sources, a, e, t)
                        term = taps[8 - t] * x
                        total = term if total is None else total + term
                        sums[8 - t] = sums[8 - t] + fold(hid * x)
                    dna[token, lanes] = total.astype(BF16)
                    sums[9] = sums[9] + fold(sources[a + 1][e])
                    sums[10] = sums[10] + fold(total)
            return tuple(sums)

        sums = lax.fori_loop(0, half, backward, tuple(jnp.zeros((8, LANES), F32) for _ in range(11)), unroll=4)
        for at, total in enumerate(sums):
            small[at : at + 1, lanes] = jnp.sum(total, 0, keepdims=True)
        return carry

    lax.fori_loop(0, width // LANES, block, 0)
    scale_sum = jnp.zeros((1, width), F32)
    for g in range(4):
        rows = pl.ds(g * group, group)
        hat, _ = standardize(xg[rows, :].astype(F32))
        scale_sum = scale_sum + jnp.sum(dna[rows, :].astype(F32) * hat, 0, keepdims=True)
    small[11:12, :] = scale_sum


def conv_back(dct, na, xg, wd, sides, seams, half, deps=()):
    tokens, model = xg.shape
    sds = jax.ShapeDtypeStruct
    args = (dct, na, xg, wd, sides, seams)
    return ordered_call(
        functools.partial(conv_back_kernel, half),
        [whole(v.shape) for v in args],
        deps,
        grid=(1,),
        out_specs=[whole((tokens, model)), whole((16, model))],
        out_shape=[sds((tokens, model), BF16), sds((16, model), F32)],
        scratch_shapes=[pltpu.VMEM((2, 4, (half + 3) * half, model), F32)],
        micros=11,
        name="conv_back",
    )(*args)


def last_kernel(half, dna, xg, dmid, mod, back, o0, o1, o2, o3, tig):
    group = half * half
    parts_of = mod_rows(mod)
    for g in range(4):
        rows = pl.ds(g * group, group)
        hat, inv = standardize(xg[rows, :].astype(F32))
        change = norm_reverse(dna[rows, :].astype(F32) * (1.0 + parts_of[1]), hat, inv)
        tig[rows, :] = (dmid[rows, :].astype(F32) + change).astype(BF16)
    give_strip(my_strip(), tig, back[...], (o0, o1, o2, o3), group, back.shape[0] // 4)


def last(dna, xg, dmid, mod, back, half, deps=()):
    tokens, model = xg.shape
    args = (dna, xg, dmid, mod, back)
    strip = back.shape[0]
    return ordered_call(
        functools.partial(last_kernel, half),
        [whole(v.shape) for v in args],
        deps,
        grid=(1,),
        out_specs=[whole((strip, model))] * 4,
        out_shape=[jax.ShapeDtypeStruct((strip, model), BF16)] * 4,
        scratch_shapes=[pltpu.VMEM((tokens, model), BF16)],
        micros=5,
        name="last",
    )(*args)


def cut_kernel(source, o1, o2, o3, held, sems):
    strip = my_strip()
    outs = (o1, o2, o3)
    fetch = [
        pltpu.make_async_copy(source.at[jnp.bitwise_xor(strip, n + 1)], held.at[n], sems.at[0, n]) for n in range(3)
    ]
    give = [pltpu.make_async_copy(held.at[n], out, sems.at[1, n]) for n, out in enumerate(outs)]
    for copy in fetch:
        copy.start()
    for first, second in zip(fetch, give):
        first.wait()
        second.start()
    for copy in give:
        copy.wait()


def cut_strips(values, deps=()):
    shape = jax.ShapeDtypeStruct(values.shape[1:], values.dtype)
    return ordered_call(
        cut_kernel,
        [pl.BlockSpec(memory_space=pl.ANY)],
        deps,
        out_specs=[pl.BlockSpec(memory_space=pl.ANY)] * 3,
        out_shape=[shape] * 3,
        scratch_shapes=[pltpu.VMEM((3,) + shape.shape, shape.dtype), pltpu.SemaphoreType.DMA((2, 3))],
        micros=2,
        name="cut_strips",
    )(values)


def gather_kernel(own, c1, c2, c3, out):
    strip = my_strip()
    for k, piece in enumerate((own, c1, c2, c3)):
        out[jnp.bitwise_xor(strip, k)] = piece[...].astype(out.dtype)


def gather_strips(own, c1, c2, c3, dtype, deps=()):
    rows, model = own.shape
    return ordered_call(
        gather_kernel,
        [whole(own.shape)] * 4,
        deps,
        grid=(1,),
        out_specs=whole((4, rows, model)),
        out_shape=jax.ShapeDtypeStruct((4, rows, model), dtype),
        vmem=20,
        micros=3,
        name="gather_strips",
    )(own, c1, c2, c3)


def swap(values, axis):
    return lax.ppermute(values, axis, [(0, 1), (1, 0)])


def fold_kernel(count, *refs):
    ins, outs = refs[: 2 * count], refs[2 * count :]
    for at, out in enumerate(outs):
        total = ins[at * count][...].astype(F32)
        for term in ins[at * count + 1 : (at + 1) * count]:
            total = total + term[...].astype(F32)
        out[...] = total.astype(BF16)


def spread_kernel(count, z_count, *refs):
    ins, outs = refs[: 2 * count], refs[2 * count :]
    z = lax.axis_index("z")
    for at in range(2):
        total = ins[at * count][0].astype(F32)
        for term in ins[at * count + 1 : (at + 1) * count]:
            total = total + term[0].astype(F32)
        total = total.astype(BF16)
        rows = total.shape[0]
        shard = rows // z_count
        line = lax.broadcasted_iota(jnp.int32, (shard, rows), 0)
        place = lax.broadcasted_iota(jnp.int32, (shard, rows), 1)
        for k, out in enumerate(outs):
            wanted = (place == line + jnp.bitwise_xor(z, k) * shard).astype(F32).astype(BF16)
            out[at, 0] = dot_nn(wanted, total).astype(BF16)


def close_kernel(together, *refs):
    outs, got = refs[-len(together) :], refs[: -len(together)]
    _, mine, _, width = got[0].shape
    part = 0
    for count, out in zip(together, outs):
        for at in range(count):
            total = got[0][part // mine, part % mine].astype(F32)
            for more in got[1:]:
                total = total + more[part // mine, part % mine].astype(F32)
            out[:, at * width : (at + 1) * width] = total
            part += 1


class SumOverAll:
    def __init__(self, place, keep, send, z_count):
        keep = [v.reshape((-1,) + v.shape[-2:]) for v in keep]
        self.place, self.z_count, self.keep = place, z_count, keep
        self.mine_parts, self.rows, self.width = keep[0].shape
        self.quarter = self.rows // 4
        self.block = min(1536, self.width)
        self.other = [swap(v.reshape((-1,) + v.shape[-2:]), "core") for v in send]

    def fold(self, terms, halves, name, spread=False, deps=()):
        first = len(terms[0])
        specs, args = [], []
        for side in terms:
            for array, row in side:
                def index(p, h, n, place, row=row):
                    return p, row(h, place[0], place[1]), n

                specs.append(pl.BlockSpec((1, self.quarter, self.block), index))
                args.append(array)
        mine = self.mine_parts
        if spread:
            shard = self.quarter // self.z_count
            out_specs = [
                pl.BlockSpec((2, 1, shard, self.block), lambda p, h, n, place: (0, p, 0, n))
            ] * self.z_count
            out_shape = [jax.ShapeDtypeStruct((2, mine, shard, self.width), BF16)] * self.z_count
            kernel = functools.partial(spread_kernel, first, self.z_count)
        else:
            out_specs = [pl.BlockSpec((1, self.quarter, self.block), lambda p, h, n, place: (p, h, n))] * 2
            out_shape = [jax.ShapeDtypeStruct((mine, halves * self.quarter, self.width), BF16)] * 2
            kernel = functools.partial(fold_kernel, first)
        return ordered_call(
            kernel,
            specs,
            deps,
            grid=(mine, halves, self.width // self.block),
            out_specs=out_specs,
            out_shape=out_shape,
            prefetch=self.place,
            micros=2,
            name=name,
        )(*args)

    def second(self):
        (k1, k2), (r1, r2) = self.keep, self.other
        away_x = lambda h, x, y: 2 * (1 - x) + h
        away_y = lambda h, x, y: 2 * h + (1 - y)
        a, b = self.fold([[(k1, away_x), (r1, away_x)], [(k2, away_y), (r2, away_y)]], 2, "fold_second")
        self.got_a, self.got_b = swap(a, "x"), swap(b, "y")
        return a, b

    def third(self):
        (k1, k2), (r1, r2) = self.keep, self.other
        near = lambda h, x, y: 2 * x + (1 - y)
        far = lambda h, x, y: 2 * (1 - x) + y
        a, b = self.fold(
            [
                [(k1, near), (r1, near), (self.got_a, lambda h, x, y: 1 - y)],
                [(k2, far), (r2, far), (self.got_b, lambda h, x, y: 1 - x)],
            ],
            1, "fold_third",
        )
        self.last_a, self.last_b = swap(a, "y"), swap(b, "x")
        return a, b

    def fourth(self, deps=()):
        (k1, k2), (r1, r2) = self.keep, self.other
        own = lambda h, x, y: 2 * x + y
        zero = lambda h, x, y: 0
        self.mine = self.fold(
            [
                [(k1, own), (r1, own), (self.got_a, lambda h, x, y: y), (self.last_a, zero)],
                [(k2, own), (r2, own), (self.got_b, lambda h, x, y: x), (self.last_b, zero)],
            ],
            1, "fold_fourth", True, deps,
        )
        pairs = lambda k: [(i, i ^ k) for i in range(self.z_count)]
        self.mine = [v if k == 0 else lax.ppermute(v, "z", pairs(k)) for k, v in enumerate(self.mine)]

    def finish(self, together, deps=()):
        shard = self.mine[0].shape[2]
        shapes = [jax.ShapeDtypeStruct((shard, count * self.width), F32) for count in together]
        return ordered_call(
            functools.partial(close_kernel, together),
            [whole(v.shape) for v in self.mine],
            deps,
            grid=(1,),
            out_specs=[whole(v.shape) for v in shapes],
            out_shape=shapes,
            vmem=20,
        micros=2,
            name="close_sums",
        )(*self.mine)


MODS = 6


def pack_kernel(groups, ff, fc2, mid, qv, last, o0, o1, o2, o3, work):
    work[...] = jnp.zeros_like(work)
    model = last.shape[1]
    strip_width = model // 4
    d_mod = [last[10:11, :], last[11:12, :]] + [mid[k : k + 1, :] for k in range(4)]
    short = [last[k : k + 1, :] for k in range(10)] + [mid[4:5, :], fc2[...]]
    for t in range(4):
        work[t, 0:11, :] = ff[0:11, t * model : (t + 1) * model]
        for k, row in enumerate(d_mod):
            work[t, 11 + k : 12 + k, :] = row
        for k, row in enumerate(short):
            work[t, 17 + k : 18 + k, 0:strip_width] = row[:, t * strip_width : (t + 1) * strip_width]
        at = (2 * t * strip_width) % model
        work[t, 29:30, 0 : 2 * strip_width] = qv[t // 2 : t // 2 + 1, at : at + 2 * strip_width]
    for k, out in enumerate((o0, o1, o2, o3)):
        out[...] = work[jnp.bitwise_xor(my_strip(), k)].astype(BF16)


def pack(ff, fc2, mid, qv, last, groups, deps=()):
    args = (ff, fc2, mid, qv, last)
    model = last.shape[1]
    return ordered_call(
        functools.partial(pack_kernel, groups),
        [whole(v.shape) for v in args],
        deps,
        grid=(1,),
        out_specs=[whole((32, model))] * 4,
        out_shape=[jax.ShapeDtypeStruct((32, model), BF16)] * 4,
        scratch_shapes=[pltpu.VMEM((4, 32, model), F32)],
        vmem=20,
        micros=2,
        name="pack_small",
    )(*args)


def repack_kernel(groups, g0, g1, g2, g3, cond, out, mods, work, common):
    model = g0.shape[1]
    work[...] = jnp.zeros_like(work)
    values = [g[...].astype(F32) for g in (g0, g1, g2, g3)]
    total = values[0] + values[1] + values[2] + values[3]
    lanes = model // LANES
    head = MODS * lanes * 4
    for part in range(MODS):
        for lb in range(lanes):
            for k in range(4):
                at = (part * lanes + lb) * 4 + jnp.bitwise_xor(my_strip(), k)
                row = values[k][11 + part : 12 + part, lb * LANES : (lb + 1) * LANES]
                common[pl.ds(at, 1), :] = row
    for part in range(MODS):
        for lb in range(lanes):
            at = (part * lanes + lb) * 4
            mods[:, (part * lanes + lb) * LANES : (part * lanes + lb + 1) * LANES] = common[at : at + 4, :].astype(BF16)
    wide, thin = model // groups, model // 4 // groups
    for u in range(groups):
        work[u, 0:11, 0:wide] = total[0:11, u * wide : (u + 1) * wide]
        work[u, 17:29, 0:thin] = total[17:29, u * thin : (u + 1) * thin]
        work[u, 29:30, 0 : 2 * thin] = total[29:30, 2 * u * thin : 2 * (u + 1) * thin]
        work[u, 32:36, 0:thin] = cond[:, u * thin : (u + 1) * thin].astype(F32)
        out[u, 0:head, :] = common[...].astype(BF16)
        out[u, head:, :] = work[u].astype(BF16)


def repack(got, cond, groups, deps=()):
    model = got[0].shape[1]
    head = MODS * (model // LANES) * 4
    args = (*got, cond)
    shapes = [(groups, head + 48, LANES), (4, MODS * model)]
    return ordered_call(
        functools.partial(repack_kernel, groups),
        [whole(v.shape) for v in args],
        deps,
        grid=(1,),
        out_specs=[whole(v) for v in shapes],
        out_shape=[jax.ShapeDtypeStruct(v, BF16) for v in shapes],
        scratch_shapes=[pltpu.VMEM((groups, 48, LANES), F32), pltpu.VMEM((head, LANES), F32)],
        vmem=20,
        micros=2,
        name="repack_small",
    )(*args)


def unpack_kernel(groups, got, wada, bada, *refs):
    outs, (mods, conds) = refs[:-2], refs[-2:]
    head = got.shape[1] - 48
    total = jnp.sum(got[:, head:, :].astype(F32), 0)
    rows = ((0, 9), (9, 10), (10, 11), (17, 26), (26, 27), (27, 28), (28, 29), (29, 30))
    for (first, end), out in zip(rows, outs):
        out[...] = total[first:end, 0 : out.shape[1]]
    for u in range(groups):
        values = got[u].astype(F32)
        conds[u * 4 : (u + 1) * 4, :] = values[head + 32 : head + 36]
        for block in range(head // 4):
            mods[u * 4 : (u + 1) * 4, block * LANES : (block + 1) * LANES] = values[block * 4 : block * 4 + 4]
    shard, own = wada.shape[0], bada.shape[1]
    wada[...] = dot_tn(conds[...].astype(BF16), mods[...].astype(BF16))[0:shard]
    index = my_strip() * groups + lax.axis_index("z") * 2 + lax.axis_index("y")
    summed = jnp.broadcast_to(jnp.sum(mods[...], 0, keepdims=True), (8, mods.shape[1]))
    bada[...] = pltpu.roll(summed, mods.shape[1] - own * index, 1)[0:1, 0:own]


def unpack(got, model, groups, deps=()):
    wide, thin = model // groups, model // 4 // groups
    shapes = [(thin, MODS * model), (1, MODS * thin)]
    shapes += [(9, wide), (1, wide), (1, wide), (9, thin), (1, thin), (1, thin), (1, thin), (1, 2 * thin)]
    return ordered_call(
        functools.partial(unpack_kernel, groups),
        [whole(got.shape)],
        deps,
        grid=(1,),
        out_specs=[whole(v) for v in shapes],
        out_shape=[jax.ShapeDtypeStruct(v, F32) for v in shapes],
        scratch_shapes=[pltpu.VMEM((4 * groups, MODS * model), F32), pltpu.VMEM((4 * groups, LANES), F32)],
        vmem=20,
        micros=2,
        name="unpack_small",
    )(got)


def cond_back_kernel(mods, wada, cond, out):
    change = dot_nt(wada[...], mods[...]).T
    values = cond[...].astype(F32)
    gain = 1.0 / (1.0 + jnp.exp(-values))
    out[...] = change * gain * (1.0 + values * (1.0 - gain))


def cond_back(mods, wada, cond, deps=()):
    canvases, model = cond.shape
    tile = model // 3
    return ordered_call(
        cond_back_kernel,
        [whole(mods.shape), pl.BlockSpec((tile, wada.shape[1]), lambda i: (i, 0)),
         pl.BlockSpec((canvases, tile), lambda i: (0, i))],
        deps,
        grid=(3,),
        out_specs=pl.BlockSpec((canvases, tile), lambda i: (0, i)),
        out_shape=jax.ShapeDtypeStruct((canvases, model), F32),
        micros=3,
        name="cond_back",
    )(mods, wada, cond)


def row_order(model, z_count):
    rows = jnp.arange(model, dtype=jnp.int32).reshape(2, 2, z_count, 2, -1)
    rows = jnp.transpose(rows, (1, 0, 3, 2, 4)).reshape(2, -1)
    rows = jnp.where(lax.axis_index("core") == 0, rows, rows[::-1]).reshape(-1)
    return (rows[:, None] == jnp.arange(model, dtype=jnp.int32)[None]).astype(BF16)


def shards(
    tokens, conditioning, latent_ids, w_ada, b_ada, w_dw1, b_dw1, w_qkv, b_qv, w_out, b_out,
    w_fc1, b_fc1, w_dw2, b_dw2, w_fc2, b_fc2, out_grad,
):
    canvases, rows, cols, model = tokens.shape
    half = cols // 2
    hidden = w_fc1.shape[1]
    z_count = lax.axis_size("z")
    groups = 2 * z_count
    devices = 4 * groups
    strip = my_strip()
    strips = ("x", "core")
    span = 256
    Order.last = ()

    def exchange(pieces):
        return [lax.ppermute(piece, strips, [(i, i ^ (k + 1)) for i in range(4)]) for k, piece in enumerate(pieces)]

    token_rows = tokens.reshape(canvases, rows * cols, model)
    grad_rows = out_grad.reshape(canvases, rows * cols, model)
    token_pieces = exchange(cut_strips(token_rows))

    cond_vals = conditioning.astype(F32)
    cond_act = jax.nn.silu(cond_vals).astype(BF16)
    mod = jnp.dot(cond_act, w_ada, preferred_element_type=F32) + b_ada.astype(F32)
    cond_cols = lax.dynamic_slice_in_dim(cond_act, strip * (model // 4), model // 4, 1)
    place = jnp.stack([lax.axis_index("x"), lax.axis_index("y")]).astype(jnp.int32)
    perm = row_order(model, z_count)

    ids = lax.dynamic_slice_in_dim(latent_ids, strip, 1, 0)
    sides, seams, mask, order, back = prep(ids, half, rows * cols)
    listed = (b_fc1, b_dw2, b_qv, b_dw1, b_out, b_fc2)
    biases = jnp.concatenate(listed).astype(F32)[None]
    places = [sum(v.shape[0] for v in listed[:n]) // listed[n].shape[0] for n in range(6)]
    wt = w_qkv.T

    xg, na, cat, *grad_cut = first_norm(
        token_rows, *token_pieces, order, mod, w_dw1, biases, sides, seams, grad_rows, half, places[3], (wt, cond_cols, perm, place)
    )
    grad_pieces = exchange(grad_cut)
    qkvt, lse, ot, proj, mid, nb, nbt = attend(
        cat, wt, biases, mask, w_out, mod, xg, perm, half, places[2], places[4]
    )
    gg, db, dbt, small_fc2 = gate(grad_rows, *grad_pieces, order, mod, perm, half)
    ff_k1, ff_s1, ff_k2, ff_s2, small_ff, branch, dnb = feed_forward(
        nb, nbt, db, dbt, w_fc1, w_dw2, w_fc2, biases, sides, seams, half, 256
    )
    ff = SumOverAll(place, (ff_k1, ff_k2), (ff_s1, ff_s2), z_count)
    *res, dmid, dot_, dpt, small_mid = middle(
        branch, dnb, mid, proj, gg, w_out, biases, mod, back, perm, half, places[5]
    )
    res = [res[0]] + exchange(res[1:])
    ff.second()
    at_k1, at_k2, at_s1, at_s2, dct, small_qv = attend_back(
        qkvt, dot_, ot, lse, mask, cat, dpt, perm, w_qkv, half, span
    )
    at = SumOverAll(place, (at_k1, at_k2), (at_s1, at_s2), z_count)
    ff.third()
    at.second()
    dna, small_last = conv_back(dct, na, xg, w_dw1, sides, seams, half)
    ff.fourth()
    tig = last(dna, xg, dmid, mod, back, half)
    tig = [tig[0]] + exchange(tig[1:])
    message = pack(small_ff, small_fc2, small_mid, small_qv, small_last, groups)
    got = [message[0]] + exchange(message[1:])
    at.third()
    token_grad = gather_strips(*tig, F32).reshape(tokens.shape)
    g_w_fc1, g_w_fc2 = ff.finish((1, 1))
    at.fourth()
    message, d_mod = repack(got, cond_cols, groups)
    got = lax.all_to_all(message, ("z", "y"), split_axis=0, concat_axis=0, tiled=True)
    grad_cond = cond_back(d_mod, w_ada, conditioning)
    g_w_ada, g_b_ada, g_w_dw2, g_b_dw2, g_b_fc1, g_w_dw1, g_b_dw1, g_b_out, g_b_fc2, g_b_qv = unpack(
        got, model, groups
    )
    result = gather_strips(*res, BF16).reshape(tokens.shape)
    g_w_qkv, g_w_out = at.finish((3, 1))
    return (
        result, token_grad, grad_cond, g_w_ada, g_b_ada[0],
        g_w_dw1, g_b_dw1[0], g_w_qkv, g_b_qv[0], g_w_out.T, g_b_out[0],
        g_w_fc1, g_b_fc1[0], g_w_dw2, g_b_dw2[0], g_w_fc2.T, g_b_fc2[0],
    )


def solution(mesh):
    strip, canvas = mesh.devices.shape
    finer = Mesh(mesh.devices.reshape(strip // 2, 2, canvas // 2, 2), ("x", "core", "z", "y"))
    strips, groups, every = ("x", "core"), ("z", "y"), ("x", "core", "z", "y")
    block = P(groups, strips, None, None)
    return jax.shard_map(
        shards,
        mesh=finer,
        in_specs=(block, P(groups, None), P(groups, None)) + (P(),) * 14 + (block,),
        out_specs=(
            block, block, P(groups, None), P(every, None), P(every),
            P(None, every), P(every), P(every, None), P(every),
            P(None, every), P(every), P(every, None), P(every),
            P(None, every), P(every), P(None, every), P(every),
        ),
        check_vma=False,
    )
```
